256 devices in a mesh: dp: 32 (over z, x_hi, core), mp: 8 (over y, x_lo).
Axes of the slice: x: 4 (x_hi: 2, x_lo: 2; x = x_hi * 2 + x_lo), y: 4, z: 8, core: 2. Of those that a mesh axis runs over, the one named last changes fastest.
Arguments:
- train_x: bfloat16 [256, 8192], P('mp', 'dp'), may hold values from -6 to 6
- train_cot: bfloat16 [256, 8192], P('mp', 'dp'), may hold values from -6 to 6
- val_x: bfloat16 [32, 8192], P('mp', 'dp'), may hold values from -6 to 6
- val_cot: bfloat16 [32, 8192], P('mp', 'dp'), may hold values from -6 to 6
- w_gate: bfloat16 [8192, 14336], P('dp', 'mp'), may hold values from -0.0625 to 0.0625
- w_up: bfloat16 [8192, 14336], P('dp', 'mp'), may hold values from -0.0625 to 0.0625
- w_down: bfloat16 [14336, 8192], P('mp', 'dp'), may hold values from -0.046875 to 0.046875
- step_weights: float32 [8], replicated, may hold values from 0.25 to 4
- example_ids: int32 [256], replicated, may hold values from 0 to 7, never falling along the last dimension, each value on 1 to 64 neighbouring positions
- val_mask: int32 [32], replicated, may hold values 0 or 1
Outputs:
- grad_gate: bfloat16 [8192, 14336], P('dp', 'mp')
- grad_up: bfloat16 [8192, 14336], P('dp', 'mp')
- grad_down: bfloat16 [14336, 8192], P('mp', 'dp')
- example_weights: float32 [8], replicated
The draws below stay inside these ranges and needn't reach their ends.
Inputs may be any that keep to these rules, and one draw needn't show every extreme that they name: `example_ids`: never falling along the tokens; each example holds 1 to 64 tokens, one exactly 64.
All inputs are finite; a program needn't handle non-finite values.
Results may differ from the reference program's by a relative error of at most 0.006.
Values may be sent and summed in bfloat16 or wider, within the bound.
A program may use at most 64 MiB of HBM per device.

```python
import math
import jax
import jax.numpy as jnp
import numpy as np
from jax import lax

D = 8192
FF = 14336
EXAMPLES = 8
TOKENS = 256
VTOKENS = 32
RUN = 64


def set_ends(values, rng, least, high):
    shape = values.shape
    index_at = [jax.random.randint(jax.random.fold_in(rng, axis), (), 0, shape[axis]) for axis in range(len(shape))]
    values = values.at[tuple(index_at)].set(least)
    longest = shape.index(max(shape))
    index_at[longest] = (index_at[longest] + 1) % shape[longest]
    return values.at[tuple(index_at)].set(high)


def levels(key, extent, shards, smallest, high):
    level, own = 1.0, jax.random.fold_in(key, 6)
    for axis_at, blocks in shards:
        steps = jnp.exp(jax.random.uniform(jax.random.fold_in(own, axis_at), (blocks,), jnp.float32, smallest / len(shards), high / len(shards)))
        level = level * jnp.repeat(steps, extent[axis_at] // blocks).reshape([-1 if axis == axis_at else 1 for axis in range(len(extent))])
    return level


def length_profile(number_of, total, bound, lean):
    weights = [(1 << 20) // math.isqrt(standing ** lean) + 1 for standing in range(2, number_of + 1)]
    rest, holding = total - bound - (number_of - 1), [1] * (number_of - 1)
    while rest > 0:
        free = [i for i in range(number_of - 1) if holding[i] < bound]
        mass, remaining = sum([weights[i] for i in free]), rest
        for i in free:
            extra = min(bound - holding[i], max(1, remaining * weights[i] // mass), rest)
            holding[i] = holding[i] + extra
            rest = rest - extra
    return np.array([bound] + holding)


def ragged_sizes(stream_key, number_of, total, most, skew):
    if number_of == 2:
        one = jax.random.randint(stream_key, (), max(1, total - most), min(most, total - 1) + 1)
        return jnp.stack([one, total - one])
    sizes = jnp.asarray(length_profile(number_of, total, most, skew), jnp.int32)
    pairs = (number_of - 1) // 2
    donor, taker = sizes[1:1 + 2 * pairs:2], sizes[2:2 + 2 * pairs:2]
    room = jnp.minimum(donor - 1, most - taker)
    shifted = jax.random.randint(jax.random.fold_in(stream_key, 1), (pairs,), 0, 1 << 20) % (room + 1)
    sizes = sizes.at[1:1 + 2 * pairs:2].set(donor - shifted).at[2:2 + 2 * pairs:2].set(taker + shifted)
    return sizes[jax.random.permutation(jax.random.fold_in(stream_key, 2), number_of)]


def centred(rng, shape, scale, reach, split=(), held_as=jnp.bfloat16):
    entries = jax.random.normal(rng, shape, jnp.float32) * scale
    if len(split) > 0:
        entries = levels(rng, shape, split, -0.22, 0.18) * entries
    return jnp.clip(entries, min=-reach, max=reach).astype(held_as)


def setup_inputs(seed: int = 0) -> dict:
    key_list = jax.random.split(jax.random.key(seed), 11)
    return {
        "train_x": centred(key_list[0], (TOKENS, D), 1.0, 6.0, ((0, 8), (1, 32))),
        "train_cot": centred(key_list[1], (TOKENS, D), 1.0, 6.0, ((0, 8), (1, 32))),
        "val_x": centred(key_list[2], (VTOKENS, D), 1.0, 6.0, ((0, 8), (1, 32))),
        "val_cot": centred(key_list[3], (VTOKENS, D), 1.0, 6.0, ((0, 8), (1, 32))),
        "w_gate": centred(key_list[4], (D, FF), D ** -0.5, 0.0625, ((0, 32), (1, 8))),
        "w_up": centred(key_list[5], (D, FF), D ** -0.5, 0.0625, ((0, 32), (1, 8))),
        "w_down": centred(key_list[6], (FF, D), FF ** -0.5, 0.046875, ((0, 8), (1, 32))),
        "step_weights": jnp.clip(jnp.exp(jax.random.uniform(key_list[7], (EXAMPLES,), jnp.float32, math.log(0.25), math.log(4.0))), 0.25, 4.0),
        "example_ids": jnp.searchsorted(jnp.cumsum(ragged_sizes(key_list[8], EXAMPLES, TOKENS, RUN, 0)), jnp.arange(TOKENS), side="right").astype(jnp.int32),
        "val_mask": set_ends((jax.random.randint(key_list[9], (VTOKENS,), 0, 4) < 3).astype(jnp.int32), jax.random.fold_in(key_list[9], 1), 0, 1),
    }


LEARN_RATE = 0.0003

def forward(inputs, cotangent, w_gate, w_up, w_down):
    gate = jnp.dot(inputs, w_gate, preferred_element_type=jnp.float32)
    up = jnp.dot(inputs, w_up, preferred_element_type=jnp.float32)
    back = jnp.dot(cotangent, w_down.T, preferred_element_type=jnp.float32)
    sig = jax.nn.sigmoid(gate)
    act = gate * sig
    hidden = (act * up).astype(jnp.bfloat16)
    d_gate = (back * up * sig * (1.0 + gate * (1.0 - sig))).astype(jnp.bfloat16)
    d_up = (back * act).astype(jnp.bfloat16)
    return (hidden, d_gate, d_up)

def gradients(inputs, cotangent, hidden, d_gate, d_up, factor):
    scaled_in = (inputs.astype(jnp.float32) * factor[:, None]).astype(jnp.bfloat16)
    scaled_cot = (cotangent.astype(jnp.float32) * factor[:, None]).astype(jnp.bfloat16)
    grad_g = jnp.dot(scaled_in.T, d_gate, preferred_element_type=jnp.float32)
    grad_u = jnp.dot(scaled_in.T, d_up, preferred_element_type=jnp.float32)
    grad_d = jnp.dot(hidden.T, scaled_cot, preferred_element_type=jnp.float32)
    return (grad_g, grad_u, grad_d)

def per_token(example_ids, table):
    labels = jnp.arange(table.shape[0], dtype=jnp.int32)
    match = example_ids[:, None] == labels[None, :]
    return lax.optimization_barrier(jnp.sum(jnp.where(match, table[None, :], jnp.zeros((), table.dtype)), axis=1))

def reference(train_x, train_cot, val_x, val_cot, w_gate, w_up, w_down, step_weights, example_ids, val_mask):
    hidden, d_gate, d_up = forward(train_x, train_cot, w_gate, w_up, w_down)
    factor = per_token(example_ids, step_weights)
    grad_g, grad_u, grad_d = gradients(train_x, train_cot, hidden, d_gate, d_up, factor)
    ahead_g = (w_gate.astype(jnp.float32) - LEARN_RATE * grad_g).astype(jnp.bfloat16)
    ahead_u = (w_up.astype(jnp.float32) - LEARN_RATE * grad_u).astype(jnp.bfloat16)
    ahead_d = (w_down.astype(jnp.float32) - LEARN_RATE * grad_d).astype(jnp.bfloat16)
    v_hidden, v_gate, v_up = forward(val_x, val_cot, ahead_g, ahead_u, ahead_d)
    mask_f = val_mask.astype(jnp.float32)
    val_g, val_u, val_d = gradients(val_x, val_cot, v_hidden, v_gate, v_up, mask_f)
    val_g = val_g.astype(jnp.bfloat16)
    val_u = val_u.astype(jnp.bfloat16)
    val_d = val_d.astype(jnp.bfloat16)
    dir_g = jnp.dot(train_x, val_g, preferred_element_type=jnp.float32)
    dir_u = jnp.dot(train_x, val_u, preferred_element_type=jnp.float32)
    dir_d = jnp.dot(train_cot, val_d.T, preferred_element_type=jnp.float32)
    inner = dir_g * d_gate.astype(jnp.float32) + dir_u * d_up.astype(jnp.float32) + dir_d * hidden.astype(jnp.float32)
    token_score = lax.optimization_barrier(jnp.sum(inner, axis=1))
    labels = jnp.arange(step_weights.shape[0], dtype=jnp.int32)
    match = example_ids[:, None] == labels[None, :]
    score = lax.optimization_barrier(jnp.sum(jnp.where(match, token_score[:, None], jnp.zeros((), token_score.dtype)), axis=0))
    spread_rms = jnp.sqrt(jnp.mean(score * score) + 1e-06)
    softened = jax.nn.softplus(score / (4.0 * spread_rms))
    weights = step_weights.shape[0] * softened / jnp.sum(softened)
    final = per_token(example_ids, weights)
    out_g, out_u, out_d = gradients(train_x, train_cot, hidden, d_gate, d_up, final)
    return (out_g.astype(jnp.bfloat16), out_u.astype(jnp.bfloat16), out_d.astype(jnp.bfloat16), weights)
```

```python
import jax
import jax.numpy as jnp
from jax import lax
from jax.experimental import pallas as pl
from jax.experimental.pallas import tpu as pltpu
from jax.sharding import PartitionSpec as P

MESH = pl.DeviceIdType.MESH
BF = jnp.bfloat16
F32 = jnp.float32

LEARN_RATE = 0.0003
NZ = 8
NM = 8
HB = 112
TOK = 256
W = 256
EX = 8


def nt(left, right):
    return lax.dot_general(left, right, (((1,), (1,)), ((), ())), preferred_element_type=F32)


def tn(left, right):
    return lax.dot_general(left, right, (((0,), (0,)), ((), ())), preferred_element_type=F32)


def comm_kernel(
    x_in, c_in, vx_in, vc_in, wg_in, wu_in, wd_in, sw, ids, mask,
    full_out, xs_out, wts_out,
    wraw, wt, wo, pk, vstage, xb, xo, va, vo, part, full,
    long_r_s, long_r_d, long_l_s, long_l_d, short_r_s, short_r_d, short_l_s, short_l_d,
    swap_s, swap_d, gram_s, gram_d, gram_x, gram_all, sc1, sc2, sc3, xt, xs,
    lsem, ssem, rsem, hsem,
):
    d = lax.axis_index("dp")
    m = lax.axis_index("mp")
    z = d // 4
    xh = (d // 2) % 2
    c = d % 2

    def dev(zz, xx, cc):
        return (zz * 4 + xx * 2 + cc, m)

    def zdev(step):
        return dev((z + step + NZ) % NZ, xh, c)

    def mdev(step):
        return (d, (m + step) % NM)

    other = dev(z, xh, 1 - c)
    across = dev(z, 1 - xh, c)
    diagonal = dev(z, 1 - xh, 1 - c)

    sends = []
    n_send = [0]

    def send(src, dst, rs, to):
        copy = pltpu.make_async_remote_copy(
            src_ref=src, dst_ref=dst, send_sem=ssem.at[n_send[0]], recv_sem=rsem.at[rs],
            device_id=to, device_id_type=MESH,
        )
        n_send[0] += 1
        copy.start()
        sends.append(copy)

    def got(dst, rs):
        pltpu.make_async_copy(dst, dst, rsem.at[rs]).wait()

    R_X, R_XO, R_W, R_RING, R_SWAP = 0, 8, 16, 24, 40
    R_GS, R_GX, R_GA, R_GC = 42, 50, 51, 59
    R_AR, R_AC, R_S1, R_S2, R_S3 = 60, 76, 84, 92, 100

    loads = [
        pltpu.make_async_copy(x_in, pk.at[0:32], lsem.at[0]),
        pltpu.make_async_copy(c_in, pk.at[32:64], lsem.at[1]),
        pltpu.make_async_copy(wg_in, wraw.at[0], lsem.at[2]),
        pltpu.make_async_copy(wu_in, wraw.at[1], lsem.at[3]),
        pltpu.make_async_copy(wd_in, wt.at[:, 2], lsem.at[4]),
    ]
    for copy in loads:
        copy.start()

    barrier = pltpu.get_barrier_semaphore()
    peers = [zdev(k) for k in range(1, NZ)] + [mdev(k) for k in range(1, NM)] + [other, across, diagonal]
    for peer in peers:
        pl.semaphore_signal(barrier, inc=1, device_id=peer, device_id_type=MESH)

    vstage[0:16] = jnp.zeros((16, W), F32)
    vstage[0:4] = vx_in[...].astype(F32)
    vstage[4:8] = vx_in[...].astype(F32)
    vstage[8:12] = vc_in[...].astype(F32)
    pk[64:80] = vstage[0:16].astype(BF)
    loads[0].wait()
    loads[1].wait()
    xb[m] = pk[...]
    pl.semaphore_wait(barrier, len(peers))

    for k in range(1, NM):
        send(pk, xb.at[m], R_X + m, mdev(k))
    send(pk, xo.at[m], R_XO + m, other)

    for w in range(2):
        loads[2 + w].wait()
        for i in range(14):
            block = wraw[w, :, 128 * i : 128 * (i + 1)].T
            at = 128 * i
            while at < 128 * (i + 1):
                b = at // HB
                end = min(128 * (i + 1), (b + 1) * HB)
                wt[b, w, at - b * HB : end - b * HB] = block[at - 128 * i : end - 128 * i]
                at = end
    loads[4].wait()
    for step in (4, 3, 5, 2, 6, 1, 7, 0):
        k = (z + step) % NZ
        send(wt.at[2 * k + 1 - c], wo.at[k], R_W + k, other)

    for k in range(1, NM):
        j = (m + NM - k) % NM
        got(xb.at[j], R_X + j)
        send(xb.at[j], xo.at[j], R_XO + j, other)
    for k in range(NM):
        j = (m + NM - k) % NM
        got(xo.at[j], R_XO + j)

    place = lax.broadcasted_iota(jnp.int32, (128, W), 0) % 16
    for src, dst in ((xb, va), (xo, vo)):
        rows = src[:, 64:80, :].reshape(128, W).astype(F32)
        for i in range(3):
            keep = jnp.logical_and(place >= 4 * i, place < 4 * i + 4)
            dst[i] = jnp.where(keep, rows, 0.0).astype(BF)

    def tokens(ref, first):
        return ref[:, 32 * first : 32 * first + 32, :].reshape(TOK, W)

    def partial_sums(k):
        got(wo.at[k], R_W + k)
        b = 2 * k + c
        val = jnp.zeros((HB, 128), F32)
        for i in range(3):
            first = 1 if i == 2 else 0
            total = nt(wt[b, i], tokens(xb, first)) + nt(wo[k, i], tokens(xo, first))
            part[k, i] = total[:, :128]
            part[k, 4 + i] = total[:, 128:]
            val = val + nt(wt[b, i], va[i]) + nt(wo[k, i], vo[i])
        part[k, 3] = val

    A, B = slice(0, 4), slice(4, 7)

    def at(step):
        return (z + step + NZ) % NZ

    RL, RS, LL, LS = R_RING, R_RING + 4, R_RING + 8, R_RING + 12

    def first(s_buf, d_buf, rows, rs, step, to):
        s_buf[0] = part[at(step), rows].astype(BF)
        send(s_buf.at[0], d_buf.at[0], rs, to)

    def onward(s_buf, d_buf, rows, rs, s, step, to):
        got(d_buf.at[s - 1], rs + s - 1)
        s_buf[s] = (part[at(step), rows] + d_buf[s - 1].astype(F32)).astype(BF)
        send(s_buf.at[s], d_buf.at[s], rs + s, to)

    right, left = zdev(1), zdev(-1)
    partial_sums(at(4))
    first(long_r_s, long_r_d, A, RL, 4, right)
    first(long_l_s, long_l_d, B, LL, 4, left)
    partial_sums(at(3))
    first(short_r_s, short_r_d, B, RS, 3, right)
    partial_sums(at(-3))
    first(short_l_s, short_l_d, A, LS, -3, left)

    def half(ref, first):
        return ref[pl.ds(4 * c, 4), 32 * first : 32 * first + 32, :].reshape(128, W)

    gram = nt(va[0], half(xb, 0)) + nt(vo[0], half(xo, 0)) + nt(va[2], half(xb, 1)) + nt(vo[2], half(xo, 1))
    gram_s[...] = gram.reshape(NZ, 16, 128)
    gram_d[z] = gram_s[z]
    for k in range(1, NZ):
        send(gram_s.at[at(k)], gram_d.at[z], R_GS + z, zdev(k))

    onward(long_r_s, long_r_d, A, RL, 1, 3, right)
    onward(long_l_s, long_l_d, B, LL, 1, -3, left)
    partial_sums(at(2))
    partial_sums(at(-2))
    onward(short_r_s, short_r_d, B, RS, 1, 2, right)
    onward(short_l_s, short_l_d, A, LS, 1, -2, left)

    for k in range(1, NZ):
        got(gram_d.at[at(k)], R_GS + at(k))
    gram_x[0] = jnp.sum(gram_d[...], axis=0)
    send(gram_x.at[0], gram_x.at[1], R_GX, across)

    onward(long_r_s, long_r_d, A, RL, 2, 2, right)
    onward(long_l_s, long_l_d, B, LL, 2, -2, left)
    partial_sums(at(1))
    partial_sums(at(-1))
    onward(short_r_s, short_r_d, B, RS, 2, 1, right)
    onward(short_l_s, short_l_d, A, LS, 2, -1, left)

    got(gram_x.at[1], R_GX)
    gram_all[c, z] = gram_x[0] + gram_x[1]
    for k in range(1, NZ):
        send(gram_all.at[c, z], gram_all.at[c, z], R_GA + z, zdev(k))

    onward(long_r_s, long_r_d, A, RL, 3, 1, right)
    onward(long_l_s, long_l_d, B, LL, 3, -1, left)
    partial_sums(z)

    for k in range(1, NZ):
        got(gram_all.at[c, at(k)], R_GA + at(k))
    send(gram_all.at[c], gram_all.at[c], R_GC, other)

    r_row = jnp.zeros((1, TOK), F32)
    for e in range(EX):
        r_row = r_row + jnp.where(ids[...] == e, sw[e], 0.0)
    for i in range(2):
        xt[i] = tokens(xb, i).T.astype(F32)

    got(short_r_d.at[2], RS + 2)
    got(long_l_d.at[3], LL + 3)
    own_b = part[z, B] + short_r_d[2].astype(F32) + long_l_d[3].astype(F32)
    part[z, B] = own_b
    swap_s[B] = own_b.astype(BF)
    send(swap_s.at[B], swap_d.at[B], R_SWAP + 1, across)
    got(short_l_d.at[2], LS + 2)
    got(long_r_d.at[3], RL + 3)
    own_a = part[z, A] + short_l_d[2].astype(F32) + long_r_d[3].astype(F32)
    part[z, A] = own_a
    swap_s[A] = own_a.astype(BF)
    send(swap_s.at[A], swap_d.at[A], R_SWAP, across)

    def block_terms(gate, up, back):
        sig = 1.0 / (1.0 + jnp.exp(-gate))
        act = gate * sig
        return act * up, back * up * sig * (1.0 + gate * (1.0 - sig)), back * act

    mine = 2 * z + c

    def ahead(lo, hi, s, block, sem, to):
        send(full.at[block, lo:hi], full.at[block, lo:hi], sem, to)

    AR, AL = R_AR, R_AR + 8
    got(swap_d.at[B], R_SWAP + 1)
    for h, lo in ((1, 4), (0, 0)):
        if h == 0:
            got(swap_d.at[A], R_SWAP)
        total = [part[z, lo + i] + swap_d[lo + i].astype(F32) for i in range(3)]
        hid, dg, du = block_terms(*total)
        full[mine, 3 * h] = hid.astype(BF)
        full[mine, 3 * h + 1] = dg.astype(BF)
        full[mine, 3 * h + 2] = du.astype(BF)
        send(full.at[mine, 3 * h : 3 * h + 3], full.at[mine, 3 * h : 3 * h + 3], AR + h, right)
        send(full.at[mine, 3 * h : 3 * h + 3], full.at[mine, 3 * h : 3 * h + 3], AL + h, left)
    send(full.at[mine], full.at[mine], R_AC + z, other)
    outs = []

    def flush(block, sem):
        copy = pltpu.make_async_copy(full.at[block], full_out.at[block], hsem.at[sem])
        copy.start()
        outs.append(copy)

    def arrived(step, base, towards, to):
        zz = at(-step) if towards > 0 else at(step)
        block = 2 * zz + c
        for h in (1, 0):
            if step == 4 and h == (1 if towards > 0 else 0):
                continue
            piece = full.at[block, 3 * h : 3 * h + 3]
            got(piece, base + (step - 1) * 2 + h)
            if step < 3 or (step == 3 and h == (0 if towards > 0 else 1)):
                send(piece, piece, base + step * 2 + h, to)
        return zz, block

    def step_of_gather(step):
        if step < 4:
            zr, br = arrived(step, AR, 1, right)
            zl, bl = arrived(step, AL, -1, left)
            send(full.at[br], full.at[br], R_AC + zr, other)
            send(full.at[bl], full.at[bl], R_AC + zl, other)
        else:
            arrived(step, AR, 1, right)
            zl, bl = arrived(step, AL, -1, left)
            send(full.at[bl], full.at[bl], R_AC + zl, other)

    got(gram_all.at[1 - c], R_GC)
    kt = jnp.concatenate([gram_all[0].reshape(128, 128), gram_all[1].reshape(128, 128)], axis=1)
    rk = (kt * r_row).astype(BF)
    hb, dgb, dub = [jnp.concatenate([full[mine, i], full[mine, 3 + i]], axis=1) for i in range(3)]
    val = part[z, 3] + swap_d[3].astype(F32)
    v_gate = val - LEARN_RATE * nt(dgb, rk)
    v_up = pltpu.roll(val, 124, 1) - LEARN_RATE * nt(dub, rk)
    v_back = pltpu.roll(val - LEARN_RATE * nt(hb, rk), 120, 1)
    lane = lax.broadcasted_iota(jnp.int32, (32, 128), 1)
    row = lax.broadcasted_iota(jnp.int32, (32, 128), 0)
    pick = jnp.logical_and(lane % 16 < 4, (lane // 16) * 4 + lane % 16 == row)
    mask_f = jnp.broadcast_to(mask[...].astype(F32), (16, 32)).astype(BF)
    mask_l = lax.dot_general(
        mask_f, jnp.where(pick, 1.0, 0.0).astype(BF), (((1,), (0,)), ((), ())), preferred_element_type=F32
    )[0:1]
    keep = jnp.broadcast_to(mask_l, (HB, 128)) > 0.5
    v_hid, v_dg, v_du = [jnp.where(keep, t, 0.0) for t in block_terms(v_gate, v_up, v_back)]
    inner = tn(v_dg.astype(BF), dgb) + tn(v_du.astype(BF), dub) + tn(pltpu.roll(v_hid, 8, 1).astype(BF), hb)
    token = jnp.sum(inner * kt, axis=0, keepdims=True)
    label = lax.broadcasted_iota(jnp.int32, (EX, TOK), 0)
    score = 0.5 * jnp.sum(jnp.where(ids[...] == label, token, 0.0), axis=1, keepdims=True)
    sc1[z] = jnp.broadcast_to(score, (EX, 128))
    for k in range(1, NZ):
        send(sc1.at[z], sc1.at[z], R_S1 + z, zdev(k))

    step_of_gather(1)
    for k in range(1, NZ):
        got(sc1.at[at(k)], R_S1 + at(k))
    sc2[m] = jnp.sum(sc1[...], axis=0)
    for k in range(1, NM):
        send(sc2.at[m], sc2.at[m], R_S2 + m, mdev(k))

    step_of_gather(2)
    for k in range(1, NM):
        j = (m + k) % NM
        got(sc2.at[j], R_S2 + j)
    slot = xh * 2 + c
    sc3[slot] = jnp.sum(sc2[...], axis=0)
    for to in (other, across, diagonal):
        send(sc3.at[slot], sc3.at[slot], R_S3 + slot, to)

    step_of_gather(3)
    for k in range(1, 4):
        j = (slot + k) % 4
        got(sc3.at[j], R_S3 + j)
    score = jnp.sum(sc3[...], axis=0)
    rms = jnp.sqrt(jnp.mean(score * score, axis=0, keepdims=True) + 1e-6)
    arg = score / (4.0 * rms)
    soft = jnp.maximum(arg, 0.0) + jnp.log(1.0 + jnp.exp(-jnp.abs(arg)))
    weights = EX * soft / jnp.sum(soft, axis=0, keepdims=True)
    diag = lax.broadcasted_iota(jnp.int32, (EX, 128), 0) == lax.broadcasted_iota(jnp.int32, (EX, 128), 1)
    wts_out[...] = jnp.sum(jnp.where(diag, weights, 0.0), axis=0, keepdims=True)[:, :EX]
    e_row = jnp.zeros((1, TOK), F32)
    for e in range(EX):
        e_row = e_row + jnp.where(ids[...] == e, weights[e : e + 1, 0:1], 0.0)
    for i in range(2):
        xs[i] = (xt[i] * e_row).astype(BF)
    copy = pltpu.make_async_copy(xs, xs_out, hsem.at[16])
    copy.start()
    outs.append(copy)

    step_of_gather(4)
    for k in range(NZ):
        flush(2 * at(k) + c, k)
    for k in range(NZ):
        block = 2 * at(k) + 1 - c
        got(full.at[block], R_AC + at(k))
        flush(block, 8 + k)
    for copy in sends:
        copy.wait_send()
    for copy in outs:
        copy.wait()


def grad_kernel(full, xs, gg, gu, gd):
    def rows(i):
        return jnp.concatenate(
            [full[:, i].reshape(8 * HB, 128), full[:, 3 + i].reshape(8 * HB, 128)], axis=1
        )

    gd[...] = nt(rows(0), xs[1]).astype(BF)
    gg[...] = nt(xs[0], rows(1)).astype(BF)
    gu[...] = nt(xs[0], rows(2)).astype(BF)


def body(train_x, train_cot, val_x, val_cot, w_gate, w_up, w_down, step_weights, example_ids, val_mask):
    hbm = pl.BlockSpec(memory_space=pl.ANY)
    vmem = pl.BlockSpec(memory_space=pltpu.VMEM)
    V = pltpu.VMEM
    full, xs, wts = pl.pallas_call(
        comm_kernel,
        out_shape=(
            jax.ShapeDtypeStruct((16, 6, HB, 128), BF),
            jax.ShapeDtypeStruct((2, W, TOK), BF),
            jax.ShapeDtypeStruct((1, EX), F32),
        ),
        in_specs=[hbm, hbm, vmem, vmem, hbm, hbm, hbm, pl.BlockSpec(memory_space=pltpu.SMEM), vmem, vmem],
        out_specs=(hbm, hbm, vmem),
        scratch_shapes=[
            V((2, W, 1792), BF),
            V((16, 3, HB, W), BF),
            V((NZ, 3, HB, W), BF),
            V((80, W), BF),
            V((16, W), F32),
            V((NM, 80, W), BF),
            V((NM, 80, W), BF),
            V((3, 128, W), BF),
            V((3, 128, W), BF),
            V((NZ, 7, HB, 128), F32),
            V((16, 6, HB, 128), BF),
            V((4, 4, HB, 128), BF),
            V((4, 4, HB, 128), BF),
            V((4, 3, HB, 128), BF),
            V((4, 3, HB, 128), BF),
            V((3, 3, HB, 128), BF),
            V((3, 3, HB, 128), BF),
            V((3, 4, HB, 128), BF),
            V((3, 4, HB, 128), BF),
            V((7, HB, 128), BF),
            V((7, HB, 128), BF),
            V((NZ, 16, 128), F32),
            V((NZ, 16, 128), F32),
            V((2, 16, 128), F32),
            V((2, NZ, 16, 128), F32),
            V((NZ, EX, 128), F32),
            V((NM, EX, 128), F32),
            V((4, EX, 128), F32),
            V((2, W, TOK), F32),
            V((2, W, TOK), BF),
            pltpu.SemaphoreType.DMA((5,)),
            pltpu.SemaphoreType.DMA((120,)),
            pltpu.SemaphoreType.DMA((104,)),
            pltpu.SemaphoreType.DMA((17,)),
        ],
        compiler_params=pltpu.CompilerParams(
            collective_id=0, has_side_effects=True, vmem_limit_bytes=40 * 1024 * 1024
        ),
        name="reduce_and_gather",
    )(
        train_x, train_cot, val_x, val_cot, w_gate, w_up, w_down.reshape(16, HB, W),
        step_weights, example_ids.reshape(1, TOK), val_mask.reshape(1, 32),
    )
    gg, gu, gd = pl.pallas_call(
        grad_kernel,
        grid=(2,),
        out_shape=(
            jax.ShapeDtypeStruct((W, 1792), BF),
            jax.ShapeDtypeStruct((W, 1792), BF),
            jax.ShapeDtypeStruct((1792, W), BF),
        ),
        in_specs=[
            pl.BlockSpec((8, 6, HB, 128), lambda i: (i, 0, 0, 0)),
            pl.BlockSpec((2, W, TOK), lambda i: (0, 0, 0)),
        ],
        out_specs=(
            pl.BlockSpec((W, 8 * HB), lambda i: (0, i)),
            pl.BlockSpec((W, 8 * HB), lambda i: (0, i)),
            pl.BlockSpec((8 * HB, W), lambda i: (i, 0)),
        ),
        compiler_params=pltpu.CompilerParams(vmem_limit_bytes=40 * 1024 * 1024),
        name="gradients",
    )(full, xs)
    return gg, gu, gd, wts.reshape(EX)


def solution(mesh):
    wide, tall = P("dp", "mp"), P("mp", "dp")
    return jax.shard_map(
        body,
        mesh=mesh,
        in_specs=(tall, tall, tall, tall, wide, wide, tall, P(), P(), P()),
        out_specs=(wide, wide, tall, P()),
        check_vma=False,
    )
```

```python
import jax
import jax.numpy as jnp
from jax import lax
from jax.experimental import pallas as pl
from jax.experimental.pallas import tpu as pltpu
from jax.sharding import PartitionSpec as P

MESH = pl.DeviceIdType.MESH
BF = jnp.bfloat16
F32 = jnp.float32

LEARN_RATE = 0.0003
NZ = 8
NM = 8
HB = 112
TOK = 256
W = 256
EX = 8


def nt(left, right):
    return lax.dot_general(left, right, (((1,), (1,)), ((), ())), preferred_element_type=F32)


def tn(left, right):
    return lax.dot_general(left, right, (((0,), (0,)), ((), ())), preferred_element_type=F32)


def comm_kernel(
    x_in, c_in, vx_in, vc_in, wg_in, wu_in, wd_in, sw_in, ids_in, mask_in,
    full, xs_out, wts_out,
    sw, ids, mask, vraw, wraw, wt, wo, pk, vstage, xb, xo, va, vo, part, own,
    ring_s, ring_d, swap_p, swap_d, gram_s, gram_d, gram_x, gram_all, sc1, sc2, xt, xs,
    lsem, ssem, rsem, hsem,
):
    d = lax.axis_index("dp")
    m = lax.axis_index("mp")
    z = d // 4
    xh = (d // 2) % 2
    c = d % 2
    slot = z * 2 + c

    def dev(zz, xx, cc):
        return (zz * 4 + xx * 2 + cc, m)

    def at(step):
        return (z + step + NZ) % NZ

    def zdev(step):
        return dev(at(step), xh, c)

    def mdev(step):
        return (d, (m + step) % NM)

    def pdev(step):
        j = (slot + step) % 16
        return dev(j // 2, xh, j % 2)

    other = dev(z, xh, 1 - c)
    across = dev(z, 1 - xh, c)
    right, left = zdev(1), zdev(-1)

    sends = []

    def send(src, dst, rs, to):
        copy = pltpu.make_async_remote_copy(
            src_ref=src, dst_ref=dst, send_sem=ssem.at[len(sends)], recv_sem=rsem.at[rs],
            device_id=to, device_id_type=MESH,
        )
        copy.start()
        sends.append(copy)

    def got(dst, rs):
        pltpu.make_async_copy(dst, dst, rsem.at[rs]).wait()

    R_X, R_XO, R_W, R_RING = 0, 8, 16, 24
    R_P, R_SHORT, R_LONG = 80, 81, 88
    R_GS, R_GX, R_GA, R_GC = 96, 104, 105, 113
    R_A, R_AC, R_S1, R_S2 = 114, 162, 171, 187

    loads = [
        pltpu.make_async_copy(x_in, pk.at[0:32], lsem.at[0]),
        pltpu.make_async_copy(c_in, pk.at[32:64], lsem.at[1]),
        pltpu.make_async_copy(wg_in, wraw.at[0], lsem.at[2]),
        pltpu.make_async_copy(wu_in, wraw.at[1], lsem.at[3]),
        pltpu.make_async_copy(vx_in, vraw.at[0], lsem.at[4]),
        pltpu.make_async_copy(vc_in, vraw.at[1], lsem.at[5]),
        pltpu.make_async_copy(wd_in.at[:, 0], wt.at[0, :, 2], lsem.at[6]),
        pltpu.make_async_copy(wd_in.at[:, 1], wt.at[1, :, 2], lsem.at[7]),
        pltpu.make_async_copy(sw_in, sw, lsem.at[8]),
        pltpu.make_async_copy(ids_in, ids, lsem.at[9]),
        pltpu.make_async_copy(mask_in, mask, lsem.at[10]),
    ]
    for copy in loads:
        copy.start()

    barrier = pltpu.get_barrier_semaphore()
    peers = [mdev(k) for k in range(1, NM)] + [across] + [pdev(k) for k in range(1, 16)]
    for peer in peers:
        pl.semaphore_signal(barrier, inc=1, device_id=peer, device_id_type=MESH)

    vstage[0:16] = jnp.zeros((16, W), F32)
    loads[4].wait()
    loads[5].wait()
    vstage[0:4] = vraw[0].astype(F32)
    vstage[4:8] = vraw[0].astype(F32)
    vstage[8:12] = vraw[1].astype(F32)
    pk[64:80] = vstage[0:16].astype(BF)
    loads[0].wait()
    loads[1].wait()
    xb[m] = pk[...]
    pl.semaphore_wait(barrier, len(peers))

    for k in range(1, NM):
        send(pk, xb.at[m], R_X + m, mdev(k))
    send(pk, xo.at[m], R_XO + m, other)

    for w in range(2):
        loads[2 + w].wait()
        for i in range(14):
            block = wraw[w, :, 128 * i : 128 * (i + 1)].T
            row = 128 * i
            while row < 128 * (i + 1):
                b = row // HB
                end = min(128 * (i + 1), (b + 1) * HB)
                wt[b % 2, b // 2, w, row - b * HB : end - b * HB] = block[row - 128 * i : end - 128 * i]
                row = end
    loads[6].wait()
    loads[7].wait()
    for step in (4, 3, 5, 2, 6, 1, 7, 0):
        send(wt.at[1 - c, at(step)], wo.at[at(step)], R_W + at(step), other)

    for k in range(1, NM):
        j = (m + NM - k) % NM
        got(xb.at[j], R_X + j)
        send(xb.at[j], xo.at[j], R_XO + j, other)
    for k in range(NM):
        j = (m + NM - k) % NM
        got(xo.at[j], R_XO + j)

    place = lax.broadcasted_iota(jnp.int32, (128, W), 0) % 16
    for src, dst in ((xb, va), (xo, vo)):
        rows = src[:, 64:80, :].reshape(128, W).astype(F32)
        for i in range(3):
            keep = jnp.logical_and(place >= 4 * i, place < 4 * i + 4)
            dst[i] = jnp.where(keep, rows, 0.0).astype(BF)

    def tokens(ref, first):
        return ref[:, 32 * first : 32 * first + 32, :].reshape(TOK, W)

    A, B = (0, 1, 2, 3), (4, 5, 6)
    RIGHT, LEFT = 0, 1
    to_dev = (right, left)

    def first(way, slab, value):
        ring_s[way, 0, slab] = value.astype(BF)
        send(ring_s.at[way, 0, slab], ring_d.at[way, 0, slab], R_RING + way * 28 + slab, to_dev[way])

    def arrived(way, s, slab):
        got(ring_d.at[way, s - 1, slab], R_RING + (way * 4 + s - 1) * 7 + slab)

    def onward(way, s, slab, step):
        arrived(way, s, slab)
        value = part[at(step), slab] + ring_d[way, s - 1, slab].astype(F32)
        ring_s[way, s, slab] = value.astype(BF)
        send(
            ring_s.at[way, s, slab], ring_d.at[way, s, slab],
            R_RING + (way * 4 + s) * 7 + slab, to_dev[way],
        )

    far = at(4)
    got(wo.at[far], R_W + far)
    for i in range(3):
        which = 1 if i == 2 else 0
        total = nt(wt[c, far, i], tokens(xb, which)) + nt(wo[far, i], tokens(xo, which))
        first(RIGHT, i, total[:, :128])
        first(LEFT, 4 + i, total[:, 128:])
    val = jnp.zeros((HB, 128), F32)
    for i in range(3):
        val = val + nt(wt[c, far, i], va[i]) + nt(wo[far, i], vo[i])
    first(RIGHT, 3, val)

    for k in range(1, NZ):
        got(wo.at[at(4 + k)], R_W + at(4 + k))
    val = jnp.zeros((NZ * HB, 128), F32)
    for i in range(3):
        which = 1 if i == 2 else 0
        lhs, lho = wt[c, :, i].reshape(NZ * HB, W), wo[:, i].reshape(NZ * HB, W)
        total = nt(lhs, tokens(xb, which)) + nt(lho, tokens(xo, which))
        part[:, i] = total[:, :128].reshape(NZ, HB, 128)
        part[:, 4 + i] = total[:, 128:].reshape(NZ, HB, 128)
        first(LEFT, i, part[at(-3), i])
        first(RIGHT, 4 + i, part[at(3), 4 + i])
        val = val + nt(lhs, va[i]) + nt(lho, vo[i])
    part[:, 3] = val.reshape(NZ, HB, 128)
    first(LEFT, 3, part[at(-3), 3])
    send(part.at[z], swap_p, R_P, across)

    def both_long(s):
        for i in range(4):
            onward(RIGHT, s, A[i], 4 - s)
            if i < 3:
                onward(LEFT, s, B[i], s - 4)

    def both_short(s):
        for i in range(4):
            if i < 3:
                onward(RIGHT, s, B[i], 3 - s)
            onward(LEFT, s, A[i], s - 3)

    def half(ref, which):
        return ref[pl.ds(4 * c, 4), 32 * which : 32 * which + 32, :].reshape(128, W)

    gram = nt(va[0], half(xb, 0)) + nt(vo[0], half(xo, 0)) + nt(va[2], half(xb, 1)) + nt(vo[2], half(xo, 1))
    gram_s[...] = gram.reshape(NZ, 16, 128)
    gram_d[z] = gram_s[z]
    for k in range(1, NZ):
        send(gram_s.at[at(k)], gram_d.at[z], R_GS + z, zdev(k))

    both_long(1)
    both_short(1)
    for copy in loads[8:]:
        copy.wait()
    for k in range(1, NZ):
        got(gram_d.at[at(k)], R_GS + at(k))
    gram_x[0] = jnp.sum(gram_d[...], axis=0)
    send(gram_x.at[0], gram_x.at[1], R_GX, across)
    both_long(2)
    both_short(2)
    got(gram_x.at[1], R_GX)
    gram_all[c, z] = gram_x[0] + gram_x[1]
    for k in range(1, NZ):
        send(gram_all.at[c, z], gram_all.at[c, z], R_GA + z, zdev(k))
    both_long(3)

    def pass_on(way, s, slab, dst, rs):
        arrived(way, s, slab)
        send(ring_d.at[way, s - 1, slab], swap_d.at[dst, slab], rs + slab, across)

    for i in range(4):
        if i < 3:
            pass_on(RIGHT, 3, B[i], 0, R_SHORT)
        pass_on(LEFT, 3, A[i], 0, R_SHORT)
    r_row = jnp.zeros((1, TOK), F32)
    for e in range(EX):
        r_row = r_row + jnp.where(ids[...] == e, sw[e], 0.0)
    for i in range(2):
        xt[i] = tokens(xb, i).T.astype(F32)
    for k in range(1, NZ):
        got(gram_all.at[c, at(k)], R_GA + at(k))
    send(gram_all.at[c], gram_all.at[c], R_GC, other)
    got(swap_p, R_P)
    for i in range(4):
        pass_on(RIGHT, 4, A[i], 1, R_LONG)
        if i < 3:
            pass_on(LEFT, 4, B[i], 1, R_LONG)

    def whole(slab):
        way = RIGHT if slab < 4 else LEFT
        mine_ = part[z, slab] + ring_d[1 - way, 2, slab].astype(F32) + ring_d[way, 3, slab].astype(F32)
        got(swap_d.at[0, slab], R_SHORT + slab)
        got(swap_d.at[1, slab], R_LONG + slab)
        theirs = swap_p[slab] + swap_d[0, slab].astype(F32) + swap_d[1, slab].astype(F32)
        return mine_ + theirs

    def block_terms(gate, up, back):
        sig = 1.0 / (1.0 + jnp.exp(-gate))
        act = gate * sig
        return act * up, back * up * sig * (1.0 + gate * (1.0 - sig)), back * act

    def gather(src, block, way, step, slab):
        send(
            src, full.at[block, slab], R_A + (way * 4 + step - 1) * 6 + slab, to_dev[way]
        )

    for h in range(2):
        terms = block_terms(*[whole(4 * h + i) for i in range(3)])
        for i in range(3):
            own[3 * h + i] = terms[i].astype(BF)
            gather(own.at[3 * h + i], slot, RIGHT, 1, 3 * h + i)
            gather(own.at[3 * h + i], slot, LEFT, 1, 3 * h + i)
    send(own, full.at[slot], R_AC + z, other)
    outs = [pltpu.make_async_copy(own, full.at[slot], hsem.at[0])]
    outs[0].start()

    def step_of_gather(step):
        blocks = [2 * at(-step) + c, 2 * at(step) + c]
        for i in range(6):
            for way in (RIGHT, LEFT):
                if step == 4 and i // 3 != way:
                    continue
                got(full.at[blocks[way], i], R_A + (way * 4 + step - 1) * 6 + i)
                if step < 3 or (step == 3 and i // 3 == way):
                    gather(full.at[blocks[way], i], blocks[way], way, step + 1, i)
        if step < 4:
            for way, zz in ((RIGHT, at(-step)), (LEFT, at(step))):
                send(full.at[blocks[way]], full.at[blocks[way]], R_AC + zz, other)
        else:
            send(full.at[blocks[0]], full.at[blocks[0]], R_AC + at(4), other)

    got(gram_all.at[1 - c], R_GC)
    kt = jnp.concatenate([gram_all[0].reshape(128, 128), gram_all[1].reshape(128, 128)], axis=1)
    rk = (kt * r_row).astype(BF)
    hb, dgb, dub = [jnp.concatenate([own[i], own[3 + i]], axis=1) for i in range(3)]
    val = whole(3)
    v_gate = val - LEARN_RATE * nt(dgb, rk)
    v_up = pltpu.roll(val, 124, 1) - LEARN_RATE * nt(dub, rk)
    v_back = pltpu.roll(val - LEARN_RATE * nt(hb, rk), 120, 1)
    lane = lax.broadcasted_iota(jnp.int32, (32, 128), 1)
    row = lax.broadcasted_iota(jnp.int32, (32, 128), 0)
    pick = jnp.logical_and(lane % 16 < 4, (lane // 16) * 4 + lane % 16 == row)
    mask_f = jnp.broadcast_to(mask[...].astype(F32), (16, 32)).astype(BF)
    mask_l = lax.dot_general(
        mask_f, jnp.where(pick, 1.0, 0.0).astype(BF), (((1,), (0,)), ((), ())), preferred_element_type=F32
    )[0:1]
    keep = jnp.broadcast_to(mask_l, (HB, 128)) > 0.5
    v_hid, v_dg, v_du = [jnp.where(keep, t, 0.0) for t in block_terms(v_gate, v_up, v_back)]
    inner = tn(v_dg.astype(BF), dgb) + tn(v_du.astype(BF), dub) + tn(pltpu.roll(v_hid, 8, 1).astype(BF), hb)
    token = jnp.sum(inner * kt, axis=0, keepdims=True)
    label = lax.broadcasted_iota(jnp.int32, (EX, TOK), 0)
    score = jnp.sum(jnp.where(ids[...] == label, token, 0.0), axis=1, keepdims=True)
    sc1[slot] = jnp.broadcast_to(score, (EX, 128))
    for k in range(1, 16):
        send(sc1.at[slot], sc1.at[slot], R_S1 + slot, pdev(k))

    step_of_gather(1)
    step_of_gather(2)
    for k in range(1, 16):
        j = (slot + k) % 16
        got(sc1.at[j], R_S1 + j)
    sc2[m] = jnp.sum(sc1[...], axis=0)
    for k in range(1, NM):
        send(sc2.at[m], sc2.at[m], R_S2 + m, mdev(k))

    step_of_gather(3)
    for k in range(1, NM):
        j = (m + k) % NM
        got(sc2.at[j], R_S2 + j)
    score = jnp.sum(sc2[...], axis=0)
    rms = jnp.sqrt(jnp.mean(score * score, axis=0, keepdims=True) + 1e-6)
    arg = score / (4.0 * rms)
    soft = jnp.maximum(arg, 0.0) + jnp.log(1.0 + jnp.exp(-jnp.abs(arg)))
    weights = EX * soft / jnp.sum(soft, axis=0, keepdims=True)
    diag = lax.broadcasted_iota(jnp.int32, (EX, 128), 0) == lax.broadcasted_iota(jnp.int32, (EX, 128), 1)
    wts_out[...] = jnp.sum(jnp.where(diag, weights, 0.0), axis=0, keepdims=True)[:, :EX]
    e_row = jnp.zeros((1, TOK), F32)
    for e in range(EX):
        e_row = e_row + jnp.where(ids[...] == e, weights[e : e + 1, 0:1], 0.0)
    for i in range(2):
        xs[i] = (xt[i] * e_row).astype(BF)
    copy = pltpu.make_async_copy(xs, xs_out, hsem.at[1])
    copy.start()
    outs.append(copy)

    step_of_gather(4)
    for k in range(NZ):
        got(full.at[2 * at(k) + 1 - c], R_AC + at(k))
    for copy in sends:
        copy.wait_send()
    for copy in outs:
        copy.wait()


def grad_kernel(full, xs, wts, gg, gu, gd, out):
    def rows(i):
        return jnp.concatenate(
            [full[:, i].reshape(8 * HB, 128), full[:, 3 + i].reshape(8 * HB, 128)], axis=1
        )

    out[...] = wts[...]
    gd[...] = nt(rows(0), xs[1]).astype(BF)
    gg[...] = nt(xs[0], rows(1)).astype(BF)
    gu[...] = nt(xs[0], rows(2)).astype(BF)


def body(train_x, train_cot, val_x, val_cot, w_gate, w_up, w_down, step_weights, example_ids, val_mask):
    hbm = pl.BlockSpec(memory_space=pltpu.HBM)
    free = pl.BlockSpec(memory_space=pl.ANY)
    vmem = pl.BlockSpec(memory_space=pltpu.VMEM)
    V = pltpu.VMEM
    full, xs, wts = pl.pallas_call(
        comm_kernel,
        out_shape=(
            jax.ShapeDtypeStruct((16, 6, HB, 128), BF),
            jax.ShapeDtypeStruct((2, W, TOK), BF),
            jax.ShapeDtypeStruct((1, EX), F32),
        ),
        in_specs=[hbm] * 10,
        out_specs=(free, free, vmem),
        scratch_shapes=[
            pltpu.SMEM((EX,), F32),
            V((1, TOK), jnp.int32),
            V((1, 32), jnp.int32),
            V((2, 4, W), BF),
            V((2, W, 1792), BF),
            V((2, NZ, 3, HB, W), BF),
            V((NZ, 3, HB, W), BF),
            V((80, W), BF),
            V((16, W), F32),
            V((NM, 80, W), BF),
            V((NM, 80, W), BF),
            V((3, 128, W), BF),
            V((3, 128, W), BF),
            V((NZ, 7, HB, 128), F32),
            V((6, HB, 128), BF),
            V((2, 4, 7, HB, 128), BF),
            V((2, 4, 7, HB, 128), BF),
            V((7, HB, 128), F32),
            V((2, 7, HB, 128), BF),
            V((NZ, 16, 128), F32),
            V((NZ, 16, 128), F32),
            V((2, 16, 128), F32),
            V((2, NZ, 16, 128), F32),
            V((16, EX, 128), F32),
            V((NM, EX, 128), F32),
            V((2, W, TOK), F32),
            V((2, W, TOK), BF),
            pltpu.SemaphoreType.DMA((11,)),
            pltpu.SemaphoreType.DMA((200,)),
            pltpu.SemaphoreType.DMA((195,)),
            pltpu.SemaphoreType.DMA((2,)),
        ],
        compiler_params=pltpu.CompilerParams(
            collective_id=0, has_side_effects=True, vmem_limit_bytes=40 * 1024 * 1024
        ),
        name="reduce_and_gather",
    )(
        *[
            pltpu.with_memory_space_constraint(a, pltpu.HBM)
            for a in (
                train_x, train_cot, val_x, val_cot, w_gate, w_up, w_down.reshape(NZ, 2, HB, W),
                step_weights, example_ids.reshape(1, TOK), val_mask.reshape(1, 32),
            )
        ]
    )
    gg, gu, gd, out = pl.pallas_call(
        grad_kernel,
        grid=(2,),
        out_shape=(
            jax.ShapeDtypeStruct((W, 1792), BF),
            jax.ShapeDtypeStruct((W, 1792), BF),
            jax.ShapeDtypeStruct((1792, W), BF),
            jax.ShapeDtypeStruct((1, EX), F32),
        ),
        in_specs=[
            pl.BlockSpec((8, 6, HB, 128), lambda i: (i, 0, 0, 0)),
            pl.BlockSpec((2, W, TOK), lambda i: (0, 0, 0)),
            pl.BlockSpec((1, EX), lambda i: (0, 0)),
        ],
        out_specs=(
            pl.BlockSpec((W, 8 * HB), lambda i: (0, i)),
            pl.BlockSpec((W, 8 * HB), lambda i: (0, i)),
            pl.BlockSpec((8 * HB, W), lambda i: (i, 0)),
            pl.BlockSpec((1, EX), lambda i: (0, 0)),
        ),
        compiler_params=pltpu.CompilerParams(vmem_limit_bytes=40 * 1024 * 1024),
        name="gradients",
    )(full, xs, wts)
    return gg, gu, gd, out.reshape(EX)


def solution(mesh):
    wide, tall = P("dp", "mp"), P("mp", "dp")
    return jax.shard_map(
        body,
        mesh=mesh,
        in_specs=(tall, tall, tall, tall, wide, wide, tall, P(), P(), P()),
        out_specs=(wide, wide, tall, P()),
        check_vma=False,
    )
```

```python
import jax
import jax.numpy as jnp
from jax import lax
from jax.experimental import pallas as pl
from jax.experimental.pallas import tpu as pltpu
from jax.sharding import PartitionSpec as P

MESH = pl.DeviceIdType.MESH
BF = jnp.bfloat16
F32 = jnp.float32

LEARN_RATE = 0.0003
NZ = 8
NM = 8
HB = 112
TOK = 256
W = 256
EX = 8


def nt(left, right):
    return lax.dot_general(left, right, (((1,), (1,)), ((), ())), preferred_element_type=F32)


def tn(left, right):
    return lax.dot_general(left, right, (((0,), (0,)), ((), ())), preferred_element_type=F32)


def comm_kernel(
    x_in, c_in, vx_in, vc_in, wg_in, wu_in, wd_in, sw_in, ids_in, mask_in,
    full, xs_out, wts_out,
    sw, ids, mask, vraw, wraw, wt, wo, pk, vstage, xb, xo, va, vo, part, vpart, own,
    pair_s, pair_d, ring_s, ring_d, last_s, last_d, swap_p, swap_d,
    gram_s, gram_d, gram_x, gram_all, sc1, sc2, sc3, xt, xs,
    lsem, ssem, rsem, hsem,
):
    d = lax.axis_index("dp")
    m = lax.axis_index("mp")
    z = d // 4
    xh = (d // 2) % 2
    c = d % 2
    slot = z * 2 + c

    def dev(zz, xx, cc):
        return (zz * 4 + xx * 2 + cc, m)

    def at(step):
        return (z + step + NZ) % NZ

    def zdev(step):
        return dev(at(step), xh, c)

    def mdev(step):
        return (d, (m + step) % NM)

    other = dev(z, xh, 1 - c)
    across = dev(z, 1 - xh, c)
    right, left = zdev(1), zdev(-1)

    sends = []

    def send(src, dst, rs, to):
        copy = pltpu.make_async_remote_copy(
            src_ref=src, dst_ref=dst, send_sem=ssem.at[len(sends)], recv_sem=rsem.at[rs],
            device_id=to, device_id_type=MESH,
        )
        copy.start()
        sends.append(copy)

    def got(dst, rs):
        pltpu.make_async_copy(dst, dst, rsem.at[rs]).wait()

    R_X, R_XO, R_W, R_PAIR, R_RING = 0, 8, 16, 24, 32
    R_P, R_SHORT, R_LONG = 64, 65, 66
    R_GS, R_GX, R_GA, R_GC = 67, 75, 76, 84
    R_A, R_OWN, R_AC = 85, 133, 134
    R_S1, R_S2, R_S3 = 150, 158, 159

    loads = [
        pltpu.make_async_copy(x_in, pk.at[0:32], lsem.at[0]),
        pltpu.make_async_copy(c_in, pk.at[32:64], lsem.at[1]),
        pltpu.make_async_copy(wg_in, wraw.at[0], lsem.at[2]),
        pltpu.make_async_copy(wu_in, wraw.at[1], lsem.at[3]),
        pltpu.make_async_copy(vx_in, vraw.at[0], lsem.at[4]),
        pltpu.make_async_copy(vc_in, vraw.at[1], lsem.at[5]),
        pltpu.make_async_copy(wd_in.at[:, 0], wt.at[0, :, 2], lsem.at[6]),
        pltpu.make_async_copy(wd_in.at[:, 1], wt.at[1, :, 2], lsem.at[7]),
        pltpu.make_async_copy(sw_in, sw, lsem.at[8]),
        pltpu.make_async_copy(ids_in, ids, lsem.at[9]),
        pltpu.make_async_copy(mask_in, mask, lsem.at[10]),
    ]
    for copy in loads:
        copy.start()

    barrier = pltpu.get_barrier_semaphore()
    peers = [mdev(k) for k in range(1, NM)] + [across, other] + [zdev(k) for k in range(1, NZ)]
    for peer in peers:
        pl.semaphore_signal(barrier, inc=1, device_id=peer, device_id_type=MESH)

    vstage[0:16] = jnp.zeros((16, W), F32)
    loads[4].wait()
    loads[5].wait()
    vstage[0:4] = vraw[0].astype(F32)
    vstage[4:8] = vraw[0].astype(F32)
    vstage[8:12] = vraw[1].astype(F32)
    pk[64:80] = vstage[0:16].astype(BF)
    loads[0].wait()
    loads[1].wait()
    xb[m] = pk[...]
    pl.semaphore_wait(barrier, len(peers))

    for k in range(1, NM):
        send(pk, xb.at[m], R_X + m, mdev(k))
    send(pk, xo.at[m], R_XO + m, other)

    for w in range(2):
        loads[2 + w].wait()
        for i in range(14):
            block = wraw[w, :, 128 * i : 128 * (i + 1)].T
            row = 128 * i
            while row < 128 * (i + 1):
                b = row // HB
                end = min(128 * (i + 1), (b + 1) * HB)
                wt[b % 2, b // 2, w, row - b * HB : end - b * HB] = block[row - 128 * i : end - 128 * i]
                row = end
    loads[6].wait()
    loads[7].wait()
    for step in (4, 3, 5, 2, 6, 1, 7, 0):
        send(wt.at[1 - c, at(step)], wo.at[at(step)], R_W + at(step), other)

    for k in range(1, NM):
        j = (m + NM - k) % NM
        got(xb.at[j], R_X + j)
        send(xb.at[j], xo.at[j], R_XO + j, other)
    place = lax.broadcasted_iota(jnp.int32, (128, W), 0) % 16

    def spread(src, dst):
        rows = src[:, 64:80, :].reshape(128, W).astype(F32)
        for i in range(3):
            keep = jnp.logical_and(place >= 4 * i, place < 4 * i + 4)
            dst[i] = jnp.where(keep, rows, 0.0).astype(BF)

    def tokens(ref, first):
        return ref[:, 32 * first : 32 * first + 32, :].reshape(TOK, W)

    spread(xb, va)
    val = jnp.zeros((NZ * HB, 128), F32)
    for i in range(3):
        lhs = wt[c, :, i].reshape(NZ * HB, W)
        total = nt(lhs, tokens(xb, 1 if i == 2 else 0))
        part[:, 0, i] = total[:, :128].reshape(NZ, HB, 128)
        part[:, 1, i] = total[:, 128:].reshape(NZ, HB, 128)
        val = val + nt(lhs, va[i])
    vpart[...] = val.reshape(NZ, HB, 128)
    for k in range(NM):
        j = (m + NM - k) % NM
        got(xo.at[j], R_XO + j)
    spread(xo, vo)

    def pair(step):
        send(pair_s.at[at(step)], pair_d.at[at(step)], R_PAIR + at(step), across)

    far = at(4)
    got(wo.at[far], R_W + far)
    away = xo[pl.ds(4 * (1 - xh), 4)]
    for i in range(3):
        which = 32 if i == 2 else 0
        total = nt(wo[far, i], away[:, which : which + 32, :].reshape(128, W))
        pair_s[far, i] = (part[far, 1 - xh, i] + total).astype(BF)
    pair(4)
    for k in range(1, NZ):
        got(wo.at[at(4 + k)], R_W + at(4 + k))
    val = jnp.zeros((NZ * HB, 128), F32)
    for i in range(3):
        lhs = wo[:, i].reshape(NZ * HB, W)
        total = nt(lhs, tokens(xo, 1 if i == 2 else 0))
        part[:, 0, i] = part[:, 0, i] + total[:, :128].reshape(NZ, HB, 128)
        part[:, 1, i] = part[:, 1, i] + total[:, 128:].reshape(NZ, HB, 128)
        val = val + nt(lhs, vo[i])
    vpart[...] = vpart[...] + val.reshape(NZ, HB, 128)
    for step in (3, -3, 2, -2, 1, -1, 0):
        pair_s[at(step)] = part[at(step), 1 - xh].astype(BF)
        pair(step)
    send(vpart.at[z], swap_p, R_P, across)

    A, B = (0, 1), (2, 3)
    RIGHT, LEFT = 0, 1
    to_dev = (right, left)

    def here(step, slab):
        if slab == 3:
            return vpart[at(step)]
        return part[at(step), xh, slab] + pair_d[at(step), slab].astype(F32)

    def paired(step):
        got(pair_d.at[at(step)], R_PAIR + at(step))

    def wide(way, s, slab):
        far_first = (slab in A) == (way == RIGHT)
        return slab < 3 and s == (3 if far_first else 2)

    def buffers(way, s, slab):
        if wide(way, s, slab):
            return last_s.at[way, slab], last_d.at[way, slab]
        return ring_s.at[way, s, slab], ring_d.at[way, s, slab]

    def ring(way, s, slab, value):
        src, dst = buffers(way, s, slab)
        src[...] = value.astype(src.dtype)
        send(src, dst, R_RING + (way * 4 + s) * 4 + slab, to_dev[way])

    def arrived(way, s, slab):
        src, dst = buffers(way, s - 1, slab)
        got(dst, R_RING + (way * 4 + s - 1) * 4 + slab)
        return dst

    def onward(way, s, slab, step):
        dst = arrived(way, s, slab)
        ring(way, s, slab, here(step, slab) + dst[...].astype(F32))

    def both_long(s):
        for i in range(2):
            onward(RIGHT, s, A[i], 4 - s)
            onward(LEFT, s, B[i], s - 4)

    def both_short(s):
        for i in range(2):
            onward(RIGHT, s, B[i], 3 - s)
            onward(LEFT, s, A[i], s - 3)

    def half(ref, which):
        return ref[pl.ds(4 * c, 4), 32 * which : 32 * which + 32, :].reshape(128, W)

    gram = nt(va[0], half(xb, 0)) + nt(vo[0], half(xo, 0)) + nt(va[2], half(xb, 1)) + nt(vo[2], half(xo, 1))
    gram_s[...] = gram.reshape(NZ, 16, 128)
    gram_d[z] = gram_s[z]
    for k in range(1, NZ):
        send(gram_s.at[at(k)], gram_d.at[z], R_GS + z, zdev(k))

    paired(4)
    for i in range(2):
        ring(RIGHT, 0, A[i], here(4, A[i]))
        ring(LEFT, 0, B[i], here(4, B[i]))
    paired(3)
    for i in range(2):
        ring(RIGHT, 0, B[i], here(3, B[i]))
    paired(-3)
    for i in range(2):
        ring(LEFT, 0, A[i], here(-3, A[i]))
    both_long(1)
    for copy in loads[8:]:
        copy.wait()
    for k in range(1, NZ):
        got(gram_d.at[at(k)], R_GS + at(k))
    gram_x[0] = jnp.sum(gram_d[...], axis=0)
    send(gram_x.at[0], gram_x.at[1], R_GX, across)
    paired(2)
    paired(-2)
    both_short(1)
    both_long(2)
    got(gram_x.at[1], R_GX)
    gram_all[c, z] = gram_x[0] + gram_x[1]
    for k in range(1, NZ):
        send(gram_all.at[c, z], gram_all.at[c, z], R_GA + z, zdev(k))
    paired(1)
    paired(-1)
    both_short(2)
    both_long(3)

    r_row = jnp.zeros((1, TOK), F32)
    for e in range(EX):
        r_row = r_row + jnp.where(ids[...] == e, sw[e], 0.0)
    for i in range(2):
        xt[i] = tokens(xb, i).T.astype(F32)
    paired(0)
    for k in range(1, NZ):
        got(gram_all.at[c, at(k)], R_GA + at(k))
    send(gram_all.at[c], gram_all.at[c], R_GC, other)
    short_v = arrived(RIGHT, 3, 3)
    send(short_v, swap_d.at[0], R_SHORT, across)

    def ended(slab):
        way = RIGHT if slab in A else LEFT
        total = here(0, slab) + arrived(1 - way, 3, slab)[...].astype(F32)
        return total + arrived(way, 4, slab)[...].astype(F32)

    def block_terms(gate, up, back):
        sig = 1.0 / (1.0 + jnp.exp(-gate))
        act = gate * sig
        return act * up, back * up * sig * (1.0 + gate * (1.0 - sig)), back * act

    terms = block_terms(ended(0), ended(1), ended(2))

    def gather(src, block, half, way, step, g, i):
        send(
            src, full.at[block, half, i],
            R_A + ((way * 4 + step - 1) * 2 + g) * 3 + i, to_dev[way],
        )

    halves = (xh, 1 - xh)

    def start_gather(g):
        for i in range(3):
            for way in (RIGHT, LEFT):
                gather(own.at[halves[g], i], slot, halves[g], way, 1, g, i)
        send(own.at[halves[g]], full.at[slot, halves[g]], R_AC + 2 * z + g, other)

    for i in range(3):
        own[xh, i] = terms[i].astype(BF)
    send(own.at[xh], own.at[xh], R_OWN, across)
    start_gather(0)
    long_v = arrived(LEFT, 4, 3)
    send(long_v, swap_d.at[1], R_LONG, across)

    def step_of_gather(step, g):
        blocks = [2 * at(-step) + c, 2 * at(step) + c]
        half = halves[g]
        whole_way = [(0, 1), (2,)] if g == 0 else [(2,), (0, 1)]
        for i in range(3):
            for way in (RIGHT, LEFT):
                if step == 4 and i not in whole_way[way]:
                    continue
                piece = full.at[blocks[way], half, i]
                got(piece, R_A + ((way * 4 + step - 1) * 2 + g) * 3 + i)
                if step < 3 or (step == 3 and i in whole_way[way]):
                    gather(piece, blocks[way], half, way, step + 1, g, i)
        for way, zz in ((RIGHT, at(-step)), (LEFT, at(step))):
            if step < 4 or way == RIGHT:
                send(full.at[blocks[way], half], full.at[blocks[way], half], R_AC + 2 * zz + g, other)

    step_of_gather(1, 0)
    got(own.at[1 - xh], R_OWN)
    start_gather(1)
    outs = [pltpu.make_async_copy(own, full.at[slot], hsem.at[0])]
    outs[0].start()

    got(gram_all.at[1 - c], R_GC)
    kt = jnp.concatenate([gram_all[0].reshape(128, 128), gram_all[1].reshape(128, 128)], axis=1)
    rk = (kt * r_row).astype(BF)
    hb, dgb, dub = [jnp.concatenate([own[0, i], own[1, i]], axis=1) for i in range(3)]
    got(swap_p, R_P)
    got(swap_d.at[0], R_SHORT)
    got(swap_d.at[1], R_LONG)
    mine = vpart[z] + short_v[...].astype(F32) + long_v[...].astype(F32)
    val = mine + (swap_p[...] + swap_d[0].astype(F32) + swap_d[1].astype(F32))
    v_gate = val - LEARN_RATE * nt(dgb, rk)
    v_up = pltpu.roll(val, 124, 1) - LEARN_RATE * nt(dub, rk)
    v_back = pltpu.roll(val - LEARN_RATE * nt(hb, rk), 120, 1)
    lane = lax.broadcasted_iota(jnp.int32, (32, 128), 1)
    row = lax.broadcasted_iota(jnp.int32, (32, 128), 0)
    pick = jnp.logical_and(lane % 16 < 4, (lane // 16) * 4 + lane % 16 == row)
    mask_f = jnp.broadcast_to(mask[...].astype(F32), (16, 32)).astype(BF)
    mask_l = lax.dot_general(
        mask_f, jnp.where(pick, 1.0, 0.0).astype(BF), (((1,), (0,)), ((), ())), preferred_element_type=F32
    )[0:1]
    keep = jnp.broadcast_to(mask_l, (HB, 128)) > 0.5
    v_hid, v_dg, v_du = [jnp.where(keep, t, 0.0) for t in block_terms(v_gate, v_up, v_back)]
    inner = tn(v_dg.astype(BF), dgb) + tn(v_du.astype(BF), dub) + tn(pltpu.roll(v_hid, 8, 1).astype(BF), hb)
    token = jnp.sum(inner * kt, axis=0, keepdims=True)
    label = lax.broadcasted_iota(jnp.int32, (EX, TOK), 0)
    score = jnp.sum(jnp.where(ids[...] == label, token, 0.0), axis=1, keepdims=True)
    sc1[z] = jnp.broadcast_to(score, (EX, 128))
    for k in range(1, NZ):
        send(sc1.at[z], sc1.at[z], R_S1 + z, zdev(k))

    step_of_gather(2, 0)
    step_of_gather(1, 1)
    step_of_gather(3, 0)
    step_of_gather(2, 1)
    for k in range(1, NZ):
        got(sc1.at[at(k)], R_S1 + at(k))
    sc2[c] = jnp.sum(sc1[...], axis=0)
    send(sc2.at[c], sc2.at[c], R_S2, other)
    step_of_gather(4, 0)
    got(sc2.at[1 - c], R_S2)
    sc3[m] = sc2[0] + sc2[1]
    for k in range(1, NM):
        send(sc3.at[m], sc3.at[m], R_S3 + m, mdev(k))
    step_of_gather(3, 1)
    for k in range(1, NM):
        j = (m + k) % NM
        got(sc3.at[j], R_S3 + j)
    score = jnp.sum(sc3[...], axis=0)
    rms = jnp.sqrt(jnp.mean(score * score, axis=0, keepdims=True) + 1e-6)
    arg = score / (4.0 * rms)
    soft = jnp.maximum(arg, 0.0) + jnp.log(1.0 + jnp.exp(-jnp.abs(arg)))
    weights = EX * soft / jnp.sum(soft, axis=0, keepdims=True)
    diag = lax.broadcasted_iota(jnp.int32, (EX, 128), 0) == lax.broadcasted_iota(jnp.int32, (EX, 128), 1)
    wts_out[...] = jnp.sum(jnp.where(diag, weights, 0.0), axis=0, keepdims=True)[:, :EX]
    e_row = jnp.zeros((1, TOK), F32)
    for e in range(EX):
        e_row = e_row + jnp.where(ids[...] == e, weights[e : e + 1, 0:1], 0.0)
    for i in range(2):
        xs[i] = (xt[i] * e_row).astype(BF)
    copy = pltpu.make_async_copy(xs, xs_out, hsem.at[1])
    copy.start()
    outs.append(copy)

    step_of_gather(4, 1)
    for g in range(2):
        for k in range(NZ):
            got(full.at[2 * at(k) + 1 - c, halves[g]], R_AC + 2 * at(k) + g)
    for copy in sends:
        copy.wait_send()
    for copy in outs:
        copy.wait()


def grad_kernel(full, xs, wts, gg, gu, gd, out):
    def rows(i):
        return jnp.concatenate(
            [full[:, 0, i].reshape(8 * HB, 128), full[:, 1, i].reshape(8 * HB, 128)], axis=1
        )

    out[...] = wts[...]
    gd[...] = nt(rows(0), xs[1]).astype(BF)
    gg[...] = nt(xs[0], rows(1)).astype(BF)
    gu[...] = nt(xs[0], rows(2)).astype(BF)


def body(train_x, train_cot, val_x, val_cot, w_gate, w_up, w_down, step_weights, example_ids, val_mask):
    hbm = pl.BlockSpec(memory_space=pltpu.HBM)
    free = pl.BlockSpec(memory_space=pl.ANY)
    vmem = pl.BlockSpec(memory_space=pltpu.VMEM)
    V = pltpu.VMEM
    full, xs, wts = pl.pallas_call(
        comm_kernel,
        out_shape=(
            jax.ShapeDtypeStruct((16, 2, 3, HB, 128), BF),
            jax.ShapeDtypeStruct((2, W, TOK), BF),
            jax.ShapeDtypeStruct((1, EX), F32),
        ),
        in_specs=[hbm] * 10,
        out_specs=(free, free, vmem),
        scratch_shapes=[
            pltpu.SMEM((EX,), F32),
            V((1, TOK), jnp.int32),
            V((1, 32), jnp.int32),
            V((2, 4, W), BF),
            V((2, W, 1792), BF),
            V((2, NZ, 3, HB, W), BF),
            V((NZ, 3, HB, W), BF),
            V((80, W), BF),
            V((16, W), F32),
            V((NM, 80, W), BF),
            V((NM, 80, W), BF),
            V((3, 128, W), BF),
            V((3, 128, W), BF),
            V((NZ, 2, 3, HB, 128), F32),
            V((NZ, HB, 128), F32),
            V((2, 3, HB, 128), BF),
            V((NZ, 3, HB, 128), BF),
            V((NZ, 3, HB, 128), BF),
            V((2, 4, 4, HB, 128), BF),
            V((2, 4, 4, HB, 128), BF),
            V((2, 3, HB, 128), F32),
            V((2, 3, HB, 128), F32),
            V((HB, 128), F32),
            V((2, HB, 128), BF),
            V((NZ, 16, 128), F32),
            V((NZ, 16, 128), F32),
            V((2, 16, 128), F32),
            V((2, NZ, 16, 128), F32),
            V((NZ, EX, 128), F32),
            V((2, EX, 128), F32),
            V((NM, EX, 128), F32),
            V((2, W, TOK), F32),
            V((2, W, TOK), BF),
            pltpu.SemaphoreType.DMA((11,)),
            pltpu.SemaphoreType.DMA((200,)),
            pltpu.SemaphoreType.DMA((195,)),
            pltpu.SemaphoreType.DMA((2,)),
        ],
        compiler_params=pltpu.CompilerParams(
            collective_id=0, has_side_effects=True, vmem_limit_bytes=40 * 1024 * 1024
        ),
        name="reduce_and_gather",
    )(
        *[
            pltpu.with_memory_space_constraint(a, pltpu.HBM)
            for a in (
                train_x, train_cot, val_x, val_cot, w_gate, w_up, w_down.reshape(NZ, 2, HB, W),
                step_weights, example_ids.reshape(1, TOK), val_mask.reshape(1, 32),
            )
        ]
    )
    gg, gu, gd, out = pl.pallas_call(
        grad_kernel,
        grid=(2,),
        out_shape=(
            jax.ShapeDtypeStruct((W, 1792), BF),
            jax.ShapeDtypeStruct((W, 1792), BF),
            jax.ShapeDtypeStruct((1792, W), BF),
            jax.ShapeDtypeStruct((1, EX), F32),
        ),
        in_specs=[
            pl.BlockSpec((8, 2, 3, HB, 128), lambda i: (i, 0, 0, 0, 0)),
            pl.BlockSpec((2, W, TOK), lambda i: (0, 0, 0)),
            pl.BlockSpec((1, EX), lambda i: (0, 0)),
        ],
        out_specs=(
            pl.BlockSpec((W, 8 * HB), lambda i: (0, i)),
            pl.BlockSpec((W, 8 * HB), lambda i: (0, i)),
            pl.BlockSpec((8 * HB, W), lambda i: (i, 0)),
            pl.BlockSpec((1, EX), lambda i: (0, 0)),
        ),
        compiler_params=pltpu.CompilerParams(vmem_limit_bytes=40 * 1024 * 1024),
        name="gradients",
    )(full, xs, wts)
    return gg, gu, gd, out.reshape(EX)


def solution(mesh):
    wide, tall = P("dp", "mp"), P("mp", "dp")
    return jax.shard_map(
        body,
        mesh=mesh,
        in_specs=(tall, tall, tall, tall, wide, wide, tall, P(), P(), P()),
        out_specs=(wide, wide, tall, P()),
        check_vma=False,
    )
```

```python
import jax
import jax.numpy as jnp
from jax import lax
from jax.experimental import pallas as pl
from jax.experimental.pallas import tpu as pltpu
from jax.sharding import PartitionSpec as P

MESH = pl.DeviceIdType.MESH
BF = jnp.bfloat16
F32 = jnp.float32

LEARN_RATE = 0.0003
NZ = 8
NM = 8
HB = 112
TOK = 256
W = 256
EX = 8


def nt(left, right):
    return lax.dot_general(left, right, (((1,), (1,)), ((), ())), preferred_element_type=F32)


def tn(left, right):
    return lax.dot_general(left, right, (((0,), (0,)), ((), ())), preferred_element_type=F32)


def comm_kernel(
    x_in, c_in, vx_in, vc_in, wg_in, wu_in, wd_in, sw_in, ids_in, mask_in,
    full, xs_out, wts_out,
    sw, ids, mask, vraw, wraw, wt, wo, pk, vstage, xb, xo, va, vo, part, own,
    ring_s, ring_d, swap_p, swap_d, gram_s, gram_d, gram_x, gram_all, sc1, sc2, sc3, xt, xs,
    lsem, ssem, rsem, hsem,
):
    d = lax.axis_index("dp")
    m = lax.axis_index("mp")
    z = d // 4
    xh = (d // 2) % 2
    c = d % 2
    slot = z * 2 + c

    def dev(zz, xx, cc):
        return (zz * 4 + xx * 2 + cc, m)

    def at(step):
        return (z + step + NZ) % NZ

    def zdev(step):
        return dev(at(step), xh, c)

    def mdev(step):
        return (d, (m + step) % NM)

    other = dev(z, xh, 1 - c)
    across = dev(z, 1 - xh, c)
    right, left = zdev(1), zdev(-1)

    sends = []
    ended = [0]

    def drain(to):
        for copy in sends[ended[0] : to]:
            copy.wait_send()
        ended[0] = to

    def send(src, dst, rs, to):
        copy = pltpu.make_async_remote_copy(
            src_ref=src, dst_ref=dst, send_sem=ssem.at[len(sends)], recv_sem=rsem.at[rs],
            device_id=to, device_id_type=MESH,
        )
        copy.start()
        sends.append(copy)

    def got(dst, rs):
        pltpu.make_async_copy(dst, dst, rsem.at[rs]).wait()

    R_X, R_XO, R_W, R_RING = 0, 8, 16, 24
    R_P, R_SHORT, R_LONG = 80, 81, 88
    R_GS, R_GX, R_GA, R_GC = 96, 104, 105, 113
    R_A, R_AC, R_S1, R_S2, R_S3 = 114, 162, 171, 179, 180

    loads = [
        pltpu.make_async_copy(x_in, pk.at[0:32], lsem.at[0]),
        pltpu.make_async_copy(c_in, pk.at[32:64], lsem.at[1]),
        pltpu.make_async_copy(wg_in, wraw.at[0], lsem.at[2]),
        pltpu.make_async_copy(wu_in, wraw.at[1], lsem.at[3]),
        pltpu.make_async_copy(vx_in, vraw.at[0], lsem.at[4]),
        pltpu.make_async_copy(vc_in, vraw.at[1], lsem.at[5]),
        pltpu.make_async_copy(wd_in.at[:, 0], wt.at[0, :, 2], lsem.at[6]),
        pltpu.make_async_copy(wd_in.at[:, 1], wt.at[1, :, 2], lsem.at[7]),
        pltpu.make_async_copy(sw_in, sw, lsem.at[8]),
        pltpu.make_async_copy(ids_in, ids, lsem.at[9]),
        pltpu.make_async_copy(mask_in, mask, lsem.at[10]),
    ]
    for copy in loads:
        copy.start()

    barrier = pltpu.get_barrier_semaphore()
    peers = [mdev(k) for k in range(1, NM)] + [across, other] + [zdev(k) for k in range(1, NZ)]
    for peer in peers:
        pl.semaphore_signal(barrier, inc=1, device_id=peer, device_id_type=MESH)

    vstage[0:16] = jnp.zeros((16, W), F32)
    loads[4].wait()
    loads[5].wait()
    vstage[0:4] = vraw[0].astype(F32)
    vstage[4:8] = vraw[0].astype(F32)
    vstage[8:12] = vraw[1].astype(F32)
    pk[64:80] = vstage[0:16].astype(BF)
    loads[0].wait()
    loads[1].wait()
    xb[m] = pk[...]
    pl.semaphore_wait(barrier, len(peers))

    for k in range(1, NM):
        send(pk, xb.at[m], R_X + m, mdev(k))
    send(pk, xo.at[m], R_XO + m, other)

    for w in range(2):
        loads[2 + w].wait()
        for i in range(14):
            block = wraw[w, :, 128 * i : 128 * (i + 1)].T
            row = 128 * i
            while row < 128 * (i + 1):
                b = row // HB
                end = min(128 * (i + 1), (b + 1) * HB)
                wt[b % 2, b // 2, w, row - b * HB : end - b * HB] = block[row - 128 * i : end - 128 * i]
                row = end
    loads[6].wait()
    loads[7].wait()
    for step in (4, 3, 5, 2, 6, 1, 7, 0):
        send(wt.at[1 - c, at(step)], wo.at[at(step)], R_W + at(step), other)

    for k in range(1, NM):
        j = (m + NM - k) % NM
        got(xb.at[j], R_X + j)
        send(xb.at[j], xo.at[j], R_XO + j, other)
    place = lax.broadcasted_iota(jnp.int32, (128, W), 0) % 16

    def spread(src, dst):
        rows = src[:, 64:80, :].reshape(128, W).astype(F32)
        for i in range(3):
            keep = jnp.logical_and(place >= 4 * i, place < 4 * i + 4)
            dst[i] = jnp.where(keep, rows, 0.0).astype(BF)

    def tokens(ref, first):
        return ref[:, 32 * first : 32 * first + 32, :].reshape(TOK, W)

    spread(xb, va)
    val = jnp.zeros((NZ * HB, 128), F32)
    for i in range(3):
        lhs = wt[c, :, i].reshape(NZ * HB, W)
        total = nt(lhs, tokens(xb, 1 if i == 2 else 0))
        part[:, i] = total[:, :128].reshape(NZ, HB, 128)
        part[:, 4 + i] = total[:, 128:].reshape(NZ, HB, 128)
        val = val + nt(lhs, va[i])
    part[:, 3] = val.reshape(NZ, HB, 128)
    for k in range(NM):
        j = (m + NM - k) % NM
        got(xo.at[j], R_XO + j)

    A, B = (0, 1, 2, 3), (4, 5, 6)
    RIGHT, LEFT = 0, 1
    to_dev = (right, left)

    def first(way, slab, value):
        ring_s[way, 0, slab] = value.astype(BF)
        send(ring_s.at[way, 0, slab], ring_d.at[way, 0, slab], R_RING + way * 28 + slab, to_dev[way])

    def arrived(way, s, slab):
        got(ring_d.at[way, s - 1, slab], R_RING + (way * 4 + s - 1) * 7 + slab)

    def onward(way, s, slab, step):
        arrived(way, s, slab)
        value = part[at(step), slab] + ring_d[way, s - 1, slab].astype(F32)
        ring_s[way, s, slab] = value.astype(BF)
        send(
            ring_s.at[way, s, slab], ring_d.at[way, s, slab],
            R_RING + (way * 4 + s) * 7 + slab, to_dev[way],
        )

    far = at(4)
    got(wo.at[far], R_W + far)
    for i in range(3):
        total = nt(wo[far, i], tokens(xo, 1 if i == 2 else 0))
        first(RIGHT, i, part[far, i] + total[:, :128])
        first(LEFT, 4 + i, part[far, 4 + i] + total[:, 128:])
    spread(xo, vo)
    val = part[far, 3]
    for i in range(3):
        val = val + nt(wo[far, i], vo[i])
    first(RIGHT, 3, val)

    for k in range(1, NZ):
        got(wo.at[at(4 + k)], R_W + at(4 + k))
    val = jnp.zeros((NZ * HB, 128), F32)
    for i in range(3):
        lhs = wo[:, i].reshape(NZ * HB, W)
        total = nt(lhs, tokens(xo, 1 if i == 2 else 0))
        part[:, i] = part[:, i] + total[:, :128].reshape(NZ, HB, 128)
        part[:, 4 + i] = part[:, 4 + i] + total[:, 128:].reshape(NZ, HB, 128)
        first(LEFT, i, part[at(-3), i])
        first(RIGHT, 4 + i, part[at(3), 4 + i])
        val = val + nt(lhs, vo[i])
    part[:, 3] = part[:, 3] + val.reshape(NZ, HB, 128)
    first(LEFT, 3, part[at(-3), 3])
    send(part.at[z], swap_p, R_P, across)

    def both_long(s):
        for i in range(4):
            onward(RIGHT, s, A[i], 4 - s)
            if i < 3:
                onward(LEFT, s, B[i], s - 4)

    def both_short(s):
        for i in range(4):
            if i < 3:
                onward(RIGHT, s, B[i], 3 - s)
            onward(LEFT, s, A[i], s - 3)

    def half(ref, which):
        return ref[pl.ds(4 * c, 4), 32 * which : 32 * which + 32, :].reshape(128, W)

    gram = nt(va[0], half(xb, 0)) + nt(vo[0], half(xo, 0)) + nt(va[2], half(xb, 1)) + nt(vo[2], half(xo, 1))
    gram_s[...] = gram.reshape(NZ, 16, 128)
    gram_d[z] = gram_s[z]
    for k in range(1, NZ):
        send(gram_s.at[at(k)], gram_d.at[z], R_GS + z, zdev(k))

    drain(len(sends) - 40)
    both_long(1)
    both_short(1)
    for copy in loads[8:]:
        copy.wait()
    for k in range(1, NZ):
        got(gram_d.at[at(k)], R_GS + at(k))
    gram_x[0] = jnp.sum(gram_d[...], axis=0)
    send(gram_x.at[0], gram_x.at[1], R_GX, across)
    both_long(2)
    both_short(2)
    got(gram_x.at[1], R_GX)
    gram_all[c, z] = gram_x[0] + gram_x[1]
    for k in range(1, NZ):
        send(gram_all.at[c, z], gram_all.at[c, z], R_GA + z, zdev(k))
    both_long(3)
    older = len(sends) - 7

    def pass_on(way, s, slab, dst, rs):
        arrived(way, s, slab)
        send(ring_d.at[way, s - 1, slab], swap_d.at[dst, slab], rs + slab, across)

    for i in range(4):
        if i < 3:
            pass_on(RIGHT, 3, B[i], 0, R_SHORT)
        pass_on(LEFT, 3, A[i], 0, R_SHORT)
    r_row = jnp.zeros((1, TOK), F32)
    for e in range(EX):
        r_row = r_row + jnp.where(ids[...] == e, sw[e], 0.0)
    for i in range(2):
        xt[i] = tokens(xb, i).T.astype(F32)
    for k in range(1, NZ):
        got(gram_all.at[c, at(k)], R_GA + at(k))
    send(gram_all.at[c], gram_all.at[c], R_GC, other)
    got(swap_p, R_P)
    for i in range(4):
        pass_on(RIGHT, 4, A[i], 1, R_LONG)
        if i < 3:
            pass_on(LEFT, 4, B[i], 1, R_LONG)

    def whole(slab):
        way = RIGHT if slab < 4 else LEFT
        mine_ = part[z, slab] + ring_d[1 - way, 2, slab].astype(F32) + ring_d[way, 3, slab].astype(F32)
        got(swap_d.at[0, slab], R_SHORT + slab)
        got(swap_d.at[1, slab], R_LONG + slab)
        theirs = swap_p[slab] + swap_d[0, slab].astype(F32) + swap_d[1, slab].astype(F32)
        return mine_ + theirs

    def block_terms(gate, up, back):
        sig = 1.0 / (1.0 + jnp.exp(-gate))
        act = gate * sig
        return act * up, back * up * sig * (1.0 + gate * (1.0 - sig)), back * act

    def gather(src, block, way, step, slab):
        send(
            src, full.at[block, slab], R_A + (way * 4 + step - 1) * 6 + slab, to_dev[way]
        )

    for h in range(2):
        terms = block_terms(*[whole(4 * h + i) for i in range(3)])
        for i in range(3):
            own[3 * h + i] = terms[i].astype(BF)
            gather(own.at[3 * h + i], slot, RIGHT, 1, 3 * h + i)
            gather(own.at[3 * h + i], slot, LEFT, 1, 3 * h + i)
    send(own, full.at[slot], R_AC + z, other)
    outs = [pltpu.make_async_copy(own, full.at[slot], hsem.at[0])]
    outs[0].start()

    def step_of_gather(step):
        blocks = [2 * at(-step) + c, 2 * at(step) + c]
        for i in range(6):
            for way in (RIGHT, LEFT):
                if step == 4 and i // 3 != way:
                    continue
                got(full.at[blocks[way], i], R_A + (way * 4 + step - 1) * 6 + i)
                if step < 3 or (step == 3 and i // 3 == way):
                    gather(full.at[blocks[way], i], blocks[way], way, step + 1, i)
        if step < 4:
            for way, zz in ((RIGHT, at(-step)), (LEFT, at(step))):
                send(full.at[blocks[way]], full.at[blocks[way]], R_AC + zz, other)
        else:
            send(full.at[blocks[0]], full.at[blocks[0]], R_AC + at(4), other)

    got(gram_all.at[1 - c], R_GC)
    kt = jnp.concatenate([gram_all[0].reshape(128, 128), gram_all[1].reshape(128, 128)], axis=1)
    rk = (kt * r_row).astype(BF)
    hb, dgb, dub = [jnp.concatenate([own[i], own[3 + i]], axis=1) for i in range(3)]
    val = whole(3)
    v_gate = val - LEARN_RATE * nt(dgb, rk)
    v_up = pltpu.roll(val, 124, 1) - LEARN_RATE * nt(dub, rk)
    v_back = pltpu.roll(val - LEARN_RATE * nt(hb, rk), 120, 1)
    lane = lax.broadcasted_iota(jnp.int32, (32, 128), 1)
    row = lax.broadcasted_iota(jnp.int32, (32, 128), 0)
    pick = jnp.logical_and(lane % 16 < 4, (lane // 16) * 4 + lane % 16 == row)
    mask_f = jnp.broadcast_to(mask[...].astype(F32), (16, 32)).astype(BF)
    mask_l = lax.dot_general(
        mask_f, jnp.where(pick, 1.0, 0.0).astype(BF), (((1,), (0,)), ((), ())), preferred_element_type=F32
    )[0:1]
    keep = jnp.broadcast_to(mask_l, (HB, 128)) > 0.5
    v_hid, v_dg, v_du = [jnp.where(keep, t, 0.0) for t in block_terms(v_gate, v_up, v_back)]
    inner = tn(v_dg.astype(BF), dgb) + tn(v_du.astype(BF), dub) + tn(pltpu.roll(v_hid, 8, 1).astype(BF), hb)
    token = jnp.sum(inner * kt, axis=0, keepdims=True)
    label = lax.broadcasted_iota(jnp.int32, (EX, TOK), 0)
    score = jnp.sum(jnp.where(ids[...] == label, token, 0.0), axis=1, keepdims=True)
    sc1[z] = jnp.broadcast_to(score, (EX, 128))
    for k in range(1, NZ):
        send(sc1.at[z], sc1.at[z], R_S1 + z, zdev(k))

    step_of_gather(1)
    drain(older)
    step_of_gather(2)
    for k in range(1, NZ):
        got(sc1.at[at(k)], R_S1 + at(k))
    sc2[c] = jnp.sum(sc1[...], axis=0)
    send(sc2.at[c], sc2.at[c], R_S2, other)
    got(sc2.at[1 - c], R_S2)
    sc3[m] = sc2[0] + sc2[1]
    for k in range(1, NM):
        send(sc3.at[m], sc3.at[m], R_S3 + m, mdev(k))
    older = len(sends) - 45

    step_of_gather(3)
    drain(older)
    for k in range(1, NM):
        j = (m + k) % NM
        got(sc3.at[j], R_S3 + j)
    score = jnp.sum(sc3[...], axis=0)
    rms = jnp.sqrt(jnp.mean(score * score, axis=0, keepdims=True) + 1e-6)
    arg = score / (4.0 * rms)
    soft = jnp.maximum(arg, 0.0) + jnp.log(1.0 + jnp.exp(-jnp.abs(arg)))
    weights = EX * soft / jnp.sum(soft, axis=0, keepdims=True)
    diag = lax.broadcasted_iota(jnp.int32, (EX, 128), 0) == lax.broadcasted_iota(jnp.int32, (EX, 128), 1)
    wts_out[...] = jnp.sum(jnp.where(diag, weights, 0.0), axis=0, keepdims=True)[:, :EX]
    e_row = jnp.zeros((1, TOK), F32)
    for e in range(EX):
        e_row = e_row + jnp.where(ids[...] == e, weights[e : e + 1, 0:1], 0.0)
    for i in range(2):
        xs[i] = (xt[i] * e_row).astype(BF)
    copy = pltpu.make_async_copy(xs, xs_out, hsem.at[1])
    copy.start()
    outs.append(copy)

    step_of_gather(4)
    for k in range(NZ):
        got(full.at[2 * at(k) + 1 - c], R_AC + at(k))
    drain(len(sends))
    for copy in outs:
        copy.wait()


def grad_kernel(full, xs, wts, gg, gu, gd, out):
    def rows(i):
        return jnp.concatenate(
            [full[:, i].reshape(8 * HB, 128), full[:, 3 + i].reshape(8 * HB, 128)], axis=1
        )

    out[...] = wts[...]
    gd[...] = nt(rows(0), xs[1]).astype(BF)
    gg[...] = nt(xs[0], rows(1)).astype(BF)
    gu[...] = nt(xs[0], rows(2)).astype(BF)


def body(train_x, train_cot, val_x, val_cot, w_gate, w_up, w_down, step_weights, example_ids, val_mask):
    hbm = pl.BlockSpec(memory_space=pltpu.HBM)
    free = pl.BlockSpec(memory_space=pl.ANY)
    vmem = pl.BlockSpec(memory_space=pltpu.VMEM)
    V = pltpu.VMEM
    full, xs, wts = pl.pallas_call(
        comm_kernel,
        out_shape=(
            jax.ShapeDtypeStruct((16, 6, HB, 128), BF),
            jax.ShapeDtypeStruct((2, W, TOK), BF),
            jax.ShapeDtypeStruct((1, EX), F32),
        ),
        in_specs=[hbm] * 10,
        out_specs=(free, free, vmem),
        scratch_shapes=[
            pltpu.SMEM((EX,), F32),
            V((1, TOK), jnp.int32),
            V((1, 32), jnp.int32),
            V((2, 4, W), BF),
            V((2, W, 1792), BF),
            V((2, NZ, 3, HB, W), BF),
            V((NZ, 3, HB, W), BF),
            V((80, W), BF),
            V((16, W), F32),
            V((NM, 80, W), BF),
            V((NM, 80, W), BF),
            V((3, 128, W), BF),
            V((3, 128, W), BF),
            V((NZ, 7, HB, 128), F32),
            V((6, HB, 128), BF),
            V((2, 4, 7, HB, 128), BF),
            V((2, 4, 7, HB, 128), BF),
            V((7, HB, 128), F32),
            V((2, 7, HB, 128), BF),
            V((NZ, 16, 128), F32),
            V((NZ, 16, 128), F32),
            V((2, 16, 128), F32),
            V((2, NZ, 16, 128), F32),
            V((NZ, EX, 128), F32),
            V((2, EX, 128), F32),
            V((NM, EX, 128), F32),
            V((2, W, TOK), F32),
            V((2, W, TOK), BF),
            pltpu.SemaphoreType.DMA((11,)),
            pltpu.SemaphoreType.DMA((200,)),
            pltpu.SemaphoreType.DMA((195,)),
            pltpu.SemaphoreType.DMA((2,)),
        ],
        compiler_params=pltpu.CompilerParams(
            collective_id=0, has_side_effects=True, vmem_limit_bytes=40 * 1024 * 1024
        ),
        name="reduce_and_gather",
    )(
        *[
            pltpu.with_memory_space_constraint(a, pltpu.HBM)
            for a in (
                train_x, train_cot, val_x, val_cot, w_gate, w_up, w_down.reshape(NZ, 2, HB, W),
                step_weights, example_ids.reshape(1, TOK), val_mask.reshape(1, 32),
            )
        ]
    )
    gg, gu, gd, out = pl.pallas_call(
        grad_kernel,
        grid=(2,),
        out_shape=(
            jax.ShapeDtypeStruct((W, 1792), BF),
            jax.ShapeDtypeStruct((W, 1792), BF),
            jax.ShapeDtypeStruct((1792, W), BF),
            jax.ShapeDtypeStruct((1, EX), F32),
        ),
        in_specs=[
            pl.BlockSpec((8, 6, HB, 128), lambda i: (i, 0, 0, 0)),
            pl.BlockSpec((2, W, TOK), lambda i: (0, 0, 0)),
            pl.BlockSpec((1, EX), lambda i: (0, 0)),
        ],
        out_specs=(
            pl.BlockSpec((W, 8 * HB), lambda i: (0, i)),
            pl.BlockSpec((W, 8 * HB), lambda i: (0, i)),
            pl.BlockSpec((8 * HB, W), lambda i: (i, 0)),
            pl.BlockSpec((1, EX), lambda i: (0, 0)),
        ),
        compiler_params=pltpu.CompilerParams(vmem_limit_bytes=40 * 1024 * 1024),
        name="gradients",
    )(full, xs, wts)
    return gg, gu, gd, out.reshape(EX)


def solution(mesh):
    wide, tall = P("dp", "mp"), P("mp", "dp")
    return jax.shard_map(
        body,
        mesh=mesh,
        in_specs=(tall, tall, tall, tall, wide, wide, tall, P(), P(), P()),
        out_specs=(wide, wide, tall, P()),
        check_vma=False,
    )
```

```python
import jax
import jax.numpy as jnp
from jax import lax
from jax.experimental import pallas as pl
from jax.experimental.pallas import tpu as pltpu
from jax.sharding import PartitionSpec as P

MESH = pl.DeviceIdType.MESH
BF = jnp.bfloat16
F32 = jnp.float32

LEARN_RATE = 0.0003
NZ = 8
NM = 8
HB = 112
TOK = 256
W = 256
EX = 8


def nt(left, right):
    return lax.dot_general(left, right, (((1,), (1,)), ((), ())), preferred_element_type=F32)


def tn(left, right):
    return lax.dot_general(left, right, (((0,), (0,)), ((), ())), preferred_element_type=F32)


def comm_kernel(
    x_in, c_in, vx_in, vc_in, wg_in, wu_in, wd_in, sw_in, ids_in, mask_in,
    full, xs_out, wts_out,
    sw, ids, mask, vraw, wraw, wt, wo, pk, vstage, xb, xo, va, vo, part, own,
    ring_s, ring_d, swap_p, swap_d, gram_s, gram_d, gram_x, gram_all, sc1, sc2, sc3, xt, xs,
    lsem, ssem, rsem, hsem,
):
    d = lax.axis_index("dp")
    m = lax.axis_index("mp")
    z = d // 4
    xh = (d // 2) % 2
    c = d % 2
    slot = z * 2 + c

    def dev(zz, xx, cc):
        return (zz * 4 + xx * 2 + cc, m)

    def at(step):
        return (z + step + NZ) % NZ

    def zdev(step):
        return dev(at(step), xh, c)

    def mdev(step):
        return (d, (m + step) % NM)

    other = dev(z, xh, 1 - c)
    across = dev(z, 1 - xh, c)
    right, left = zdev(1), zdev(-1)

    def send(src, dst, ss, rs, to):
        pltpu.make_async_remote_copy(
            src_ref=src, dst_ref=dst, send_sem=ssem.at[ss], recv_sem=rsem.at[rs],
            device_id=to, device_id_type=MESH,
        ).start()

    def got(dst, rs):
        pltpu.make_async_copy(dst, dst, rsem.at[rs]).wait()

    R_X, R_XO, R_W, R_P, R_GS, R_GX, R_GA, R_GC, R_AC, R_S1, R_S2, R_S3 = 0, 8, 9, 11, 12, 13, 14, 15, 16, 17, 18, 19
    R_SHORT, R_LONG, R_RING, R_A = 20, 27, 34, 83

    (S_X, S_W, S_XO, S_RING, S_LAST, S_P, S_SHORT, S_LONG, S_GS, S_GX, S_GA, S_GC, S_A, S_AC, S_S1, S_S2, S_S3) = range(17)

    loads = [
        pltpu.make_async_copy(x_in, pk.at[0:32], lsem.at[0]),
        pltpu.make_async_copy(c_in, pk.at[32:64], lsem.at[1]),
        pltpu.make_async_copy(wg_in, wraw.at[0], lsem.at[2]),
        pltpu.make_async_copy(wu_in, wraw.at[1], lsem.at[3]),
        pltpu.make_async_copy(vx_in, vraw.at[0], lsem.at[4]),
        pltpu.make_async_copy(vc_in, vraw.at[1], lsem.at[5]),
        pltpu.make_async_copy(wd_in.at[:, 0], wt.at[0, :, 2], lsem.at[6]),
        pltpu.make_async_copy(wd_in.at[:, 1], wt.at[1, :, 2], lsem.at[7]),
        pltpu.make_async_copy(sw_in, sw, lsem.at[8]),
        pltpu.make_async_copy(ids_in, ids, lsem.at[9]),
        pltpu.make_async_copy(mask_in, mask, lsem.at[10]),
    ]
    for copy in loads:
        copy.start()

    barrier = pltpu.get_barrier_semaphore()
    peers = [mdev(k) for k in range(1, NM)] + [across, other] + [zdev(k) for k in range(1, NZ)]
    for peer in peers:
        pl.semaphore_signal(barrier, inc=1, device_id=peer, device_id_type=MESH)

    vstage[0:16] = jnp.zeros((16, W), F32)
    loads[4].wait()
    loads[5].wait()
    vstage[0:4] = vraw[0].astype(F32)
    vstage[4:8] = vraw[0].astype(F32)
    vstage[8:12] = vraw[1].astype(F32)
    pk[64:80] = vstage[0:16].astype(BF)
    loads[0].wait()
    loads[1].wait()
    xb[m] = pk[...]
    pl.semaphore_wait(barrier, len(peers))

    for k in range(1, NM):
        send(pk, xb.at[m], S_X, R_X + m, mdev(k))
    send(pk, xo.at[m], S_X, R_XO, other)

    for w in range(2):
        loads[2 + w].wait()
        for i in range(14):
            block = wraw[w, :, 128 * i : 128 * (i + 1)].T
            row = 128 * i
            while row < 128 * (i + 1):
                b = row // HB
                end = min(128 * (i + 1), (b + 1) * HB)
                wt[b % 2, b // 2, w, row - b * HB : end - b * HB] = block[row - 128 * i : end - 128 * i]
                row = end
    loads[6].wait()
    loads[7].wait()
    for step in (4, 3, 5, 2, 6, 1, 7, 0):
        send(wt.at[1 - c, at(step)], wo.at[at(step)], S_W, R_W if step == 4 else R_W + 1, other)

    for k in range(1, NM):
        j = (m + NM - k) % NM
        got(xb.at[j], R_X + j)
        send(xb.at[j], xo.at[j], S_XO, R_XO, other)
    place = lax.broadcasted_iota(jnp.int32, (128, W), 0) % 16

    def spread(src, dst):
        rows = src[:, 64:80, :].reshape(128, W).astype(F32)
        for i in range(3):
            keep = jnp.logical_and(place >= 4 * i, place < 4 * i + 4)
            dst[i] = jnp.where(keep, rows, 0.0).astype(BF)

    def tokens(ref, first):
        return ref[:, 32 * first : 32 * first + 32, :].reshape(TOK, W)

    spread(xb, va)
    val = jnp.zeros((NZ * HB, 128), F32)
    for i in range(3):
        lhs = wt[c, :, i].reshape(NZ * HB, W)
        total = nt(lhs, tokens(xb, 1 if i == 2 else 0))
        part[:, i] = total[:, :128].reshape(NZ, HB, 128)
        part[:, 4 + i] = total[:, 128:].reshape(NZ, HB, 128)
        val = val + nt(lhs, va[i])
    part[:, 3] = val.reshape(NZ, HB, 128)
    got(xo, R_XO)

    A, B = (0, 1, 2, 3), (4, 5, 6)
    RIGHT, LEFT = 0, 1
    to_dev = (right, left)

    def ring_sem(way, s, slab):
        if s < 3:
            return R_RING + (way * 3 + s) * 7 + slab
        return R_RING + 42 + slab

    def ring(way, s, slab, value):
        ring_s[way, s, slab] = value.astype(BF)
        send(
            ring_s.at[way, s, slab], ring_d.at[way, s, slab],
            S_LAST if s == 3 else S_RING, ring_sem(way, s, slab), to_dev[way],
        )

    def first(way, slab, value):
        ring(way, 0, slab, value)

    def arrived(way, s, slab):
        got(ring_d.at[way, s - 1, slab], ring_sem(way, s - 1, slab))

    def onward(way, s, slab, step):
        arrived(way, s, slab)
        ring(way, s, slab, part[at(step), slab] + ring_d[way, s - 1, slab].astype(F32))

    far = at(4)
    got(wo.at[far], R_W)
    for i in range(3):
        total = nt(wo[far, i], tokens(xo, 1 if i == 2 else 0))
        first(RIGHT, i, part[far, i] + total[:, :128])
        first(LEFT, 4 + i, part[far, 4 + i] + total[:, 128:])
    spread(xo, vo)
    val = part[far, 3]
    for i in range(3):
        val = val + nt(wo[far, i], vo[i])
    first(RIGHT, 3, val)

    got(wo.at[0:7], R_W + 1)
    val = jnp.zeros((NZ * HB, 128), F32)
    for i in range(3):
        lhs = wo[:, i].reshape(NZ * HB, W)
        total = nt(lhs, tokens(xo, 1 if i == 2 else 0))
        part[:, i] = part[:, i] + total[:, :128].reshape(NZ, HB, 128)
        part[:, 4 + i] = part[:, 4 + i] + total[:, 128:].reshape(NZ, HB, 128)
        first(LEFT, i, part[at(-3), i])
        first(RIGHT, 4 + i, part[at(3), 4 + i])
        val = val + nt(lhs, vo[i])
    part[:, 3] = part[:, 3] + val.reshape(NZ, HB, 128)
    first(LEFT, 3, part[at(-3), 3])
    send(part.at[z], swap_p, S_P, R_P, across)

    def both_long(s):
        for i in range(4):
            onward(RIGHT, s, A[i], 4 - s)
            if i < 3:
                onward(LEFT, s, B[i], s - 4)

    def both_short(s):
        for i in range(4):
            if i < 3:
                onward(RIGHT, s, B[i], 3 - s)
            onward(LEFT, s, A[i], s - 3)

    def half(ref, which):
        return ref[pl.ds(4 * c, 4), 32 * which : 32 * which + 32, :].reshape(128, W)

    gram = nt(va[0], half(xb, 0)) + nt(vo[0], half(xo, 0)) + nt(va[2], half(xb, 1)) + nt(vo[2], half(xo, 1))
    gram_s[...] = gram.reshape(NZ, 16, 128)
    gram_d[z] = gram_s[z]
    for k in range(1, NZ):
        send(gram_s.at[at(k)], gram_d.at[z], S_GS, R_GS, zdev(k))

    both_long(1)
    both_short(1)
    for copy in loads[8:]:
        copy.wait()
    got(gram_d.at[0:7], R_GS)
    gram_x[0] = jnp.sum(gram_d[...], axis=0)
    send(gram_x.at[0], gram_x.at[1], S_GX, R_GX, across)
    both_long(2)
    both_short(2)
    got(gram_x.at[1], R_GX)
    gram_all[c, z] = gram_x[0] + gram_x[1]
    for k in range(1, NZ):
        send(gram_all.at[c, z], gram_all.at[c, z], S_GA, R_GA, zdev(k))
    both_long(3)

    def pass_on(way, s, slab, dst, ss, rs):
        arrived(way, s, slab)
        send(ring_d.at[way, s - 1, slab], swap_d.at[dst, slab], ss, rs + slab, across)

    for i in range(4):
        if i < 3:
            pass_on(RIGHT, 3, B[i], 0, S_SHORT, R_SHORT)
        pass_on(LEFT, 3, A[i], 0, S_SHORT, R_SHORT)
    r_row = jnp.zeros((1, TOK), F32)
    for e in range(EX):
        r_row = r_row + jnp.where(ids[...] == e, sw[e], 0.0)
    for i in range(2):
        xt[i] = tokens(xb, i).T.astype(F32)
    got(gram_all.at[c, 0:7], R_GA)
    send(gram_all.at[c], gram_all.at[c], S_GC, R_GC, other)
    got(swap_p, R_P)
    for i in range(4):
        pass_on(RIGHT, 4, A[i], 1, S_LONG, R_LONG)
        if i < 3:
            pass_on(LEFT, 4, B[i], 1, S_LONG, R_LONG)

    def whole(slab):
        way = RIGHT if slab < 4 else LEFT
        mine_ = part[z, slab] + ring_d[1 - way, 2, slab].astype(F32) + ring_d[way, 3, slab].astype(F32)
        got(swap_d.at[0, slab], R_SHORT + slab)
        got(swap_d.at[1, slab], R_LONG + slab)
        theirs = swap_p[slab] + swap_d[0, slab].astype(F32) + swap_d[1, slab].astype(F32)
        return mine_ + theirs

    def block_terms(gate, up, back):
        sig = 1.0 / (1.0 + jnp.exp(-gate))
        act = gate * sig
        return act * up, back * up * sig * (1.0 + gate * (1.0 - sig)), back * act

    def gather_sem(way, step, slab):
        if step < 4:
            return R_A + (way * 3 + step - 1) * 6 + slab
        return R_A + 36 + slab

    def gather(src, block, way, step, slab):
        send(src, full.at[block, slab], S_A, gather_sem(way, step, slab), to_dev[way])

    for h in range(2):
        terms = block_terms(*[whole(4 * h + i) for i in range(3)])
        for i in range(3):
            own[3 * h + i] = terms[i].astype(BF)
            gather(own.at[3 * h + i], slot, RIGHT, 1, 3 * h + i)
            gather(own.at[3 * h + i], slot, LEFT, 1, 3 * h + i)
    send(own, full.at[slot], S_AC, R_AC, other)
    outs = [pltpu.make_async_copy(own, full.at[slot], hsem.at[0])]
    outs[0].start()

    def step_of_gather(step):
        blocks = [2 * at(-step) + c, 2 * at(step) + c]
        for i in range(6):
            for way in (RIGHT, LEFT):
                if step == 4 and i // 3 != way:
                    continue
                got(full.at[blocks[way], i], gather_sem(way, step, i))
                if step < 3 or (step == 3 and i // 3 == way):
                    gather(full.at[blocks[way], i], blocks[way], way, step + 1, i)
        if step < 4:
            for way in (RIGHT, LEFT):
                send(full.at[blocks[way]], full.at[blocks[way]], S_AC, R_AC, other)
        else:
            send(full.at[blocks[0]], full.at[blocks[0]], S_AC, R_AC, other)

    got(gram_all.at[1 - c], R_GC)
    kt = jnp.concatenate([gram_all[0].reshape(128, 128), gram_all[1].reshape(128, 128)], axis=1)
    rk = (kt * r_row).astype(BF)
    hb, dgb, dub = [jnp.concatenate([own[i], own[3 + i]], axis=1) for i in range(3)]
    val = whole(3)
    v_gate = val - LEARN_RATE * nt(dgb, rk)
    v_up = pltpu.roll(val, 124, 1) - LEARN_RATE * nt(dub, rk)
    v_back = pltpu.roll(val - LEARN_RATE * nt(hb, rk), 120, 1)
    lane = lax.broadcasted_iota(jnp.int32, (32, 128), 1)
    row = lax.broadcasted_iota(jnp.int32, (32, 128), 0)
    pick = jnp.logical_and(lane % 16 < 4, (lane // 16) * 4 + lane % 16 == row)
    mask_f = jnp.broadcast_to(mask[...].astype(F32), (16, 32)).astype(BF)
    mask_l = lax.dot_general(
        mask_f, jnp.where(pick, 1.0, 0.0).astype(BF), (((1,), (0,)), ((), ())), preferred_element_type=F32
    )[0:1]
    keep = jnp.broadcast_to(mask_l, (HB, 128)) > 0.5
    v_hid, v_dg, v_du = [jnp.where(keep, t, 0.0) for t in block_terms(v_gate, v_up, v_back)]
    inner = tn(v_dg.astype(BF), dgb) + tn(v_du.astype(BF), dub) + tn(pltpu.roll(v_hid, 8, 1).astype(BF), hb)
    token = jnp.sum(inner * kt, axis=0, keepdims=True)
    label = lax.broadcasted_iota(jnp.int32, (EX, TOK), 0)
    score = jnp.sum(jnp.where(ids[...] == label, token, 0.0), axis=1, keepdims=True)
    sc1[z] = jnp.broadcast_to(score, (EX, 128))
    for k in range(1, NZ):
        send(sc1.at[z], sc1.at[z], S_S1, R_S1, zdev(k))

    step_of_gather(1)
    step_of_gather(2)
    got(sc1.at[0:7], R_S1)
    sc2[c] = jnp.sum(sc1[...], axis=0)
    send(sc2.at[c], sc2.at[c], S_S2, R_S2, other)
    got(sc2.at[1 - c], R_S2)
    sc3[m] = sc2[0] + sc2[1]
    for k in range(1, NM):
        send(sc3.at[m], sc3.at[m], S_S3, R_S3, mdev(k))

    step_of_gather(3)
    got(sc3.at[0:7], R_S3)
    score = jnp.sum(sc3[...], axis=0)
    rms = jnp.sqrt(jnp.mean(score * score, axis=0, keepdims=True) + 1e-6)
    arg = score / (4.0 * rms)
    soft = jnp.maximum(arg, 0.0) + jnp.log(1.0 + jnp.exp(-jnp.abs(arg)))
    weights = EX * soft / jnp.sum(soft, axis=0, keepdims=True)
    diag = lax.broadcasted_iota(jnp.int32, (EX, 128), 0) == lax.broadcasted_iota(jnp.int32, (EX, 128), 1)
    wts_out[...] = jnp.sum(jnp.where(diag, weights, 0.0), axis=0, keepdims=True)[:, :EX]
    e_row = jnp.zeros((1, TOK), F32)
    for e in range(EX):
        e_row = e_row + jnp.where(ids[...] == e, weights[e : e + 1, 0:1], 0.0)
    for i in range(2):
        xs[i] = (xt[i] * e_row).astype(BF)
    copy = pltpu.make_async_copy(xs, xs_out, hsem.at[1])
    copy.start()
    outs.append(copy)

    step_of_gather(4)
    got(full.at[0:8], R_AC)
    for ref, ss in (
        (xb, S_X), (wo, S_W), (xb.at[0:7], S_XO), (ring_s.at[:, 0:3], S_RING), (swap_d.at[0], S_LAST), (swap_p, S_P),
        (swap_d.at[0], S_SHORT), (swap_d.at[1], S_LONG), (gram_d.at[0:7], S_GS), (gram_x.at[0], S_GX),
        (gram_all.at[0, 0:7], S_GA), (gram_all.at[0], S_GC), (full.at[0:7], S_A), (full.at[0:8], S_AC),
        (sc1.at[0:7], S_S1), (sc2.at[0], S_S2), (sc3.at[0:7], S_S3),
    ):
        pltpu.make_async_copy(ref, ref, ssem.at[ss]).wait()
    for copy in outs:
        copy.wait()


def grad_kernel(full, xs, wts, gg, gu, gd, out):
    def rows(i):
        return jnp.concatenate(
            [full[:, i].reshape(8 * HB, 128), full[:, 3 + i].reshape(8 * HB, 128)], axis=1
        )

    out[...] = wts[...]
    gd[...] = nt(rows(0), xs[1]).astype(BF)
    gg[...] = nt(xs[0], rows(1)).astype(BF)
    gu[...] = nt(xs[0], rows(2)).astype(BF)


def body(train_x, train_cot, val_x, val_cot, w_gate, w_up, w_down, step_weights, example_ids, val_mask):
    hbm = pl.BlockSpec(memory_space=pltpu.HBM)
    free = pl.BlockSpec(memory_space=pl.ANY)
    vmem = pl.BlockSpec(memory_space=pltpu.VMEM)
    V = pltpu.VMEM
    full, xs, wts = pl.pallas_call(
        comm_kernel,
        out_shape=(
            jax.ShapeDtypeStruct((16, 6, HB, 128), BF),
            jax.ShapeDtypeStruct((2, W, TOK), BF),
            jax.ShapeDtypeStruct((1, EX), F32),
        ),
        in_specs=[hbm] * 10,
        out_specs=(free, free, vmem),
        scratch_shapes=[
            pltpu.SMEM((EX,), F32),
            V((1, TOK), jnp.int32),
            V((1, 32), jnp.int32),
            V((2, 4, W), BF),
            V((2, W, 1792), BF),
            V((2, NZ, 3, HB, W), BF),
            V((NZ, 3, HB, W), BF),
            V((80, W), BF),
            V((16, W), F32),
            V((NM, 80, W), BF),
            V((NM, 80, W), BF),
            V((3, 128, W), BF),
            V((3, 128, W), BF),
            V((NZ, 7, HB, 128), F32),
            V((6, HB, 128), BF),
            V((2, 4, 7, HB, 128), BF),
            V((2, 4, 7, HB, 128), BF),
            V((7, HB, 128), F32),
            V((2, 7, HB, 128), BF),
            V((NZ, 16, 128), F32),
            V((NZ, 16, 128), F32),
            V((2, 16, 128), F32),
            V((2, NZ, 16, 128), F32),
            V((NZ, EX, 128), F32),
            V((2, EX, 128), F32),
            V((NM, EX, 128), F32),
            V((2, W, TOK), F32),
            V((2, W, TOK), BF),
            pltpu.SemaphoreType.DMA((11,)),
            pltpu.SemaphoreType.DMA((17,)),
            pltpu.SemaphoreType.DMA((125,)),
            pltpu.SemaphoreType.DMA((2,)),
        ],
        compiler_params=pltpu.CompilerParams(
            collective_id=0, has_side_effects=True, vmem_limit_bytes=40 * 1024 * 1024
        ),
        name="reduce_and_gather",
    )(
        *[
            pltpu.with_memory_space_constraint(a, pltpu.HBM)
            for a in (
                train_x, train_cot, val_x, val_cot, w_gate, w_up, w_down.reshape(NZ, 2, HB, W),
                step_weights, example_ids.reshape(1, TOK), val_mask.reshape(1, 32),
            )
        ]
    )
    gg, gu, gd, out = pl.pallas_call(
        grad_kernel,
        grid=(2,),
        out_shape=(
            jax.ShapeDtypeStruct((W, 1792), BF),
            jax.ShapeDtypeStruct((W, 1792), BF),
            jax.ShapeDtypeStruct((1792, W), BF),
            jax.ShapeDtypeStruct((1, EX), F32),
        ),
        in_specs=[
            pl.BlockSpec((8, 6, HB, 128), lambda i: (i, 0, 0, 0)),
            pl.BlockSpec((2, W, TOK), lambda i: (0, 0, 0)),
            pl.BlockSpec((1, EX), lambda i: (0, 0)),
        ],
        out_specs=(
            pl.BlockSpec((W, 8 * HB), lambda i: (0, i)),
            pl.BlockSpec((W, 8 * HB), lambda i: (0, i)),
            pl.BlockSpec((8 * HB, W), lambda i: (i, 0)),
            pl.BlockSpec((1, EX), lambda i: (0, 0)),
        ),
        compiler_params=pltpu.CompilerParams(vmem_limit_bytes=40 * 1024 * 1024),
        name="gradients",
    )(full, xs, wts)
    return gg, gu, gd, out.reshape(EX)


def solution(mesh):
    wide, tall = P("dp", "mp"), P("mp", "dp")
    return jax.shard_map(
        body,
        mesh=mesh,
        in_specs=(tall, tall, tall, tall, wide, wide, tall, P(), P(), P()),
        out_specs=(wide, wide, tall, P()),
        check_vma=False,
    )
```

```python
import jax
import jax.numpy as jnp
from jax import lax
from jax.experimental import pallas as pl
from jax.experimental.pallas import tpu as pltpu
from jax.sharding import PartitionSpec as P

MESH = pl.DeviceIdType.MESH
BF = jnp.bfloat16
F32 = jnp.float32

LEARN_RATE = 0.0003
NZ = 8
NM = 8
HB = 112
TOK = 256
W = 256
EX = 8


def nt(left, right):
    return lax.dot_general(left, right, (((1,), (1,)), ((), ())), preferred_element_type=F32)


def tn(left, right):
    return lax.dot_general(left, right, (((0,), (0,)), ((), ())), preferred_element_type=F32)


def comm_kernel(
    x_in, c_in, vx_in, vc_in, wg_in, wu_in, wd_in, sw_in, ids_in, mask_in,
    full, xs_out, wts_out,
    sw, ids, mask, vraw, wraw, wt, wo, pk, vstage, xb, xo, va, vo, part, own,
    ring_s, ring_d, swap_p, swap_d, gram_s, gram_d, gram_x, gram_all, sc1, sc2, sc3, xt, xs,
    lsem, ssem, rsem, hsem,
):
    d = lax.axis_index("dp")
    m = lax.axis_index("mp")
    z = d // 4
    xh = (d // 2) % 2
    c = d % 2
    slot = z * 2 + c

    def dev(zz, xx, cc):
        return (zz * 4 + xx * 2 + cc, m)

    def at(step):
        return (z + step + NZ) % NZ

    def zdev(step):
        return dev(at(step), xh, c)

    def mdev(step):
        return (d, (m + step) % NM)

    other = dev(z, xh, 1 - c)
    across = dev(z, 1 - xh, c)
    right, left = zdev(1), zdev(-1)

    def send(src, dst, ss, rs, to):
        pltpu.make_async_remote_copy(
            src_ref=src, dst_ref=dst, send_sem=ssem.at[ss], recv_sem=rsem.at[rs],
            device_id=to, device_id_type=MESH,
        ).start()

    def got(dst, rs):
        pltpu.make_async_copy(dst, dst, rsem.at[rs]).wait()

    R_X, R_XO, R_W, R_P, R_GS, R_GX, R_GA, R_GC, R_AC, R_S1, R_S2, R_S3 = 0, 8, 9, 11, 12, 13, 14, 15, 16, 17, 18, 19
    R_SHORT, R_LONG, R_RING, R_A = 20, 27, 34, 83

    (S_X, S_W, S_XO, S_RING, S_LAST, S_P, S_SHORT, S_LONG, S_GS, S_GX, S_GA, S_GC, S_A, S_AC, S_S1, S_S2, S_S3) = range(17)

    loads = [
        pltpu.make_async_copy(x_in, pk.at[0:32], lsem.at[0]),
        pltpu.make_async_copy(c_in, pk.at[32:64], lsem.at[1]),
        pltpu.make_async_copy(wg_in, wraw.at[0], lsem.at[2]),
        pltpu.make_async_copy(wu_in, wraw.at[1], lsem.at[3]),
        pltpu.make_async_copy(vx_in, vraw.at[0], lsem.at[4]),
        pltpu.make_async_copy(vc_in, vraw.at[1], lsem.at[5]),
        pltpu.make_async_copy(wd_in.at[:, 0], wt.at[0, :, 2], lsem.at[6]),
        pltpu.make_async_copy(wd_in.at[:, 1], wt.at[1, :, 2], lsem.at[7]),
        pltpu.make_async_copy(sw_in, sw, lsem.at[8]),
        pltpu.make_async_copy(ids_in, ids, lsem.at[9]),
        pltpu.make_async_copy(mask_in, mask, lsem.at[10]),
    ]
    for copy in loads:
        copy.start()

    barrier = pltpu.get_barrier_semaphore()
    peers = [mdev(k) for k in range(1, NM)] + [across, other] + [zdev(k) for k in range(1, NZ)]
    for peer in peers:
        pl.semaphore_signal(barrier, inc=1, device_id=peer, device_id_type=MESH)

    vstage[0:16] = jnp.zeros((16, W), F32)
    loads[4].wait()
    loads[5].wait()
    vstage[0:4] = vraw[0].astype(F32)
    vstage[4:8] = vraw[0].astype(F32)
    vstage[8:12] = vraw[1].astype(F32)
    pk[64:80] = vstage[0:16].astype(BF)
    loads[0].wait()
    loads[1].wait()
    xb[m] = pk[...]
    pl.semaphore_wait(barrier, len(peers))

    for k in range(1, NM):
        send(pk, xb.at[m], S_X, R_X + m, mdev(k))
    send(pk, xo.at[m], S_X, R_XO, other)

    for w in range(2):
        loads[2 + w].wait()
        for i in range(14):
            block = wraw[w, :, 128 * i : 128 * (i + 1)].T
            row = 128 * i
            while row < 128 * (i + 1):
                b = row // HB
                end = min(128 * (i + 1), (b + 1) * HB)
                wt[b % 2, b // 2, w, row - b * HB : end - b * HB] = block[row - 128 * i : end - 128 * i]
                row = end
    loads[6].wait()
    loads[7].wait()
    for step in (4, 3, 5, 2, 6, 1, 7, 0):
        send(wt.at[1 - c, at(step)], wo.at[at(step)], S_W, R_W if step == 4 else R_W + 1, other)

    for k in range(1, NM):
        j = (m + NM - k) % NM
        got(xb.at[j], R_X + j)
        send(xb.at[j], xo.at[j], S_XO, R_XO, other)
    place = lax.broadcasted_iota(jnp.int32, (128, W), 0) % 16

    def spread(src, dst):
        rows = src[:, 64:80, :].reshape(128, W).astype(F32)
        for i in range(3):
            keep = jnp.logical_and(place >= 4 * i, place < 4 * i + 4)
            dst[i] = jnp.where(keep, rows, 0.0).astype(BF)

    def tokens(ref, first):
        return ref[:, 32 * first : 32 * first + 32, :].reshape(TOK, W)

    spread(xb, va)
    val = jnp.zeros((NZ * HB, 128), F32)
    for i in range(3):
        lhs = wt[c, :, i].reshape(NZ * HB, W)
        total = nt(lhs, tokens(xb, 1 if i == 2 else 0))
        part[:, i] = total[:, :128].reshape(NZ, HB, 128)
        part[:, 4 + i] = total[:, 128:].reshape(NZ, HB, 128)
        val = val + nt(lhs, va[i])
    part[:, 3] = val.reshape(NZ, HB, 128)
    got(xo, R_XO)

    A, B = (0, 1, 2, 3), (4, 5, 6)
    RIGHT, LEFT = 0, 1
    to_dev = (right, left)

    def ring_sem(way, s, slab):
        if s < 3:
            return R_RING + (way * 3 + s) * 7 + slab
        return R_RING + 42 + slab

    def ring(way, s, slab, value):
        ring_s[way, s, slab] = value.astype(BF)
        send(
            ring_s.at[way, s, slab], ring_d.at[way, s, slab],
            S_LAST if s == 3 else S_RING, ring_sem(way, s, slab), to_dev[way],
        )

    def first(way, slab, value):
        ring(way, 0, slab, value)

    def arrived(way, s, slab):
        got(ring_d.at[way, s - 1, slab], ring_sem(way, s - 1, slab))

    def onward(way, s, slab, step):
        arrived(way, s, slab)
        ring(way, s, slab, part[at(step), slab] + ring_d[way, s - 1, slab].astype(F32))

    far = at(4)
    got(wo.at[far], R_W)
    for i in range(3):
        total = nt(wo[far, i], tokens(xo, 1 if i == 2 else 0))
        first(RIGHT, i, part[far, i] + total[:, :128])
        first(LEFT, 4 + i, part[far, 4 + i] + total[:, 128:])
    spread(xo, vo)
    val = part[far, 3]
    for i in range(3):
        val = val + nt(wo[far, i], vo[i])
    first(RIGHT, 3, val)

    got(wo.at[0:7], R_W + 1)
    val = jnp.zeros((NZ * HB, 128), F32)
    for i in range(3):
        lhs = wo[:, i].reshape(NZ * HB, W)
        total = nt(lhs, tokens(xo, 1 if i == 2 else 0))
        part[:, i] = part[:, i] + total[:, :128].reshape(NZ, HB, 128)
        part[:, 4 + i] = part[:, 4 + i] + total[:, 128:].reshape(NZ, HB, 128)
        first(LEFT, i, part[at(-3), i])
        first(RIGHT, 4 + i, part[at(3), 4 + i])
        val = val + nt(lhs, vo[i])
    part[:, 3] = part[:, 3] + val.reshape(NZ, HB, 128)
    first(LEFT, 3, part[at(-3), 3])
    send(part.at[z], swap_p, S_P, R_P, across)

    def both_long(s):
        for i in range(4):
            onward(RIGHT, s, A[i], 4 - s)
            if i < 3:
                onward(LEFT, s, B[i], s - 4)

    def both_short(s):
        for i in range(4):
            if i < 3:
                onward(RIGHT, s, B[i], 3 - s)
            onward(LEFT, s, A[i], s - 3)

    def half(ref, which):
        return ref[pl.ds(4 * c, 4), 32 * which : 32 * which + 32, :].reshape(128, W)

    gram = nt(va[0], half(xb, 0)) + nt(vo[0], half(xo, 0)) + nt(va[2], half(xb, 1)) + nt(vo[2], half(xo, 1))
    gram_s[...] = gram.reshape(NZ, 16, 128)
    gram_d[z] = gram_s[z]
    for k in range(1, NZ):
        send(gram_s.at[at(k)], gram_d.at[z], S_GS, R_GS, zdev(k))

    both_long(1)
    both_short(1)
    for copy in loads[8:]:
        copy.wait()
    got(gram_d.at[0:7], R_GS)
    gram_x[0] = jnp.sum(gram_d[...], axis=0)
    send(gram_x.at[0], gram_x.at[1], S_GX, R_GX, across)
    both_long(2)
    both_short(2)
    got(gram_x.at[1], R_GX)
    gram_all[c, z] = gram_x[0] + gram_x[1]
    for k in range(1, NZ):
        send(gram_all.at[c, z], gram_all.at[c, z], S_GA, R_GA, zdev(k))
    both_long(3)

    def pass_on(way, s, slab, dst, ss, rs):
        arrived(way, s, slab)
        send(ring_d.at[way, s - 1, slab], swap_d.at[dst, slab], ss, rs + slab, across)

    for i in range(3):
        pass_on(LEFT, 3, A[i], 0, S_SHORT, R_SHORT)
    for i in range(3):
        pass_on(RIGHT, 3, B[i], 0, S_SHORT, R_SHORT)
    pass_on(LEFT, 3, 3, 0, S_SHORT, R_SHORT)
    r_row = jnp.zeros((1, TOK), F32)
    for e in range(EX):
        r_row = r_row + jnp.where(ids[...] == e, sw[e], 0.0)
    for i in range(2):
        xt[i] = tokens(xb, i).T.astype(F32)
    got(gram_all.at[c, 0:7], R_GA)
    send(gram_all.at[c], gram_all.at[c], S_GC, R_GC, other)
    got(swap_p, R_P)
    for i in range(3):
        pass_on(RIGHT, 4, A[i], 1, S_LONG, R_LONG)
    for i in range(3):
        pass_on(LEFT, 4, B[i], 1, S_LONG, R_LONG)
    pass_on(RIGHT, 4, 3, 1, S_LONG, R_LONG)

    def whole(slab):
        way = RIGHT if slab < 4 else LEFT
        mine_ = part[z, slab] + ring_d[1 - way, 2, slab].astype(F32) + ring_d[way, 3, slab].astype(F32)
        got(swap_d.at[0, slab], R_SHORT + slab)
        got(swap_d.at[1, slab], R_LONG + slab)
        theirs = swap_p[slab] + swap_d[0, slab].astype(F32) + swap_d[1, slab].astype(F32)
        return mine_ + theirs

    def block_terms(gate, up, back):
        sig = 1.0 / (1.0 + jnp.exp(-gate))
        act = gate * sig
        return act * up, back * up * sig * (1.0 + gate * (1.0 - sig)), back * act

    def gather_sem(way, step, slab):
        if step < 4:
            return R_A + (way * 3 + step - 1) * 6 + slab
        return R_A + 36 + slab

    def gather(src, block, way, step, slab):
        send(src, full.at[block, slab], S_A, gather_sem(way, step, slab), to_dev[way])

    for h in range(2):
        terms = block_terms(*[whole(4 * h + i) for i in range(3)])
        for i in range(3):
            own[3 * h + i] = terms[i].astype(BF)
            gather(own.at[3 * h + i], slot, RIGHT, 1, 3 * h + i)
            gather(own.at[3 * h + i], slot, LEFT, 1, 3 * h + i)
    send(own, full.at[slot], S_AC, R_AC, other)
    outs = [pltpu.make_async_copy(own, full.at[slot], hsem.at[0])]
    outs[0].start()

    def step_of_gather(step):
        blocks = [2 * at(-step) + c, 2 * at(step) + c]
        for i in range(6):
            for way in (RIGHT, LEFT):
                if step == 4 and i // 3 != way:
                    continue
                got(full.at[blocks[way], i], gather_sem(way, step, i))
                if step < 3 or (step == 3 and i // 3 == way):
                    gather(full.at[blocks[way], i], blocks[way], way, step + 1, i)
        if step < 4:
            for way in (RIGHT, LEFT):
                send(full.at[blocks[way]], full.at[blocks[way]], S_AC, R_AC, other)
        else:
            send(full.at[blocks[0]], full.at[blocks[0]], S_AC, R_AC, other)

    got(gram_all.at[1 - c], R_GC)
    kt = jnp.concatenate([gram_all[0].reshape(128, 128), gram_all[1].reshape(128, 128)], axis=1)
    rk = (kt * r_row).astype(BF)
    hb, dgb, dub = [jnp.concatenate([own[i], own[3 + i]], axis=1) for i in range(3)]
    val = whole(3)
    v_gate = val - LEARN_RATE * nt(dgb, rk)
    v_up = pltpu.roll(val, 124, 1) - LEARN_RATE * nt(dub, rk)
    v_back = pltpu.roll(val - LEARN_RATE * nt(hb, rk), 120, 1)
    lane = lax.broadcasted_iota(jnp.int32, (32, 128), 1)
    row = lax.broadcasted_iota(jnp.int32, (32, 128), 0)
    pick = jnp.logical_and(lane % 16 < 4, (lane // 16) * 4 + lane % 16 == row)
    mask_f = jnp.broadcast_to(mask[...].astype(F32), (16, 32)).astype(BF)
    mask_l = lax.dot_general(
        mask_f, jnp.where(pick, 1.0, 0.0).astype(BF), (((1,), (0,)), ((), ())), preferred_element_type=F32
    )[0:1]
    keep = jnp.broadcast_to(mask_l, (HB, 128)) > 0.5
    v_hid, v_dg, v_du = [jnp.where(keep, t, 0.0) for t in block_terms(v_gate, v_up, v_back)]
    inner = tn(v_dg.astype(BF), dgb) + tn(v_du.astype(BF), dub) + tn(pltpu.roll(v_hid, 8, 1).astype(BF), hb)
    token = jnp.sum(inner * kt, axis=0, keepdims=True)
    label = lax.broadcasted_iota(jnp.int32, (EX, TOK), 0)
    score = jnp.sum(jnp.where(ids[...] == label, token, 0.0), axis=1, keepdims=True)
    sc1[z] = jnp.broadcast_to(score, (EX, 128))
    for k in range(1, NZ):
        send(sc1.at[z], sc1.at[z], S_S1, R_S1, zdev(k))

    step_of_gather(1)
    step_of_gather(2)
    got(sc1.at[0:7], R_S1)
    sc2[c] = jnp.sum(sc1[...], axis=0)
    send(sc2.at[c], sc2.at[c], S_S2, R_S2, other)
    got(sc2.at[1 - c], R_S2)
    sc3[m] = sc2[0] + sc2[1]
    for k in range(1, NM):
        send(sc3.at[m], sc3.at[m], S_S3, R_S3, mdev(k))

    step_of_gather(3)
    got(sc3.at[0:7], R_S3)
    score = jnp.sum(sc3[...], axis=0)
    rms = jnp.sqrt(jnp.mean(score * score, axis=0, keepdims=True) + 1e-6)
    arg = score / (4.0 * rms)
    soft = jnp.maximum(arg, 0.0) + jnp.log(1.0 + jnp.exp(-jnp.abs(arg)))
    weights = EX * soft / jnp.sum(soft, axis=0, keepdims=True)
    diag = lax.broadcasted_iota(jnp.int32, (EX, 128), 0) == lax.broadcasted_iota(jnp.int32, (EX, 128), 1)
    wts_out[...] = jnp.sum(jnp.where(diag, weights, 0.0), axis=0, keepdims=True)[:, :EX]
    e_row = jnp.zeros((1, TOK), F32)
    for e in range(EX):
        e_row = e_row + jnp.where(ids[...] == e, weights[e : e + 1, 0:1], 0.0)
    for i in range(2):
        xs[i] = (xt[i] * e_row).astype(BF)
    copy = pltpu.make_async_copy(xs, xs_out, hsem.at[1])
    copy.start()
    outs.append(copy)

    step_of_gather(4)
    got(full.at[0:8], R_AC)
    for ref, ss in (
        (xb, S_X), (wo, S_W), (xb.at[0:7], S_XO), (ring_s.at[:, 0:3], S_RING), (swap_d.at[0], S_LAST), (swap_p, S_P),
        (swap_d.at[0], S_SHORT), (swap_d.at[1], S_LONG), (gram_d.at[0:7], S_GS), (gram_x.at[0], S_GX),
        (gram_all.at[0, 0:7], S_GA), (gram_all.at[0], S_GC), (full.at[0:7], S_A), (full.at[0:8], S_AC),
        (sc1.at[0:7], S_S1), (sc2.at[0], S_S2), (sc3.at[0:7], S_S3),
    ):
        pltpu.make_async_copy(ref, ref, ssem.at[ss]).wait()
    for copy in outs:
        copy.wait()


def grad_kernel(full, xs, wts, gg, gu, gd, out, bg, bu, bd, sems):
    copies = []

    def write(src, dst):
        copies.append(pltpu.make_async_copy(src, dst, sems.at[len(copies)]))
        copies[-1].start()

    out[...] = wts[...]
    for h in range(2):
        part = slice(8 * HB * h, 8 * HB * (h + 1))

        def rows(i):
            block = full[8 * h : 8 * h + 8]
            return jnp.concatenate(
                [block[:, i].reshape(8 * HB, 128), block[:, 3 + i].reshape(8 * HB, 128)], axis=1
            )

        bd[part] = nt(rows(0), xs[1]).astype(BF)
        write(bd.at[part], gd.at[part])
        bg[:, part] = nt(xs[0], rows(1)).astype(BF)
        write(bg.at[:, part], gg.at[:, part])
        bu[:, part] = nt(xs[0], rows(2)).astype(BF)
        write(bu.at[:, part], gu.at[:, part])
    for copy in copies:
        copy.wait()


def body(train_x, train_cot, val_x, val_cot, w_gate, w_up, w_down, step_weights, example_ids, val_mask):
    hbm = pl.BlockSpec(memory_space=pltpu.HBM)
    free = pl.BlockSpec(memory_space=pl.ANY)
    vmem = pl.BlockSpec(memory_space=pltpu.VMEM)
    V = pltpu.VMEM
    full, xs, wts = pl.pallas_call(
        comm_kernel,
        out_shape=(
            jax.ShapeDtypeStruct((16, 6, HB, 128), BF),
            jax.ShapeDtypeStruct((2, W, TOK), BF),
            jax.ShapeDtypeStruct((1, EX), F32),
        ),
        in_specs=[hbm] * 10,
        out_specs=(free, free, vmem),
        scratch_shapes=[
            pltpu.SMEM((EX,), F32),
            V((1, TOK), jnp.int32),
            V((1, 32), jnp.int32),
            V((2, 4, W), BF),
            V((2, W, 1792), BF),
            V((2, NZ, 3, HB, W), BF),
            V((NZ, 3, HB, W), BF),
            V((80, W), BF),
            V((16, W), F32),
            V((NM, 80, W), BF),
            V((NM, 80, W), BF),
            V((3, 128, W), BF),
            V((3, 128, W), BF),
            V((NZ, 7, HB, 128), F32),
            V((6, HB, 128), BF),
            V((2, 4, 7, HB, 128), BF),
            V((2, 4, 7, HB, 128), BF),
            V((7, HB, 128), F32),
            V((2, 7, HB, 128), BF),
            V((NZ, 16, 128), F32),
            V((NZ, 16, 128), F32),
            V((2, 16, 128), F32),
            V((2, NZ, 16, 128), F32),
            V((NZ, EX, 128), F32),
            V((2, EX, 128), F32),
            V((NM, EX, 128), F32),
            V((2, W, TOK), F32),
            V((2, W, TOK), BF),
            pltpu.SemaphoreType.DMA((11,)),
            pltpu.SemaphoreType.DMA((17,)),
            pltpu.SemaphoreType.DMA((125,)),
            pltpu.SemaphoreType.DMA((2,)),
        ],
        compiler_params=pltpu.CompilerParams(
            collective_id=0, has_side_effects=True, vmem_limit_bytes=40 * 1024 * 1024
        ),
        name="reduce_and_gather",
    )(
        *[
            pltpu.with_memory_space_constraint(a, pltpu.HBM)
            for a in (
                train_x, train_cot, val_x, val_cot, w_gate, w_up, w_down.reshape(NZ, 2, HB, W),
                step_weights, example_ids.reshape(1, TOK), val_mask.reshape(1, 32),
            )
        ]
    )
    gg, gu, gd, out = pl.pallas_call(
        grad_kernel,
        out_shape=(
            jax.ShapeDtypeStruct((W, 1792), BF),
            jax.ShapeDtypeStruct((W, 1792), BF),
            jax.ShapeDtypeStruct((1792, W), BF),
            jax.ShapeDtypeStruct((1, EX), F32),
        ),
        in_specs=[vmem] * 3,
        out_specs=(free, free, free, vmem),
        scratch_shapes=[V((W, 1792), BF), V((W, 1792), BF), V((1792, W), BF), pltpu.SemaphoreType.DMA((6,))],
        compiler_params=pltpu.CompilerParams(vmem_limit_bytes=40 * 1024 * 1024),
        name="gradients",
    )(full, xs, wts)
    return gg, gu, gd, out.reshape(EX)


def solution(mesh):
    wide, tall = P("dp", "mp"), P("mp", "dp")
    return jax.shard_map(
        body,
        mesh=mesh,
        in_specs=(tall, tall, tall, tall, wide, wide, tall, P(), P(), P()),
        out_specs=(wide, wide, tall, P()),
        check_vma=False,
    )
```

```python
import jax
import jax.numpy as jnp
from jax import lax
from jax.experimental import pallas as pl
from jax.experimental.pallas import tpu as pltpu
from jax.sharding import PartitionSpec as P

MESH = pl.DeviceIdType.MESH
BF = jnp.bfloat16
F32 = jnp.float32

LEARN_RATE = 0.0003
NZ = 8
NM = 8
HB = 112
TOK = 256
W = 256
EX = 8


def nt(left, right):
    return lax.dot_general(left, right, (((1,), (1,)), ((), ())), preferred_element_type=F32)


def tn(left, right):
    return lax.dot_general(left, right, (((0,), (0,)), ((), ())), preferred_element_type=F32)


def comm_kernel(
    x_in, c_in, vx_in, vc_in, wg_in, wu_in, wd_in, sw_in, ids_in, mask_in,
    full, xs_out, wts_out,
    sw, ids, mask, vraw, wraw, wt, wo, pk, vstage, xb, xo, va, vo, part, own,
    ring_s, ring_d, swap_p, swap_d, gram_s, gram_d, gram_x, gram_all, sc1, sc2, sc3, xt, xs,
    lsem, ssem, rsem, hsem,
):
    d = lax.axis_index("dp")
    m = lax.axis_index("mp")
    z = d // 4
    xh = (d // 2) % 2
    c = d % 2
    slot = z * 2 + c

    def dev(zz, xx, cc):
        return (zz * 4 + xx * 2 + cc, m)

    def at(step):
        return (z + step + NZ) % NZ

    def zdev(step):
        return dev(at(step), xh, c)

    def mdev(step):
        return (d, (m + step) % NM)

    other = dev(z, xh, 1 - c)
    across = dev(z, 1 - xh, c)
    right, left = zdev(1), zdev(-1)

    def send(src, dst, ss, rs, to):
        pltpu.make_async_remote_copy(
            src_ref=src, dst_ref=dst, send_sem=ssem.at[ss], recv_sem=rsem.at[rs],
            device_id=to, device_id_type=MESH,
        ).start()

    def got(dst, rs):
        pltpu.make_async_copy(dst, dst, rsem.at[rs]).wait()

    R_X, R_XO, R_W, R_P, R_GS, R_GX, R_GA, R_GC, R_AC, R_S1, R_S2, R_S3 = 0, 8, 9, 11, 12, 13, 14, 15, 16, 17, 18, 19
    R_SHORT, R_LONG, R_RING, R_A, R_Y, R_YO = 20, 27, 34, 83, 125, 133

    (S_X, S_W, S_XO, S_RING, S_LAST, S_P, S_SHORT, S_LONG, S_GS, S_GX, S_GA, S_GC, S_A, S_AC, S_S1, S_S2, S_S3, S_Y, S_YO) = range(19)

    barrier = pltpu.get_barrier_semaphore()
    peers = [mdev(k) for k in range(1, NM)] + [across, other] + [zdev(k) for k in range(1, NZ)]
    for peer in peers:
        pl.semaphore_signal(barrier, inc=1, device_id=peer, device_id_type=MESH)

    loads = [
        pltpu.make_async_copy(x_in, pk.at[0:32], lsem.at[0]),
        pltpu.make_async_copy(c_in, pk.at[48:80], lsem.at[1]),
        pltpu.make_async_copy(wg_in, wraw.at[0], lsem.at[2]),
        pltpu.make_async_copy(wu_in, wraw.at[1], lsem.at[3]),
        pltpu.make_async_copy(vx_in, vraw.at[0], lsem.at[4]),
        pltpu.make_async_copy(vc_in, vraw.at[1], lsem.at[5]),
        pltpu.make_async_copy(wd_in.at[:, 0], wt.at[0, :, 2], lsem.at[6]),
        pltpu.make_async_copy(wd_in.at[:, 1], wt.at[1, :, 2], lsem.at[7]),
        pltpu.make_async_copy(sw_in, sw, lsem.at[8]),
        pltpu.make_async_copy(ids_in, ids, lsem.at[9]),
        pltpu.make_async_copy(mask_in, mask, lsem.at[10]),
    ]
    for copy in loads:
        copy.start()

    vstage[0:16] = jnp.zeros((16, W), F32)
    loads[4].wait()
    loads[5].wait()
    vstage[0:4] = vraw[0].astype(F32)
    vstage[4:8] = vraw[0].astype(F32)
    vstage[8:12] = vraw[1].astype(F32)
    pk[32:48] = vstage[0:16].astype(BF)
    loads[0].wait()
    loads[1].wait()
    xb[m] = pk[...]
    pl.semaphore_wait(barrier, len(peers))

    for k in (4, 3, 5, 2, 6, 1, 7):
        send(pk.at[0:48], xb.at[m, 0:48], S_X, R_X + m, mdev(k))
    send(pk.at[0:48], xo.at[m, 0:48], S_X, R_XO, other)
    for k in (4, 3, 5, 2, 6, 1, 7):
        send(pk.at[48:80], xb.at[m, 48:80], S_Y, R_Y + m, mdev(k))
    send(pk.at[48:80], xo.at[m, 48:80], S_Y, R_YO, other)

    for w in range(2):
        loads[2 + w].wait()
        for i in range(14):
            block = wraw[w, :, 128 * i : 128 * (i + 1)].T
            row = 128 * i
            while row < 128 * (i + 1):
                b = row // HB
                end = min(128 * (i + 1), (b + 1) * HB)
                wt[b % 2, b // 2, w, row - b * HB : end - b * HB] = block[row - 128 * i : end - 128 * i]
                row = end
    loads[6].wait()
    loads[7].wait()
    for step in (4, 3, 5, 2, 6, 1, 7, 0):
        send(wt.at[1 - c, at(step)], wo.at[at(step)], S_W, R_W if step == 4 else R_W + 1, other)

    for k in (1, 7, 2, 6, 3, 5, 4):
        j = (m + NM - k) % NM
        got(xb.at[j, 0:48], R_X + j)
        send(xb.at[j, 0:48], xo.at[j, 0:48], S_XO, R_XO, other)
    place = lax.broadcasted_iota(jnp.int32, (128, W), 0) % 16

    def spread(src, dst):
        rows = src[:, 32:48, :].reshape(128, W).astype(F32)
        for i in range(3):
            keep = jnp.logical_and(place >= 4 * i, place < 4 * i + 4)
            dst[i] = jnp.where(keep, rows, 0.0).astype(BF)

    def tokens(ref, first):
        return ref[:, 48 * first : 48 * first + 32, :].reshape(TOK, W)

    def own_width(i):
        lhs = wt[c, :, i].reshape(NZ * HB, W)
        total = nt(lhs, tokens(xb, 1 if i == 2 else 0))
        part[:, i] = total[:, :128].reshape(NZ, HB, 128)
        part[:, 4 + i] = total[:, 128:].reshape(NZ, HB, 128)

    own_width(0)
    own_width(1)
    for k in (1, 7, 2, 6, 3, 5, 4):
        j = (m + NM - k) % NM
        got(xb.at[j, 48:80], R_Y + j)
        send(xb.at[j, 48:80], xo.at[j, 48:80], S_YO, R_YO, other)
    got(xo.at[:, 0:48], R_XO)

    A, B = (0, 1, 2, 3), (4, 5, 6)
    RIGHT, LEFT = 0, 1
    to_dev = (right, left)

    def ring_sem(way, s, slab):
        if s < 3:
            return R_RING + (way * 3 + s) * 7 + slab
        return R_RING + 42 + slab

    def ring(way, s, slab, value):
        ring_s[way, s, slab] = value.astype(BF)
        send(
            ring_s.at[way, s, slab], ring_d.at[way, s, slab],
            S_LAST if s == 3 else S_RING, ring_sem(way, s, slab), to_dev[way],
        )

    def first(way, slab, value):
        ring(way, 0, slab, value)

    def arrived(way, s, slab):
        got(ring_d.at[way, s - 1, slab], ring_sem(way, s - 1, slab))

    def onward(way, s, slab, step):
        arrived(way, s, slab)
        ring(way, s, slab, part[at(step), slab] + ring_d[way, s - 1, slab].astype(F32))

    far = at(4)
    got(wo.at[far], R_W)
    for i in range(3):
        if i == 2:
            own_width(2)
            got(xo.at[:, 48:80], R_YO)
        total = nt(wo[far, i], tokens(xo, 1 if i == 2 else 0))
        first(RIGHT, i, part[far, i] + total[:, :128])
        first(LEFT, 4 + i, part[far, 4 + i] + total[:, 128:])
    spread(xb, va)
    spread(xo, vo)
    val = jnp.zeros((HB, 128), F32)
    for i in range(3):
        val = val + nt(wt[c, far, i], va[i]) + nt(wo[far, i], vo[i])
    first(RIGHT, 3, val)

    got(wo.at[0:7], R_W + 1)
    val = jnp.zeros((NZ * HB, 128), F32)
    for i in range(3):
        lhs = wo[:, i].reshape(NZ * HB, W)
        total = nt(lhs, tokens(xo, 1 if i == 2 else 0))
        part[:, i] = part[:, i] + total[:, :128].reshape(NZ, HB, 128)
        part[:, 4 + i] = part[:, 4 + i] + total[:, 128:].reshape(NZ, HB, 128)
        first(LEFT, i, part[at(-3), i])
        first(RIGHT, 4 + i, part[at(3), 4 + i])
        val = val + nt(lhs, vo[i]) + nt(wt[c, :, i].reshape(NZ * HB, W), va[i])
    part[:, 3] = val.reshape(NZ, HB, 128)
    first(LEFT, 3, part[at(-3), 3])
    send(part.at[z], swap_p, S_P, R_P, across)

    def both_long(s):
        for i in range(4):
            onward(RIGHT, s, A[i], 4 - s)
            if i < 3:
                onward(LEFT, s, B[i], s - 4)

    def both_short(s):
        for i in range(4):
            if i < 3:
                onward(RIGHT, s, B[i], 3 - s)
            onward(LEFT, s, A[i], s - 3)

    def half(ref, which):
        return ref[pl.ds(4 * c, 4), 48 * which : 48 * which + 32, :].reshape(128, W)

    gram = nt(va[0], half(xb, 0)) + nt(vo[0], half(xo, 0)) + nt(va[2], half(xb, 1)) + nt(vo[2], half(xo, 1))
    gram_s[...] = gram.reshape(NZ, 16, 128)
    gram_d[z] = gram_s[z]
    for k in range(1, NZ):
        send(gram_s.at[at(k)], gram_d.at[z], S_GS, R_GS, zdev(k))

    both_long(1)
    both_short(1)
    for copy in loads[8:]:
        copy.wait()
    got(gram_d.at[0:7], R_GS)
    gram_x[0] = jnp.sum(gram_d[...], axis=0)
    send(gram_x.at[0], gram_x.at[1], S_GX, R_GX, across)
    both_long(2)
    both_short(2)
    got(gram_x.at[1], R_GX)
    gram_all[c, z] = gram_x[0] + gram_x[1]
    for k in range(1, NZ):
        send(gram_all.at[c, z], gram_all.at[c, z], S_GA, R_GA, zdev(k))
    both_long(3)

    def pass_on(way, s, slab, dst, ss, rs):
        arrived(way, s, slab)
        send(ring_d.at[way, s - 1, slab], swap_d.at[dst, slab], ss, rs + slab, across)

    for i in range(3):
        pass_on(LEFT, 3, A[i], 0, S_SHORT, R_SHORT)
    for i in range(3):
        pass_on(RIGHT, 3, B[i], 0, S_SHORT, R_SHORT)
    pass_on(LEFT, 3, 3, 0, S_SHORT, R_SHORT)
    r_row = jnp.zeros((1, TOK), F32)
    for e in range(EX):
        r_row = r_row + jnp.where(ids[...] == e, sw[e], 0.0)
    for i in range(2):
        xt[i] = tokens(xb, i).T.astype(F32)
    got(gram_all.at[c, 0:7], R_GA)
    send(gram_all.at[c], gram_all.at[c], S_GC, R_GC, other)
    got(swap_p, R_P)
    for i in range(3):
        pass_on(RIGHT, 4, A[i], 1, S_LONG, R_LONG)
    for i in range(3):
        pass_on(LEFT, 4, B[i], 1, S_LONG, R_LONG)
    pass_on(RIGHT, 4, 3, 1, S_LONG, R_LONG)

    def whole(slab):
        way = RIGHT if slab < 4 else LEFT
        mine_ = part[z, slab] + ring_d[1 - way, 2, slab].astype(F32) + ring_d[way, 3, slab].astype(F32)
        got(swap_d.at[0, slab], R_SHORT + slab)
        got(swap_d.at[1, slab], R_LONG + slab)
        theirs = swap_p[slab] + swap_d[0, slab].astype(F32) + swap_d[1, slab].astype(F32)
        return mine_ + theirs

    def block_terms(gate, up, back):
        sig = 1.0 / (1.0 + jnp.exp(-gate))
        act = gate * sig
        return act * up, back * up * sig * (1.0 + gate * (1.0 - sig)), back * act

    def gather_sem(way, step, slab):
        if step < 4:
            return R_A + (way * 3 + step - 1) * 6 + slab
        return R_A + 36 + slab

    def gather(src, block, way, step, slab):
        send(src, full.at[block, slab], S_A, gather_sem(way, step, slab), to_dev[way])

    for h in range(2):
        terms = block_terms(*[whole(4 * h + i) for i in range(3)])
        for i in range(3):
            own[3 * h + i] = terms[i].astype(BF)
            gather(own.at[3 * h + i], slot, RIGHT, 1, 3 * h + i)
            gather(own.at[3 * h + i], slot, LEFT, 1, 3 * h + i)
    send(own, full.at[slot], S_AC, R_AC, other)
    outs = [pltpu.make_async_copy(own, full.at[slot], hsem.at[0])]
    outs[0].start()

    def step_of_gather(step):
        blocks = [2 * at(-step) + c, 2 * at(step) + c]
        order = (0, 3, 1, 4, 2, 5) if step == 4 else range(6)
        for i in order:
            for way in (RIGHT, LEFT):
                if step == 4 and i // 3 != way:
                    continue
                got(full.at[blocks[way], i], gather_sem(way, step, i))
                if step < 3 or (step == 3 and i // 3 == way):
                    gather(full.at[blocks[way], i], blocks[way], way, step + 1, i)
                if step == 4:
                    send(full.at[blocks[way], i], full.at[blocks[way], i], S_AC, R_AC, other)
        if step < 4:
            for way in (RIGHT, LEFT):
                send(full.at[blocks[way]], full.at[blocks[way]], S_AC, R_AC, other)

    got(gram_all.at[1 - c], R_GC)
    kt = jnp.concatenate([gram_all[0].reshape(128, 128), gram_all[1].reshape(128, 128)], axis=1)
    rk = (kt * r_row).astype(BF)
    hb, dgb, dub = [jnp.concatenate([own[i], own[3 + i]], axis=1) for i in range(3)]
    val = whole(3)
    v_gate = val - LEARN_RATE * nt(dgb, rk)
    v_up = pltpu.roll(val, 124, 1) - LEARN_RATE * nt(dub, rk)
    v_back = pltpu.roll(val - LEARN_RATE * nt(hb, rk), 120, 1)
    lane = lax.broadcasted_iota(jnp.int32, (32, 128), 1)
    row = lax.broadcasted_iota(jnp.int32, (32, 128), 0)
    pick = jnp.logical_and(lane % 16 < 4, (lane // 16) * 4 + lane % 16 == row)
    mask_f = jnp.broadcast_to(mask[...].astype(F32), (16, 32)).astype(BF)
    mask_l = lax.dot_general(
        mask_f, jnp.where(pick, 1.0, 0.0).astype(BF), (((1,), (0,)), ((), ())), preferred_element_type=F32
    )[0:1]
    keep = jnp.broadcast_to(mask_l, (HB, 128)) > 0.5
    v_hid, v_dg, v_du = [jnp.where(keep, t, 0.0) for t in block_terms(v_gate, v_up, v_back)]
    inner = tn(v_dg.astype(BF), dgb) + tn(v_du.astype(BF), dub) + tn(pltpu.roll(v_hid, 8, 1).astype(BF), hb)
    token = jnp.sum(inner * kt, axis=0, keepdims=True)
    label = lax.broadcasted_iota(jnp.int32, (EX, TOK), 0)
    score = jnp.sum(jnp.where(ids[...] == label, token, 0.0), axis=1, keepdims=True)
    sc1[z] = jnp.broadcast_to(score, (EX, 128))
    for k in range(1, NZ):
        send(sc1.at[z], sc1.at[z], S_S1, R_S1, zdev(k))

    step_of_gather(1)
    step_of_gather(2)
    got(sc1.at[0:7], R_S1)
    sc2[c] = jnp.sum(sc1[...], axis=0)
    send(sc2.at[c], sc2.at[c], S_S2, R_S2, other)
    got(sc2.at[1 - c], R_S2)
    sc3[m] = sc2[0] + sc2[1]
    for k in range(1, NM):
        send(sc3.at[m], sc3.at[m], S_S3, R_S3, mdev(k))

    step_of_gather(3)
    got(sc3.at[0:7], R_S3)
    score = jnp.sum(sc3[...], axis=0)
    rms = jnp.sqrt(jnp.mean(score * score, axis=0, keepdims=True) + 1e-6)
    arg = score / (4.0 * rms)
    soft = jnp.maximum(arg, 0.0) + jnp.log(1.0 + jnp.exp(-jnp.abs(arg)))
    weights = EX * soft / jnp.sum(soft, axis=0, keepdims=True)
    diag = lax.broadcasted_iota(jnp.int32, (EX, 128), 0) == lax.broadcasted_iota(jnp.int32, (EX, 128), 1)
    wts_out[...] = jnp.sum(jnp.where(diag, weights, 0.0), axis=0, keepdims=True)[:, :EX]
    e_row = jnp.zeros((1, TOK), F32)
    for e in range(EX):
        e_row = e_row + jnp.where(ids[...] == e, weights[e : e + 1, 0:1], 0.0)
    for i in range(2):
        xs[i] = (xt[i] * e_row).astype(BF)
    copy = pltpu.make_async_copy(xs, xs_out, hsem.at[1])
    copy.start()
    outs.append(copy)

    step_of_gather(4)
    got(full.at[0:8], R_AC)
    for ref, ss in (
        (xb.at[:, 0:48], S_X), (xb.at[:, 48:80], S_Y), (wo, S_W), (xb.at[0:7, 0:48], S_XO), (xb.at[0:7, 48:80], S_YO), (ring_s.at[:, 0:3], S_RING), (swap_d.at[0], S_LAST), (swap_p, S_P),
        (swap_d.at[0], S_SHORT), (swap_d.at[1], S_LONG), (gram_d.at[0:7], S_GS), (gram_x.at[0], S_GX),
        (gram_all.at[0, 0:7], S_GA), (gram_all.at[0], S_GC), (full.at[0:7], S_A), (full.at[0:8], S_AC),
        (sc1.at[0:7], S_S1), (sc2.at[0], S_S2), (sc3.at[0:7], S_S3),
    ):
        pltpu.make_async_copy(ref, ref, ssem.at[ss]).wait()
    for copy in outs:
        copy.wait()


def grad_kernel(whole, xs, wts, gg, gu, gd, out):
    full = whole[pl.ds(8 * pl.program_id(0), 8)]

    def rows(i):
        return jnp.concatenate(
            [full[:, i].reshape(8 * HB, 128), full[:, 3 + i].reshape(8 * HB, 128)], axis=1
        )

    out[...] = wts[...]
    gd[...] = nt(rows(0), xs[1]).astype(BF)
    gg[...] = nt(xs[0], rows(1)).astype(BF)
    gu[...] = nt(xs[0], rows(2)).astype(BF)


def body(train_x, train_cot, val_x, val_cot, w_gate, w_up, w_down, step_weights, example_ids, val_mask):
    hbm = pl.BlockSpec(memory_space=pltpu.HBM)
    free = pl.BlockSpec(memory_space=pl.ANY)
    vmem = pl.BlockSpec(memory_space=pltpu.VMEM)
    V = pltpu.VMEM
    full, xs, wts = pl.pallas_call(
        comm_kernel,
        out_shape=(
            jax.ShapeDtypeStruct((16, 6, HB, 128), BF),
            jax.ShapeDtypeStruct((2, W, TOK), BF),
            jax.ShapeDtypeStruct((1, EX), F32),
        ),
        in_specs=[hbm] * 10,
        out_specs=(free, free, vmem),
        scratch_shapes=[
            pltpu.SMEM((EX,), F32),
            V((1, TOK), jnp.int32),
            V((1, 32), jnp.int32),
            V((2, 4, W), BF),
            V((2, W, 1792), BF),
            V((2, NZ, 3, HB, W), BF),
            V((NZ, 3, HB, W), BF),
            V((80, W), BF),
            V((16, W), F32),
            V((NM, 80, W), BF),
            V((NM, 80, W), BF),
            V((3, 128, W), BF),
            V((3, 128, W), BF),
            V((NZ, 7, HB, 128), F32),
            V((6, HB, 128), BF),
            V((2, 4, 7, HB, 128), BF),
            V((2, 4, 7, HB, 128), BF),
            V((7, HB, 128), F32),
            V((2, 7, HB, 128), BF),
            V((NZ, 16, 128), F32),
            V((NZ, 16, 128), F32),
            V((2, 16, 128), F32),
            V((2, NZ, 16, 128), F32),
            V((NZ, EX, 128), F32),
            V((2, EX, 128), F32),
            V((NM, EX, 128), F32),
            V((2, W, TOK), F32),
            V((2, W, TOK), BF),
            pltpu.SemaphoreType.DMA((11,)),
            pltpu.SemaphoreType.DMA((19,)),
            pltpu.SemaphoreType.DMA((134,)),
            pltpu.SemaphoreType.DMA((2,)),
        ],
        compiler_params=pltpu.CompilerParams(
            collective_id=0, has_side_effects=True, vmem_limit_bytes=40 * 1024 * 1024
        ),
        name="reduce_and_gather",
    )(
        *[
            pltpu.with_memory_space_constraint(a, pltpu.HBM)
            for a in (
                train_x, train_cot, val_x, val_cot, w_gate, w_up, w_down.reshape(NZ, 2, HB, W),
                step_weights, example_ids.reshape(1, TOK), val_mask.reshape(1, 32),
            )
        ]
    )
    gg, gu, gd, out = pl.pallas_call(
        grad_kernel,
        grid=(2,),
        out_shape=(
            jax.ShapeDtypeStruct((W, 1792), BF),
            jax.ShapeDtypeStruct((W, 1792), BF),
            jax.ShapeDtypeStruct((1792, W), BF),
            jax.ShapeDtypeStruct((1, EX), F32),
        ),
        in_specs=[
            vmem,
            vmem,
            vmem,
        ],
        out_specs=(
            pl.BlockSpec((W, 8 * HB), lambda i: (0, i)),
            pl.BlockSpec((W, 8 * HB), lambda i: (0, i)),
            pl.BlockSpec((8 * HB, W), lambda i: (i, 0)),
            pl.BlockSpec((1, EX), lambda i: (0, 0)),
        ),
        compiler_params=pltpu.CompilerParams(vmem_limit_bytes=40 * 1024 * 1024),
        name="gradients",
    )(full, xs, wts)
    return gg, gu, gd, out.reshape(EX)


def solution(mesh):
    wide, tall = P("dp", "mp"), P("mp", "dp")
    return jax.shard_map(
        body,
        mesh=mesh,
        in_specs=(tall, tall, tall, tall, wide, wide, tall, P(), P(), P()),
        out_specs=(wide, wide, tall, P()),
        check_vma=False,
    )
```

```python
import jax
import jax.numpy as jnp
from jax import lax
from jax.experimental import pallas as pl
from jax.experimental.pallas import tpu as pltpu
from jax.sharding import PartitionSpec as P

MESH = pl.DeviceIdType.MESH
BF = jnp.bfloat16
F32 = jnp.float32

LEARN_RATE = 0.0003
NZ = 8
NM = 8
HB = 112
TOK = 256
W = 256
EX = 8


def nt(left, right):
    return lax.dot_general(left, right, (((1,), (1,)), ((), ())), preferred_element_type=F32)


def tn(left, right):
    return lax.dot_general(left, right, (((0,), (0,)), ((), ())), preferred_element_type=F32)


def comm_kernel(
    x_in, c_in, vx_in, vc_in, wg_in, wu_in, wd_in, sw_in, ids_in, mask_in,
    full, xs_out, wts_out,
    sw, ids, mask, vraw, wraw, wt, wo, pk, vstage, xb, xo, va, vo, part, own,
    ring_s, ring_d, swap_p, swap_d, gram_s, gram_d, gram_x, gram_all, sc1, sc2, sc3, xt, xs,
    lsem, ssem, rsem, hsem,
):
    d = lax.axis_index("dp")
    m = lax.axis_index("mp")
    z = d // 4
    xh = (d // 2) % 2
    c = d % 2
    slot = z * 2 + c

    def dev(zz, xx, cc):
        return (zz * 4 + xx * 2 + cc, m)

    def at(step):
        return (z + step + NZ) % NZ

    def zdev(step):
        return dev(at(step), xh, c)

    def mdev(step):
        return (d, (m + step) % NM)

    other = dev(z, xh, 1 - c)
    across = dev(z, 1 - xh, c)
    right, left = zdev(1), zdev(-1)

    def send(src, dst, ss, rs, to):
        pltpu.make_async_remote_copy(
            src_ref=src, dst_ref=dst, send_sem=ssem.at[ss], recv_sem=rsem.at[rs],
            device_id=to, device_id_type=MESH,
        ).start()

    def got(dst, rs):
        pltpu.make_async_copy(dst, dst, rsem.at[rs]).wait()

    R_X, R_XO, R_W, R_P, R_GS, R_GX, R_GA, R_GC, R_AC, R_S1, R_S2, R_S3 = 0, 8, 9, 11, 12, 13, 14, 15, 16, 17, 18, 19
    R_SHORT, R_LONG, R_RING, R_A, R_Y, R_YO = 20, 23, 26, 75, 117, 118

    (S_X, S_W, S_XO, S_RING, S_LAST, S_P, S_SHORT, S_LONG, S_GS, S_GX, S_GA, S_GC, S_A, S_AC, S_S1, S_S2, S_S3, S_Y, S_YO) = range(19)

    barrier = pltpu.get_barrier_semaphore()
    peers = [mdev(k) for k in range(1, NM)] + [across, other] + [zdev(k) for k in range(1, NZ)]
    for peer in peers:
        pl.semaphore_signal(barrier, inc=1, device_id=peer, device_id_type=MESH)

    loads = [
        pltpu.make_async_copy(x_in, pk.at[0:32], lsem.at[0]),
        pltpu.make_async_copy(c_in, pk.at[48:80], lsem.at[1]),
        pltpu.make_async_copy(wg_in, wraw.at[0], lsem.at[2]),
        pltpu.make_async_copy(wu_in, wraw.at[1], lsem.at[3]),
        pltpu.make_async_copy(vx_in, vraw.at[0], lsem.at[4]),
        pltpu.make_async_copy(vc_in, vraw.at[1], lsem.at[5]),
        pltpu.make_async_copy(wd_in.at[:, 0], wt.at[0, :, 2], lsem.at[6]),
        pltpu.make_async_copy(wd_in.at[:, 1], wt.at[1, :, 2], lsem.at[7]),
        pltpu.make_async_copy(sw_in, sw, lsem.at[8]),
        pltpu.make_async_copy(ids_in, ids, lsem.at[9]),
        pltpu.make_async_copy(mask_in, mask, lsem.at[10]),
    ]
    for copy in loads:
        copy.start()

    vstage[0:16] = jnp.zeros((16, W), F32)
    loads[4].wait()
    loads[5].wait()
    vstage[0:4] = vraw[0].astype(F32)
    vstage[4:8] = vraw[0].astype(F32)
    vstage[8:12] = vraw[1].astype(F32)
    pk[32:48] = vstage[0:16].astype(BF)
    loads[0].wait()
    loads[1].wait()
    xb[m] = pk[...]
    pl.semaphore_wait(barrier, len(peers))

    for k in (4, 3, 5, 2, 6, 1, 7):
        send(pk.at[0:48], xb.at[m, 0:48], S_X, R_X + m, mdev(k))
    send(pk.at[0:48], xo.at[m, 0:48], S_X, R_XO, other)
    for k in (4, 3, 5, 2, 6, 1, 7):
        send(pk.at[48:80], xb.at[m, 48:80], S_Y, R_Y, mdev(k))
    send(pk.at[48:80], xo.at[m, 48:80], S_Y, R_YO, other)

    for w in range(2):
        loads[2 + w].wait()
        for i in range(14):
            block = wraw[w, :, 128 * i : 128 * (i + 1)].T
            row = 128 * i
            while row < 128 * (i + 1):
                b = row // HB
                end = min(128 * (i + 1), (b + 1) * HB)
                wt[b % 2, b // 2, w, row - b * HB : end - b * HB] = block[row - 128 * i : end - 128 * i]
                row = end
    loads[6].wait()
    loads[7].wait()
    for step in (4, 3, 5, 2, 6, 1, 7, 0):
        send(wt.at[1 - c, at(step)], wo.at[at(step)], S_W, R_W if step == 4 else R_W + 1, other)

    for k in (1, 7, 2, 6, 3, 5, 4):
        j = (m + NM - k) % NM
        got(xb.at[j, 0:48], R_X + j)
        send(xb.at[j, 0:48], xo.at[j, 0:48], S_XO, R_XO, other)
    place = lax.broadcasted_iota(jnp.int32, (128, W), 0) % 16

    def spread(src, dst):
        rows = src[:, 32:48, :].reshape(128, W).astype(F32)
        for i in range(3):
            keep = jnp.logical_and(place >= 4 * i, place < 4 * i + 4)
            dst[i] = jnp.where(keep, rows, 0.0).astype(BF)

    def tokens(ref, first):
        return ref[:, 48 * first : 48 * first + 32, :].reshape(TOK, W)

    def own_width(i):
        lhs = wt[c, :, i].reshape(NZ * HB, W)
        total = nt(lhs, tokens(xb, 1 if i == 2 else 0))
        part[:, i] = total[:, :128].reshape(NZ, HB, 128)
        part[:, 4 + i] = total[:, 128:].reshape(NZ, HB, 128)

    own_width(0)
    own_width(1)
    got(xb.at[0:7, 48:80], R_Y)
    for k in (1, 7, 2, 6, 3, 5, 4):
        j = (m + NM - k) % NM
        send(xb.at[j, 48:80], xo.at[j, 48:80], S_YO, R_YO, other)
    got(xo.at[:, 0:48], R_XO)

    A, B = (0, 1, 2, 3), (4, 5, 6)
    RIGHT, LEFT = 0, 1
    to_dev = (right, left)

    def ring_sem(way, s, slab):
        if s < 3:
            return R_RING + (way * 3 + s) * 7 + slab
        return R_RING + 42 + slab

    def ring(way, s, slab, value):
        ring_s[way, s, slab] = value.astype(BF)
        send(
            ring_s.at[way, s, slab], ring_d.at[way, s, slab],
            S_LAST if s == 3 else S_RING, ring_sem(way, s, slab), to_dev[way],
        )

    def first(way, slab, value):
        ring(way, 0, slab, value)

    def arrived(way, s, slab):
        got(ring_d.at[way, s - 1, slab], ring_sem(way, s - 1, slab))

    def onward(way, s, slab, step):
        arrived(way, s, slab)
        ring(way, s, slab, part[at(step), slab] + ring_d[way, s - 1, slab].astype(F32))

    far = at(4)
    got(wo.at[far], R_W)
    for i in range(3):
        if i == 2:
            own_width(2)
            got(xo.at[:, 48:80], R_YO)
        total = nt(wo[far, i], tokens(xo, 1 if i == 2 else 0))
        first(RIGHT, i, part[far, i] + total[:, :128])
        first(LEFT, 4 + i, part[far, 4 + i] + total[:, 128:])
    spread(xb, va)
    spread(xo, vo)
    val = jnp.zeros((HB, 128), F32)
    for i in range(3):
        val = val + nt(wt[c, far, i], va[i]) + nt(wo[far, i], vo[i])
    first(RIGHT, 3, val)

    got(wo.at[0:7], R_W + 1)
    val = jnp.zeros((NZ * HB, 128), F32)
    for i in range(3):
        lhs = wo[:, i].reshape(NZ * HB, W)
        total = nt(lhs, tokens(xo, 1 if i == 2 else 0))
        part[:, i] = part[:, i] + total[:, :128].reshape(NZ, HB, 128)
        part[:, 4 + i] = part[:, 4 + i] + total[:, 128:].reshape(NZ, HB, 128)
        first(LEFT, i, part[at(-3), i])
        first(RIGHT, 4 + i, part[at(3), 4 + i])
        val = val + nt(lhs, vo[i]) + nt(wt[c, :, i].reshape(NZ * HB, W), va[i])
    part[:, 3] = val.reshape(NZ, HB, 128)
    first(LEFT, 3, part[at(-3), 3])
    send(part.at[z], swap_p, S_P, R_P, across)

    def both_long(s):
        for i in range(3):
            onward(RIGHT, s, A[i], 4 - s)
            onward(LEFT, s, B[i], s - 4)

    def both_short(s):
        for i in range(3):
            onward(RIGHT, s, B[i], 3 - s)
            onward(LEFT, s, A[i], s - 3)
        onward(RIGHT, s, 3, 4 - s)
        onward(LEFT, s, 3, s - 3)

    def half(ref, which):
        return ref[pl.ds(4 * c, 4), 48 * which : 48 * which + 32, :].reshape(128, W)

    gram = nt(va[0], half(xb, 0)) + nt(vo[0], half(xo, 0)) + nt(va[2], half(xb, 1)) + nt(vo[2], half(xo, 1))
    gram_s[...] = gram.reshape(NZ, 16, 128)
    gram_d[z] = gram_s[z]
    for k in range(1, NZ):
        send(gram_s.at[at(k)], gram_d.at[z], S_GS, R_GS, zdev(k))

    both_long(1)
    both_short(1)
    for copy in loads[8:]:
        copy.wait()
    both_long(2)
    both_short(2)
    got(gram_d.at[0:7], R_GS)
    gram_x[0] = jnp.sum(gram_d[...], axis=0)
    send(gram_x.at[0], gram_x.at[1], S_GX, R_GX, across)
    both_long(3)

    def pass_on(way, s, slab, dst, ss, rs):
        arrived(way, s, slab)
        send(ring_d.at[way, s - 1, slab], swap_d.at[dst, slab], ss, rs + (0, 0, 0, 1, 2, 2, 2)[slab], across)

    for i in range(3):
        pass_on(LEFT, 3, A[i], 0, S_SHORT, R_SHORT)
    for i in range(3):
        pass_on(RIGHT, 3, B[i], 0, S_SHORT, R_SHORT)
    onward(RIGHT, 3, 3, 1)
    pass_on(LEFT, 3, 3, 0, S_SHORT, R_SHORT)
    r_row = jnp.zeros((1, TOK), F32)
    for e in range(EX):
        r_row = r_row + jnp.where(ids[...] == e, sw[e], 0.0)
    for i in range(2):
        xt[i] = tokens(xb, i).T.astype(F32)
    got(gram_x.at[1], R_GX)
    gram_all[c, z] = gram_x[0] + gram_x[1]
    for k in range(1, NZ):
        send(gram_all.at[c, z], gram_all.at[c, z], S_GA, R_GA, zdev(k))
    got(swap_p, R_P)
    for i in range(3):
        pass_on(RIGHT, 4, A[i], 1, S_LONG, R_LONG)
    for i in range(3):
        pass_on(LEFT, 4, B[i], 1, S_LONG, R_LONG)
    pass_on(RIGHT, 4, 3, 1, S_LONG, R_LONG)
    got(gram_all.at[c, 0:7], R_GA)
    send(gram_all.at[c], gram_all.at[c], S_GC, R_GC, other)

    def passed(group, slab, count):
        got(swap_d.at[0, slab : slab + count], R_SHORT + group)
        got(swap_d.at[1, slab : slab + count], R_LONG + group)

    def whole(slab):
        way = RIGHT if slab < 4 else LEFT
        mine_ = part[z, slab] + ring_d[1 - way, 2, slab].astype(F32) + ring_d[way, 3, slab].astype(F32)
        theirs = swap_p[slab] + swap_d[0, slab].astype(F32) + swap_d[1, slab].astype(F32)
        return mine_ + theirs

    def block_terms(gate, up, back):
        sig = 1.0 / (1.0 + jnp.exp(-gate))
        act = gate * sig
        return act * up, back * up * sig * (1.0 + gate * (1.0 - sig)), back * act

    def gather_sem(way, step, slab):
        if step < 4:
            return R_A + (way * 3 + step - 1) * 6 + slab
        return R_A + 36 + slab

    def gather(src, block, way, step, slab):
        send(src, full.at[block, slab], S_A, gather_sem(way, step, slab), to_dev[way])

    for h in range(2):
        passed(2 * h, 4 * h, 3)
        terms = block_terms(*[whole(4 * h + i) for i in range(3)])
        for i in range(3):
            own[3 * h + i] = terms[i].astype(BF)
            gather(own.at[3 * h + i], slot, RIGHT, 1, 3 * h + i)
            gather(own.at[3 * h + i], slot, LEFT, 1, 3 * h + i)
    send(own, full.at[slot], S_AC, R_AC, other)
    outs = [pltpu.make_async_copy(own, full.at[slot], hsem.at[0])]
    outs[0].start()

    def step_of_gather(step):
        blocks = [2 * at(-step) + c, 2 * at(step) + c]
        order = (0, 3, 1, 4, 2, 5) if step == 4 else range(6)
        for i in order:
            for way in (RIGHT, LEFT):
                if step == 4 and i // 3 != way:
                    continue
                got(full.at[blocks[way], i], gather_sem(way, step, i))
                if step < 3 or (step == 3 and i // 3 == way):
                    gather(full.at[blocks[way], i], blocks[way], way, step + 1, i)
                if step == 4:
                    send(full.at[blocks[way], i], full.at[blocks[way], i], S_AC, R_AC, other)
        if step < 4:
            for way in (RIGHT, LEFT):
                send(full.at[blocks[way]], full.at[blocks[way]], S_AC, R_AC, other)

    got(gram_all.at[1 - c], R_GC)
    kt = jnp.concatenate([gram_all[0].reshape(128, 128), gram_all[1].reshape(128, 128)], axis=1)
    rk = (kt * r_row).astype(BF)
    hb, dgb, dub = [jnp.concatenate([own[i], own[3 + i]], axis=1) for i in range(3)]
    passed(1, 3, 1)
    val = whole(3)
    v_gate = val - LEARN_RATE * nt(dgb, rk)
    v_up = pltpu.roll(val, 124, 1) - LEARN_RATE * nt(dub, rk)
    v_back = pltpu.roll(val - LEARN_RATE * nt(hb, rk), 120, 1)
    lane = lax.broadcasted_iota(jnp.int32, (32, 128), 1)
    row = lax.broadcasted_iota(jnp.int32, (32, 128), 0)
    pick = jnp.logical_and(lane % 16 < 4, (lane // 16) * 4 + lane % 16 == row)
    mask_f = jnp.broadcast_to(mask[...].astype(F32), (16, 32)).astype(BF)
    mask_l = lax.dot_general(
        mask_f, jnp.where(pick, 1.0, 0.0).astype(BF), (((1,), (0,)), ((), ())), preferred_element_type=F32
    )[0:1]
    keep = jnp.broadcast_to(mask_l, (HB, 128)) > 0.5
    v_hid, v_dg, v_du = [jnp.where(keep, t, 0.0) for t in block_terms(v_gate, v_up, v_back)]
    inner = tn(v_dg.astype(BF), dgb) + tn(v_du.astype(BF), dub) + tn(pltpu.roll(v_hid, 8, 1).astype(BF), hb)
    token = jnp.sum(inner * kt, axis=0, keepdims=True)
    label = lax.broadcasted_iota(jnp.int32, (EX, TOK), 0)
    score = jnp.sum(jnp.where(ids[...] == label, token, 0.0), axis=1, keepdims=True)
    sc1[z] = jnp.broadcast_to(score, (EX, 128))
    for k in range(1, NZ):
        send(sc1.at[z], sc1.at[z], S_S1, R_S1, zdev(k))

    step_of_gather(1)
    step_of_gather(2)
    got(sc1.at[0:7], R_S1)
    sc2[c] = jnp.sum(sc1[...], axis=0)
    send(sc2.at[c], sc2.at[c], S_S2, R_S2, other)
    got(sc2.at[1 - c], R_S2)
    sc3[m] = sc2[0] + sc2[1]
    for k in range(1, NM):
        send(sc3.at[m], sc3.at[m], S_S3, R_S3, mdev(k))

    step_of_gather(3)
    got(sc3.at[0:7], R_S3)
    score = jnp.sum(sc3[...], axis=0)
    rms = jnp.sqrt(jnp.mean(score * score, axis=0, keepdims=True) + 1e-6)
    arg = score / (4.0 * rms)
    soft = jnp.maximum(arg, 0.0) + jnp.log(1.0 + jnp.exp(-jnp.abs(arg)))
    weights = EX * soft / jnp.sum(soft, axis=0, keepdims=True)
    diag = lax.broadcasted_iota(jnp.int32, (EX, 128), 0) == lax.broadcasted_iota(jnp.int32, (EX, 128), 1)
    wts_out[...] = jnp.sum(jnp.where(diag, weights, 0.0), axis=0, keepdims=True)[:, :EX]
    e_row = jnp.zeros((1, TOK), F32)
    for e in range(EX):
        e_row = e_row + jnp.where(ids[...] == e, weights[e : e + 1, 0:1], 0.0)
    for i in range(2):
        xs[i] = (xt[i] * e_row).astype(BF)
    copy = pltpu.make_async_copy(xs, xs_out, hsem.at[1])
    copy.start()
    outs.append(copy)

    step_of_gather(4)
    got(full.at[0:8], R_AC)
    for ref, ss in (
        (xb.at[:, 0:48], S_X), (xb.at[:, 48:80], S_Y), (wo, S_W), (xb.at[0:7, 0:48], S_XO), (xb.at[0:7, 48:80], S_YO), (ring_s.at[:, 0:3], S_RING), (swap_d.at[0], S_LAST), (swap_p, S_P),
        (swap_d.at[0], S_SHORT), (swap_d.at[1], S_LONG), (gram_d.at[0:7], S_GS), (gram_x.at[0], S_GX),
        (gram_all.at[0, 0:7], S_GA), (gram_all.at[0], S_GC), (full.at[0:7], S_A), (full.at[0:8], S_AC),
        (sc1.at[0:7], S_S1), (sc2.at[0], S_S2), (sc3.at[0:7], S_S3),
    ):
        pltpu.make_async_copy(ref, ref, ssem.at[ss]).wait()
    for copy in outs:
        copy.wait()


def grad_kernel(whole, xs, wts, gg, gu, gd, out):
    full = whole[pl.ds(8 * pl.program_id(0), 8)]

    def rows(i):
        return jnp.concatenate(
            [full[:, i].reshape(8 * HB, 128), full[:, 3 + i].reshape(8 * HB, 128)], axis=1
        )

    out[...] = wts[...]
    gd[...] = nt(rows(0), xs[1]).astype(BF)
    gg[...] = nt(xs[0], rows(1)).astype(BF)
    gu[...] = nt(xs[0], rows(2)).astype(BF)


def body(train_x, train_cot, val_x, val_cot, w_gate, w_up, w_down, step_weights, example_ids, val_mask):
    hbm = pl.BlockSpec(memory_space=pltpu.HBM)
    free = pl.BlockSpec(memory_space=pl.ANY)
    vmem = pl.BlockSpec(memory_space=pltpu.VMEM)
    V = pltpu.VMEM
    full, xs, wts = pl.pallas_call(
        comm_kernel,
        out_shape=(
            jax.ShapeDtypeStruct((16, 6, HB, 128), BF),
            jax.ShapeDtypeStruct((2, W, TOK), BF),
            jax.ShapeDtypeStruct((1, EX), F32),
        ),
        in_specs=[hbm] * 10,
        out_specs=(free, free, vmem),
        scratch_shapes=[
            pltpu.SMEM((EX,), F32),
            V((1, TOK), jnp.int32),
            V((1, 32), jnp.int32),
            V((2, 4, W), BF),
            V((2, W, 1792), BF),
            V((2, NZ, 3, HB, W), BF),
            V((NZ, 3, HB, W), BF),
            V((80, W), BF),
            V((16, W), F32),
            V((NM, 80, W), BF),
            V((NM, 80, W), BF),
            V((3, 128, W), BF),
            V((3, 128, W), BF),
            V((NZ, 7, HB, 128), F32),
            V((6, HB, 128), BF),
            V((2, 4, 7, HB, 128), BF),
            V((2, 4, 7, HB, 128), BF),
            V((7, HB, 128), F32),
            V((2, 7, HB, 128), BF),
            V((NZ, 16, 128), F32),
            V((NZ, 16, 128), F32),
            V((2, 16, 128), F32),
            V((2, NZ, 16, 128), F32),
            V((NZ, EX, 128), F32),
            V((2, EX, 128), F32),
            V((NM, EX, 128), F32),
            V((2, W, TOK), F32),
            V((2, W, TOK), BF),
            pltpu.SemaphoreType.DMA((11,)),
            pltpu.SemaphoreType.DMA((19,)),
            pltpu.SemaphoreType.DMA((119,)),
            pltpu.SemaphoreType.DMA((2,)),
        ],
        compiler_params=pltpu.CompilerParams(
            collective_id=0, has_side_effects=True, vmem_limit_bytes=40 * 1024 * 1024
        ),
        name="reduce_and_gather",
    )(
        *[
            pltpu.with_memory_space_constraint(a, pltpu.HBM)
            for a in (
                train_x, train_cot, val_x, val_cot, w_gate, w_up, w_down.reshape(NZ, 2, HB, W),
                step_weights, example_ids.reshape(1, TOK), val_mask.reshape(1, 32),
            )
        ]
    )
    gg, gu, gd, out = pl.pallas_call(
        grad_kernel,
        grid=(2,),
        out_shape=(
            jax.ShapeDtypeStruct((W, 1792), BF),
            jax.ShapeDtypeStruct((W, 1792), BF),
            jax.ShapeDtypeStruct((1792, W), BF),
            jax.ShapeDtypeStruct((1, EX), F32),
        ),
        in_specs=[
            vmem,
            vmem,
            vmem,
        ],
        out_specs=(
            pl.BlockSpec((W, 8 * HB), lambda i: (0, i)),
            pl.BlockSpec((W, 8 * HB), lambda i: (0, i)),
            pl.BlockSpec((8 * HB, W), lambda i: (i, 0)),
            pl.BlockSpec((1, EX), lambda i: (0, 0)),
        ),
        compiler_params=pltpu.CompilerParams(vmem_limit_bytes=40 * 1024 * 1024),
        name="gradients",
    )(full, xs, wts)
    return gg, gu, gd, out.reshape(EX)


def solution(mesh):
    wide, tall = P("dp", "mp"), P("mp", "dp")
    return jax.shard_map(
        body,
        mesh=mesh,
        in_specs=(tall, tall, tall, tall, wide, wide, tall, P(), P(), P()),
        out_specs=(wide, wide, tall, P()),
        check_vma=False,
    )
```

```python
import jax
import jax.numpy as jnp
from jax import lax
from jax.experimental import pallas as pl
from jax.experimental.pallas import tpu as pltpu
from jax.sharding import PartitionSpec as P

MESH = pl.DeviceIdType.MESH
BF = jnp.bfloat16
F32 = jnp.float32

LEARN_RATE = 0.0003
NZ = 8
NM = 8
HB = 112
TOK = 256
W = 256
EX = 8


def nt(left, right):
    return lax.dot_general(left, right, (((1,), (1,)), ((), ())), preferred_element_type=F32)


def tn(left, right):
    return lax.dot_general(left, right, (((0,), (0,)), ((), ())), preferred_element_type=F32)


def comm_kernel(
    x_in, c_in, vx_in, vc_in, wg_in, wu_in, wd_in, sw_in, ids_in, mask_in,
    full, xs_out, wts_out,
    sw, ids, mask, vraw, wraw, wt, wo, pk, vstage, xb, xo, va, vo, part, own,
    ring_s, ring_d, swap_p, swap_d, gram_s, gram_d, gram_x, gram_all, sc1, sc2, sc3, xt, xs,
    lsem, ssem, rsem, hsem,
):
    d = lax.axis_index("dp")
    m = lax.axis_index("mp")
    z = d // 4
    xh = (d // 2) % 2
    c = d % 2
    slot = z * 2 + c

    def dev(zz, xx, cc):
        return (zz * 4 + xx * 2 + cc, m)

    def at(step):
        return (z + step + NZ) % NZ

    def zdev(step):
        return dev(at(step), xh, c)

    def mdev(step):
        return (d, (m + step) % NM)

    other = dev(z, xh, 1 - c)
    across = dev(z, 1 - xh, c)
    right, left = zdev(1), zdev(-1)

    def send(src, dst, ss, rs, to):
        pltpu.make_async_remote_copy(
            src_ref=src, dst_ref=dst, send_sem=ssem.at[ss], recv_sem=rsem.at[rs],
            device_id=to, device_id_type=MESH,
        ).start()

    def got(dst, rs):
        pltpu.make_async_copy(dst, dst, rsem.at[rs]).wait()

    R_X, R_XO, R_W, R_P, R_GS, R_GX, R_GA, R_GC, R_AC, R_S1, R_S2, R_S3 = 0, 8, 9, 11, 12, 13, 14, 15, 16, 17, 18, 19
    R_SHORT, R_LONG, R_RING, R_A, R_Y, R_YO = 20, 23, 26, 75, 93, 94

    (S_X, S_W, S_XO, S_RING, S_LAST, S_P, S_SHORT, S_LONG, S_GS, S_GX, S_GA, S_GC, S_A, S_AC, S_S1, S_S2, S_S3, S_Y, S_YO) = range(19)

    barrier = pltpu.get_barrier_semaphore()
    peers = [mdev(k) for k in range(1, NM)] + [across, other] + [zdev(k) for k in range(1, NZ)]
    for peer in peers:
        pl.semaphore_signal(barrier, inc=1, device_id=peer, device_id_type=MESH)

    loads = [
        pltpu.make_async_copy(x_in, pk.at[0:32], lsem.at[0]),
        pltpu.make_async_copy(c_in, pk.at[48:80], lsem.at[1]),
        pltpu.make_async_copy(wg_in, wraw.at[0], lsem.at[2]),
        pltpu.make_async_copy(wu_in, wraw.at[1], lsem.at[3]),
        pltpu.make_async_copy(vx_in, vraw.at[0], lsem.at[4]),
        pltpu.make_async_copy(vc_in, vraw.at[1], lsem.at[5]),
        pltpu.make_async_copy(wd_in.at[:, 0], wt.at[0, :, 2], lsem.at[6]),
        pltpu.make_async_copy(wd_in.at[:, 1], wt.at[1, :, 2], lsem.at[7]),
        pltpu.make_async_copy(sw_in, sw, lsem.at[8]),
        pltpu.make_async_copy(ids_in, ids, lsem.at[9]),
        pltpu.make_async_copy(mask_in, mask, lsem.at[10]),
    ]
    for copy in loads:
        copy.start()

    vstage[0:16] = jnp.zeros((16, W), F32)
    loads[4].wait()
    loads[5].wait()
    vstage[0:4] = vraw[0].astype(F32)
    vstage[4:8] = vraw[0].astype(F32)
    vstage[8:12] = vraw[1].astype(F32)
    pk[32:48] = vstage[0:16].astype(BF)
    loads[0].wait()
    loads[1].wait()
    xb[m] = pk[...]
    pl.semaphore_wait(barrier, len(peers))

    for k in (4, 3, 5, 2, 6, 1, 7):
        send(pk.at[0:48], xb.at[m, 0:48], S_X, R_X + m, mdev(k))
    send(pk.at[0:48], xo.at[m, 0:48], S_X, R_XO, other)
    for k in (4, 3, 5, 2, 6, 1, 7):
        send(pk.at[48:80], xb.at[m, 48:80], S_Y, R_Y, mdev(k))
    send(pk.at[48:80], xo.at[m, 48:80], S_Y, R_YO, other)

    for w in range(2):
        loads[2 + w].wait()
        for i in range(14):
            block = wraw[w, :, 128 * i : 128 * (i + 1)].T
            row = 128 * i
            while row < 128 * (i + 1):
                b = row // HB
                end = min(128 * (i + 1), (b + 1) * HB)
                wt[b % 2, b // 2, w, row - b * HB : end - b * HB] = block[row - 128 * i : end - 128 * i]
                row = end
    loads[6].wait()
    loads[7].wait()
    for step in (4, 3, 5, 2, 6, 1, 7, 0):
        send(wt.at[1 - c, at(step)], wo.at[at(step)], S_W, R_W if step == 4 else R_W + 1, other)

    for k in (1, 7, 2, 6, 3, 5, 4):
        j = (m + NM - k) % NM
        got(xb.at[j, 0:48], R_X + j)
        send(xb.at[j, 0:48], xo.at[j, 0:48], S_XO, R_XO, other)
    place = lax.broadcasted_iota(jnp.int32, (128, W), 0) % 16

    def spread(src, dst):
        rows = src[:, 32:48, :].reshape(128, W).astype(F32)
        for i in range(3):
            keep = jnp.logical_and(place >= 4 * i, place < 4 * i + 4)
            dst[i] = jnp.where(keep, rows, 0.0).astype(BF)

    def tokens(ref, first):
        return ref[:, 48 * first : 48 * first + 32, :].reshape(TOK, W)

    def own_width(i):
        lhs = wt[c, :, i].reshape(NZ * HB, W)
        total = nt(lhs, tokens(xb, 1 if i == 2 else 0))
        part[:, i] = total[:, :128].reshape(NZ, HB, 128)
        part[:, 4 + i] = total[:, 128:].reshape(NZ, HB, 128)

    own_width(0)
    own_width(1)
    got(xb.at[0:7, 48:80], R_Y)
    for k in (1, 7, 2, 6, 3, 5, 4):
        j = (m + NM - k) % NM
        send(xb.at[j, 48:80], xo.at[j, 48:80], S_YO, R_YO, other)
    got(xo.at[:, 0:48], R_XO)

    A, B = (0, 1, 2, 3), (4, 5, 6)
    RIGHT, LEFT = 0, 1
    to_dev = (right, left)

    def ring_sem(way, s, slab):
        if s < 3:
            return R_RING + (way * 3 + s) * 7 + slab
        return R_RING + 42 + slab

    def ring(way, s, slab, value):
        ring_s[way, s, slab] = value.astype(BF)
        send(
            ring_s.at[way, s, slab], ring_d.at[way, s, slab],
            S_LAST if s == 3 else S_RING, ring_sem(way, s, slab), to_dev[way],
        )

    def first(way, slab, value):
        ring(way, 0, slab, value)

    def arrived(way, s, slab):
        got(ring_d.at[way, s - 1, slab], ring_sem(way, s - 1, slab))

    def onward(way, s, slab, step):
        arrived(way, s, slab)
        ring(way, s, slab, part[at(step), slab] + ring_d[way, s - 1, slab].astype(F32))

    far = at(4)
    got(wo.at[far], R_W)
    for i in range(3):
        if i == 2:
            own_width(2)
            got(xo.at[:, 48:80], R_YO)
        total = nt(wo[far, i], tokens(xo, 1 if i == 2 else 0))
        first(RIGHT, i, part[far, i] + total[:, :128])
        first(LEFT, 4 + i, part[far, 4 + i] + total[:, 128:])
    spread(xb, va)
    spread(xo, vo)
    val = jnp.zeros((HB, 128), F32)
    for i in range(3):
        val = val + nt(wt[c, far, i], va[i]) + nt(wo[far, i], vo[i])
    first(RIGHT, 3, val)

    got(wo.at[0:7], R_W + 1)
    val = jnp.zeros((NZ * HB, 128), F32)
    for i in range(3):
        lhs = wo[:, i].reshape(NZ * HB, W)
        total = nt(lhs, tokens(xo, 1 if i == 2 else 0))
        part[:, i] = part[:, i] + total[:, :128].reshape(NZ, HB, 128)
        part[:, 4 + i] = part[:, 4 + i] + total[:, 128:].reshape(NZ, HB, 128)
        first(LEFT, i, part[at(-3), i])
        first(RIGHT, 4 + i, part[at(3), 4 + i])
        val = val + nt(lhs, vo[i]) + nt(wt[c, :, i].reshape(NZ * HB, W), va[i])
    part[:, 3] = val.reshape(NZ, HB, 128)
    first(LEFT, 3, part[at(-3), 3])
    send(part.at[z], swap_p, S_P, R_P, across)

    def both_long(s):
        for i in range(3):
            onward(RIGHT, s, A[i], 4 - s)
            onward(LEFT, s, B[i], s - 4)

    def both_short(s):
        for i in range(3):
            onward(RIGHT, s, B[i], 3 - s)
            onward(LEFT, s, A[i], s - 3)
        onward(RIGHT, s, 3, 4 - s)
        onward(LEFT, s, 3, s - 3)

    def half(ref, which):
        return ref[pl.ds(4 * c, 4), 48 * which : 48 * which + 32, :].reshape(128, W)

    gram = nt(va[0], half(xb, 0)) + nt(vo[0], half(xo, 0)) + nt(va[2], half(xb, 1)) + nt(vo[2], half(xo, 1))
    gram_s[...] = gram.reshape(NZ, 16, 128)
    gram_d[z] = gram_s[z]
    for k in range(1, NZ):
        send(gram_s.at[at(k)], gram_d.at[z], S_GS, R_GS, zdev(k))

    both_long(1)
    both_short(1)
    for copy in loads[8:]:
        copy.wait()
    both_long(2)
    both_short(2)
    got(gram_d.at[0:7], R_GS)
    gram_x[0] = jnp.sum(gram_d[...], axis=0)
    send(gram_x.at[0], gram_x.at[1], S_GX, R_GX, across)
    both_long(3)

    def pass_on(way, s, slab, dst, ss, rs):
        arrived(way, s, slab)
        send(ring_d.at[way, s - 1, slab], swap_d.at[dst, slab], ss, rs + (0, 0, 0, 1, 2, 2, 2)[slab], across)

    for i in range(3):
        pass_on(LEFT, 3, A[i], 0, S_SHORT, R_SHORT)
    for i in range(3):
        pass_on(RIGHT, 3, B[i], 0, S_SHORT, R_SHORT)
    onward(RIGHT, 3, 3, 1)
    pass_on(LEFT, 3, 3, 0, S_SHORT, R_SHORT)
    r_row = jnp.zeros((1, TOK), F32)
    for e in range(EX):
        r_row = r_row + jnp.where(ids[...] == e, sw[e], 0.0)
    for i in range(2):
        xt[i] = tokens(xb, i).T.astype(F32)
    got(gram_x.at[1], R_GX)
    gram_all[c, z] = gram_x[0] + gram_x[1]
    for k in range(1, NZ):
        send(gram_all.at[c, z], gram_all.at[c, z], S_GA, R_GA, zdev(k))
    got(swap_p, R_P)
    for i in range(3):
        pass_on(RIGHT, 4, A[i], 1, S_LONG, R_LONG)
    for i in range(3):
        pass_on(LEFT, 4, B[i], 1, S_LONG, R_LONG)
    pass_on(RIGHT, 4, 3, 1, S_LONG, R_LONG)
    got(gram_all.at[c, 0:7], R_GA)
    send(gram_all.at[c], gram_all.at[c], S_GC, R_GC, other)

    def passed(group, slab, count):
        got(swap_d.at[0, slab : slab + count], R_SHORT + group)
        got(swap_d.at[1, slab : slab + count], R_LONG + group)

    def whole(slab):
        way = RIGHT if slab < 4 else LEFT
        mine_ = part[z, slab] + ring_d[1 - way, 2, slab].astype(F32) + ring_d[way, 3, slab].astype(F32)
        theirs = swap_p[slab] + swap_d[0, slab].astype(F32) + swap_d[1, slab].astype(F32)
        return mine_ + theirs

    def block_terms(gate, up, back):
        sig = 1.0 / (1.0 + jnp.exp(-gate))
        act = gate * sig
        return act * up, back * up * sig * (1.0 + gate * (1.0 - sig)), back * act

    def gather_sem(way, step, slab):
        if step < 3:
            return ring_sem(way, step - 1, slab)
        return R_A + (way * 6 + slab if step == 3 else 12 + slab)

    def gather(src, block, way, step, slab):
        send(src, full.at[block, slab], S_A, gather_sem(way, step, slab), to_dev[way])

    for h in range(2):
        passed(2 * h, 4 * h, 3)
        terms = block_terms(*[whole(4 * h + i) for i in range(3)])
        for i in range(3):
            own[3 * h + i] = terms[i].astype(BF)
            gather(own.at[3 * h + i], slot, RIGHT, 1, 3 * h + i)
            gather(own.at[3 * h + i], slot, LEFT, 1, 3 * h + i)
    send(own, full.at[slot], S_AC, R_AC, other)
    outs = [pltpu.make_async_copy(own, full.at[slot], hsem.at[0])]
    outs[0].start()

    def step_of_gather(step):
        blocks = [2 * at(-step) + c, 2 * at(step) + c]
        order = (0, 3, 1, 4, 2, 5) if step == 4 else range(6)
        for i in order:
            for way in (RIGHT, LEFT):
                if step == 4 and i // 3 != way:
                    continue
                got(full.at[blocks[way], i], gather_sem(way, step, i))
                if step < 3 or (step == 3 and i // 3 == way):
                    gather(full.at[blocks[way], i], blocks[way], way, step + 1, i)
                if step == 4:
                    send(full.at[blocks[way], i], full.at[blocks[way], i], S_AC, R_AC, other)
        if step < 4:
            for way in (RIGHT, LEFT):
                send(full.at[blocks[way]], full.at[blocks[way]], S_AC, R_AC, other)

    got(gram_all.at[1 - c], R_GC)
    kt = jnp.concatenate([gram_all[0].reshape(128, 128), gram_all[1].reshape(128, 128)], axis=1)
    rk = (kt * r_row).astype(BF)
    hb, dgb, dub = [jnp.concatenate([own[i], own[3 + i]], axis=1) for i in range(3)]
    passed(1, 3, 1)
    val = whole(3)
    v_gate = val - LEARN_RATE * nt(dgb, rk)
    v_up = pltpu.roll(val, 124, 1) - LEARN_RATE * nt(dub, rk)
    v_back = pltpu.roll(val - LEARN_RATE * nt(hb, rk), 120, 1)
    lane = lax.broadcasted_iota(jnp.int32, (32, 128), 1)
    row = lax.broadcasted_iota(jnp.int32, (32, 128), 0)
    pick = jnp.logical_and(lane % 16 < 4, (lane // 16) * 4 + lane % 16 == row)
    mask_f = jnp.broadcast_to(mask[...].astype(F32), (16, 32)).astype(BF)
    mask_l = lax.dot_general(
        mask_f, jnp.where(pick, 1.0, 0.0).astype(BF), (((1,), (0,)), ((), ())), preferred_element_type=F32
    )[0:1]
    keep = jnp.broadcast_to(mask_l, (HB, 128)) > 0.5
    v_hid, v_dg, v_du = [jnp.where(keep, t, 0.0) for t in block_terms(v_gate, v_up, v_back)]
    inner = tn(v_dg.astype(BF), dgb) + tn(v_du.astype(BF), dub) + tn(pltpu.roll(v_hid, 8, 1).astype(BF), hb)
    token = jnp.sum(inner * kt, axis=0, keepdims=True)
    label = lax.broadcasted_iota(jnp.int32, (EX, TOK), 0)
    score = jnp.sum(jnp.where(ids[...] == label, token, 0.0), axis=1, keepdims=True)
    sc1[z] = jnp.broadcast_to(score, (EX, 128))
    for k in range(1, NZ):
        send(sc1.at[z], sc1.at[z], S_S1, R_S1, zdev(k))

    step_of_gather(1)
    step_of_gather(2)
    got(sc1.at[0:7], R_S1)
    sc2[c] = jnp.sum(sc1[...], axis=0)
    send(sc2.at[c], sc2.at[c], S_S2, R_S2, other)
    got(sc2.at[1 - c], R_S2)
    sc3[m] = sc2[0] + sc2[1]
    for k in range(1, NM):
        send(sc3.at[m], sc3.at[m], S_S3, R_S3, mdev(k))

    step_of_gather(3)
    got(sc3.at[0:7], R_S3)
    score = jnp.sum(sc3[...], axis=0)
    rms = jnp.sqrt(jnp.mean(score * score, axis=0, keepdims=True) + 1e-6)
    arg = score / (4.0 * rms)
    soft = jnp.maximum(arg, 0.0) + jnp.log(1.0 + jnp.exp(-jnp.abs(arg)))
    weights = EX * soft / jnp.sum(soft, axis=0, keepdims=True)
    diag = lax.broadcasted_iota(jnp.int32, (EX, 128), 0) == lax.broadcasted_iota(jnp.int32, (EX, 128), 1)
    wts_out[...] = jnp.sum(jnp.where(diag, weights, 0.0), axis=0, keepdims=True)[:, :EX]
    e_row = jnp.zeros((1, TOK), F32)
    for e in range(EX):
        e_row = e_row + jnp.where(ids[...] == e, weights[e : e + 1, 0:1], 0.0)
    for i in range(2):
        xs[i] = (xt[i] * e_row).astype(BF)
    copy = pltpu.make_async_copy(xs, xs_out, hsem.at[1])
    copy.start()
    outs.append(copy)

    step_of_gather(4)
    got(full.at[0:8], R_AC)
    for ref, ss in (
        (xb.at[:, 0:48], S_X), (xb.at[:, 48:80], S_Y), (wo, S_W), (xb.at[0:7, 0:48], S_XO), (xb.at[0:7, 48:80], S_YO), (ring_s.at[:, 0:3], S_RING), (swap_d.at[0], S_LAST), (swap_p, S_P),
        (swap_d.at[0], S_SHORT), (swap_d.at[1], S_LONG), (gram_d.at[0:7], S_GS), (gram_x.at[0], S_GX),
        (gram_all.at[0, 0:7], S_GA), (gram_all.at[0], S_GC), (full.at[0:7], S_A), (full.at[0:8], S_AC),
        (sc1.at[0:7], S_S1), (sc2.at[0], S_S2), (sc3.at[0:7], S_S3),
    ):
        pltpu.make_async_copy(ref, ref, ssem.at[ss]).wait()
    for copy in outs:
        copy.wait()


def grad_kernel(whole, xs, wts, gg, gu, gd, out):
    full = whole[pl.ds(8 * pl.program_id(0), 8)]

    def rows(i):
        return jnp.concatenate(
            [full[:, i].reshape(8 * HB, 128), full[:, 3 + i].reshape(8 * HB, 128)], axis=1
        )

    out[...] = wts[...]
    gd[...] = nt(rows(0), xs[1]).astype(BF)
    gg[...] = nt(xs[0], rows(1)).astype(BF)
    gu[...] = nt(xs[0], rows(2)).astype(BF)


def body(train_x, train_cot, val_x, val_cot, w_gate, w_up, w_down, step_weights, example_ids, val_mask):
    hbm = pl.BlockSpec(memory_space=pltpu.HBM)
    free = pl.BlockSpec(memory_space=pl.ANY)
    vmem = pl.BlockSpec(memory_space=pltpu.VMEM)
    V = pltpu.VMEM
    full, xs, wts = pl.pallas_call(
        comm_kernel,
        out_shape=(
            jax.ShapeDtypeStruct((16, 6, HB, 128), BF),
            jax.ShapeDtypeStruct((2, W, TOK), BF),
            jax.ShapeDtypeStruct((1, EX), F32),
        ),
        in_specs=[hbm] * 10,
        out_specs=(free, free, vmem),
        scratch_shapes=[
            pltpu.SMEM((EX,), F32),
            V((1, TOK), jnp.int32),
            V((1, 32), jnp.int32),
            V((2, 4, W), BF),
            V((2, W, 1792), BF),
            V((2, NZ, 3, HB, W), BF),
            V((NZ, 3, HB, W), BF),
            V((80, W), BF),
            V((16, W), F32),
            V((NM, 80, W), BF),
            V((NM, 80, W), BF),
            V((3, 128, W), BF),
            V((3, 128, W), BF),
            V((NZ, 7, HB, 128), F32),
            V((6, HB, 128), BF),
            V((2, 4, 7, HB, 128), BF),
            V((2, 4, 7, HB, 128), BF),
            V((7, HB, 128), F32),
            V((2, 7, HB, 128), BF),
            V((NZ, 16, 128), F32),
            V((NZ, 16, 128), F32),
            V((2, 16, 128), F32),
            V((2, NZ, 16, 128), F32),
            V((NZ, EX, 128), F32),
            V((2, EX, 128), F32),
            V((NM, EX, 128), F32),
            V((2, W, TOK), F32),
            V((2, W, TOK), BF),
            pltpu.SemaphoreType.DMA((11,)),
            pltpu.SemaphoreType.DMA((19,)),
            pltpu.SemaphoreType.DMA((95,)),
            pltpu.SemaphoreType.DMA((2,)),
        ],
        compiler_params=pltpu.CompilerParams(
            collective_id=0, has_side_effects=True, vmem_limit_bytes=40 * 1024 * 1024
        ),
        name="reduce_and_gather",
    )(
        *[
            pltpu.with_memory_space_constraint(a, pltpu.HBM)
            for a in (
                train_x, train_cot, val_x, val_cot, w_gate, w_up, w_down.reshape(NZ, 2, HB, W),
                step_weights, example_ids.reshape(1, TOK), val_mask.reshape(1, 32),
            )
        ]
    )
    gg, gu, gd, out = pl.pallas_call(
        grad_kernel,
        grid=(2,),
        out_shape=(
            jax.ShapeDtypeStruct((W, 1792), BF),
            jax.ShapeDtypeStruct((W, 1792), BF),
            jax.ShapeDtypeStruct((1792, W), BF),
            jax.ShapeDtypeStruct((1, EX), F32),
        ),
        in_specs=[
            vmem,
            vmem,
            vmem,
        ],
        out_specs=(
            pl.BlockSpec((W, 8 * HB), lambda i: (0, i)),
            pl.BlockSpec((W, 8 * HB), lambda i: (0, i)),
            pl.BlockSpec((8 * HB, W), lambda i: (i, 0)),
            pl.BlockSpec((1, EX), lambda i: (0, 0)),
        ),
        compiler_params=pltpu.CompilerParams(vmem_limit_bytes=40 * 1024 * 1024),
        name="gradients",
    )(full, xs, wts)
    return gg, gu, gd, out.reshape(EX)


def solution(mesh):
    wide, tall = P("dp", "mp"), P("mp", "dp")
    return jax.shard_map(
        body,
        mesh=mesh,
        in_specs=(tall, tall, tall, tall, wide, wide, tall, P(), P(), P()),
        out_specs=(wide, wide, tall, P()),
        check_vma=False,
    )
```
